32 devices in a mesh: fsdp: 4 (over x, core), ctx: 4 (over z), tp: 2 (over y).
Axes of the slice: x: 2, y: 2, z: 4, core: 2. Of those that a mesh axis runs over, the one named last changes fastest.
Arguments:
- tokens: bfloat16 [6144, 1536], P(('fsdp', 'ctx')), may hold values from -6 to 6
- out_grad: bfloat16 [6144, 1536], P(('fsdp', 'ctx')), may hold values from -6 to 6
- lengths: int32 [4, 4], P('fsdp'), may hold values from 1 to 1344, 1536 in all within a row
- routes: int32 [6144, 8], P(('fsdp', 'ctx')), may hold values from 0 to 15, all different within a row; in each aligned block of 384 rows (0 to 383, 384 to 767, ...) at most 240 rows name the same one
- gate_weights: float32 [6144, 8], P(('fsdp', 'ctx')), may hold values from 0.2 to 0.6
- qkv_weight: float32 [1536, 2560], P(('fsdp', 'ctx'), 'tp'), may hold values from -0.15625 to 0.15625
- out_weight: float32 [1536, 1536], P('tp', ('fsdp', 'ctx')), may hold values from -6 to 6
- norm_gains: float32 [2, 1536], P(None, ('fsdp', 'ctx')), may hold values from 0.5 to 1.5
- expert_in: float32 [16, 2, 1536, 512], P(('fsdp', 'ctx'), None, None, 'tp'), may hold values from -0.15625 to 0.15625
- expert_down: float32 [16, 512, 1536], P(('fsdp', 'ctx'), 'tp'), may hold values from -0.25 to 0.25
- qkv_moment: float32 [1536, 2560], P(('fsdp', 'ctx'), 'tp'), may hold values from -448 to 448
- qkv_average: float32 [1536, 2560], P(('fsdp', 'ctx'), 'tp'), may hold values from -0.15625 to 0.15625
- out_moment: float32 [1536, 1536], P('tp', ('fsdp', 'ctx')), may hold values from -16 to 16
- out_average: float32 [1536, 1536], P('tp', ('fsdp', 'ctx')), may hold values from -6 to 6
- gain_moment: float32 [2, 1536], P(None, ('fsdp', 'ctx')), may hold values from -448 to 448
- gain_average: float32 [2, 1536], P(None, ('fsdp', 'ctx')), may hold values from 0.5 to 1.5
- in_moment: float32 [16, 2, 1536, 512], P(('fsdp', 'ctx'), None, None, 'tp'), may hold values from -96 to 96
- in_average: float32 [16, 2, 1536, 512], P(('fsdp', 'ctx'), None, None, 'tp'), may hold values from -0.15625 to 0.15625
- down_moment: float32 [16, 512, 1536], P(('fsdp', 'ctx'), 'tp'), may hold values from -64 to 64
- down_average: float32 [16, 512, 1536], P(('fsdp', 'ctx'), 'tp'), may hold values from -0.25 to 0.25
Outputs:
- block_out: bfloat16 [6144, 1536], P(('fsdp', 'ctx'))
- in_grad: bfloat16 [6144, 1536], P(('fsdp', 'ctx'))
- qkv_moment_new: float32 [1536, 2560], P(('fsdp', 'ctx'), 'tp')
- qkv_average_new: float32 [1536, 2560], P(('fsdp', 'ctx'), 'tp')
- qkv_weight_new: float32 [1536, 2560], P(('fsdp', 'ctx'), 'tp')
- out_moment_new: float32 [1536, 1536], P('tp', ('fsdp', 'ctx'))
- out_average_new: float32 [1536, 1536], P('tp', ('fsdp', 'ctx'))
- out_weight_new: float32 [1536, 1536], P('tp', ('fsdp', 'ctx'))
- gain_moment_new: float32 [2, 1536], P(None, ('fsdp', 'ctx'))
- gain_average_new: float32 [2, 1536], P(None, ('fsdp', 'ctx'))
- gain_weight_new: float32 [2, 1536], P(None, ('fsdp', 'ctx'))
- in_moment_new: float32 [16, 2, 1536, 512], P(('fsdp', 'ctx'), None, None, 'tp')
- in_average_new: float32 [16, 2, 1536, 512], P(('fsdp', 'ctx'), None, None, 'tp')
- in_weight_new: float32 [16, 2, 1536, 512], P(('fsdp', 'ctx'), None, None, 'tp')
- down_moment_new: float32 [16, 512, 1536], P(('fsdp', 'ctx'), 'tp')
- down_average_new: float32 [16, 512, 1536], P(('fsdp', 'ctx'), 'tp')
- down_weight_new: float32 [16, 512, 1536], P(('fsdp', 'ctx'), 'tp')
The draws below stay inside these ranges and needn't reach their ends.
Inputs may be any that keep to these rules, and one draw needn't show every extreme that they name: `lengths`: row f lists the documents of the packed stream of fsdp index f in order; they sum to 1536. `routes`: among the 384 rows of one device no expert is named more than 240 times; in some device's rows some expert is named exactly 240 times.
All inputs are finite; a program needn't handle non-finite values.
Results may differ from the reference program's by a relative error of at most 0.02.
Values may be sent and summed in bfloat16 or wider, within the bound.
No kernel may reach another device: no remote copies, remote signals or barrier semaphores. Data moves between devices by JAX's collectives and lax.ppermute only.
A program may use at most 256 MiB of HBM per device.

```python
import functools
import math
import jax
import jax.numpy as jnp
import numpy as np
from jax import lax

D = 1536
H = 24
KV = 8
HD = 64
FF = 512
TOP = 8
GROUP = 3
TOK_DEV = 384
NDOCS = 4
EXPERTS = 16
SEQ = 1536
TOKENS = 6144
CAP = 240
MOST = 1344
N_FSDP = 4
N_CTX = 4


def shard_levels(stream_key, shape, cuts, low, top_value):
    def one(axis_at, parts):
        steps = jax.random.uniform(jax.random.fold_in(jax.random.fold_in(stream_key, 6), axis_at), (parts,), jnp.float32, low / len(cuts), top_value / len(cuts))
        return jnp.repeat(jnp.exp(steps), shape[axis_at] // parts).reshape((-1,) + (1,) * (len(shape) - axis_at - 1))

    loudness = one(*cuts[0])
    for cut in cuts[1:]:
        loudness = loudness * one(*cut)
    return loudness


def profile(count, total, limit, skew):
    loads = [(1 << 20) // math.isqrt(standing ** skew) + 1 for standing in range(2, count + 1)]
    rest, holding = total - limit - (count - 1), [1] * (count - 1)
    while rest > 0:
        free = [i for i in range(count - 1) if holding[i] < limit]
        whole, budget = sum([loads[i] for i in free]), rest
        for i in free:
            addition = min(limit - holding[i], max(1, budget * loads[i] // whole), rest)
            holding[i] = holding[i] + addition
            rest = rest - addition
    return np.array([limit] + holding)


def uneven_parts(own_key, amount, total, bound, slope):
    if amount == 2:
        one = jax.random.randint(own_key, (), max(1, total - bound), min(bound, total - 1) + 1)
        return jnp.stack([one, total - one])
    tallies = jnp.asarray(profile(amount, total, bound, slope), jnp.int32)
    pairs = (amount - 1) // 2
    giver, sink = tallies[1:1 + 2 * pairs:2], tallies[2:2 + 2 * pairs:2]
    slack = jnp.minimum(giver - 1, bound - sink)
    moved = jax.random.randint(jax.random.fold_in(own_key, 1), (pairs,), 0, 1 << 20) % (slack + 1)
    tallies = tallies.at[1:1 + 2 * pairs:2].set(giver - moved).at[2:2 + 2 * pairs:2].set(sink + moved)
    return tallies[jax.random.permutation(jax.random.fold_in(own_key, 2), amount)]


def deal_out(rng, own, number, rows, amount, top, bound, slope):
    sequence = jax.random.permutation(rng, amount)
    packed, common = load_shares(amount, rows * top, bound, slope, True), load_shares(amount, rows * top, bound, slope, False)
    places = jnp.arange(amount)

    def named(tallies, offset_by):
        used = int((tallies > 0).sum())
        fixed = max(1, used // 4)
        shifted = fixed + (places - fixed + offset_by * (used - fixed)) % max(1, amount - fixed)
        return jnp.zeros((amount,), jnp.int32).at[sequence[jnp.where(places < fixed, places, shifted)]].set(jnp.asarray(tallies, jnp.int32))

    tallies = jnp.where(number % 4 == 0, named(packed, number // 4), named(common, number - number // 4 - 1))
    mixed = jax.random.permutation(jax.random.fold_in(own, 3), amount)
    source_of, taker = mixed[0:amount // 2 * 2:2], mixed[1:amount // 2 * 2:2]
    room = jnp.minimum(tallies[source_of] - 1, bound - tallies[taker]) // 2
    room = jnp.where((source_of == sequence[0]) | (taker == sequence[0]) | (tallies[taker] == 0), 0, jnp.maximum(room, 0))
    shifted = jax.random.randint(jax.random.fold_in(own, 4), (amount // 2,), 0, 1 << 20) % (room + 1)
    tallies = tallies.at[source_of].add(-shifted).at[taker].add(shifted)
    items = jnp.searchsorted(jnp.cumsum(tallies), jnp.arange(rows * top), side="right").astype(jnp.int32)
    table = items.reshape(top, rows).T
    table = table[jax.random.permutation(jax.random.fold_in(own, 1), rows)]
    offset_by = jax.random.randint(jax.random.fold_in(own, 2), (rows, 1), 0, top)
    return jnp.take_along_axis(table, (jnp.arange(top)[None, :] + offset_by) % top, axis=1)


def load_shares(amount, total, bound, lean, full):
    portions = [(1 << 20) // math.isqrt(standing ** lean) + 1 for standing in range(1, amount + 1)]
    largest = bound if full else min(bound, max(-(-total // amount), total * portions[0] // sum(portions)))
    least = 1 if total - largest >= amount - 1 else 0
    holding, spare = [largest] + [least] * (amount - 1), total - largest - least * (amount - 1)
    while spare > 0:
        free = [i for i in range(1, amount) if holding[i] < largest] or [i for i in range(1, amount) if holding[i] < bound]
        pool, left = sum([portions[i] for i in free]), spare
        for i in free:
            more = min(bound - holding[i], max(1, left * portions[i] // pool), spare)
            holding[i] = holding[i] + more
            spare = spare - more
    return np.array(holding)


def bell_draw(stream_key, shape, spread, most, shards=(), kind=jnp.bfloat16):
    entries = spread * jax.random.normal(stream_key, shape, jnp.float32)
    if shards:
        entries = entries * shard_levels(stream_key, shape, shards, -0.22, 0.18)
    return jnp.clip(entries, -most, most).astype(kind)


def setup_inputs(seed: int = 0) -> dict:
    keys = jax.random.split(jax.random.key(seed), 21)
    tokens = bell_draw(keys[0], (TOKENS, D), 1.0, 6.0, ((0, 16),))
    out_grad = bell_draw(keys[1], (TOKENS, D), 1.0, 6.0, ((0, 16),))
    lengths = jax.vmap(lambda own: uneven_parts(own, NDOCS, SEQ, MOST, 2))(jax.random.split(keys[2], N_FSDP)).reshape((N_FSDP, NDOCS)).astype(jnp.int32)
    routes_keys = jax.random.split(jax.random.fold_in(keys[3], 1), TOKENS // TOK_DEV)
    routes_turns = jax.random.permutation(jax.random.fold_in(keys[3], 3), TOKENS // TOK_DEV)
    routes = jax.vmap(lambda own, number: deal_out(jax.random.fold_in(keys[3], 2), own, number, TOK_DEV, EXPERTS, TOP, CAP, 2))(routes_keys, routes_turns).reshape((TOKENS, TOP))
    gate_weights = jnp.clip(0.2 + 0.400000021 * jax.random.uniform(keys[4], (TOKENS, TOP), jnp.float32) ** shard_levels(keys[4], (TOKENS, TOP), ((0, 16),), -0.2, 0.2), 0.2, 0.6)
    qkv_weight = bell_draw(keys[5], (D, (H + 2 * KV) * HD), D ** -0.5, 0.15625, ((0, 16), (1, 2)), jnp.float32)
    out_weight = bell_draw(keys[6], (H * HD, D), ((TOK_DEV * N_CTX) ** 0.5 * (2 * H * HD) ** -0.5), 6.0, ((0, 2), (1, 16)), jnp.float32)
    norm_gains = jnp.clip(1.0 + 0.1 * jax.random.normal(keys[7], (2, D), jnp.float32), 0.5, 1.5)
    expert_in = bell_draw(keys[8], (EXPERTS, 2, D, FF), D ** -0.5, 0.15625, ((0, 16), (3, 2)), jnp.float32)
    expert_down = bell_draw(keys[9], (EXPERTS, FF, D), FF ** -0.5, 0.25, ((0, 16), (1, 2)), jnp.float32)
    qkv_moment = bell_draw(keys[10], (D, (H + 2 * KV) * HD), ((TOK_DEV * N_FSDP * N_CTX) ** 0.5), 448.0, ((0, 16), (1, 2)), jnp.float32)
    qkv_average = bell_draw(keys[11], (D, (H + 2 * KV) * HD), D ** -0.5, 0.15625, ((0, 16), (1, 2)), jnp.float32)
    out_moment = bell_draw(keys[12], (H * HD, D), ((2 * N_FSDP) ** 0.5), 16.0, ((0, 2), (1, 16)), jnp.float32)
    out_average = bell_draw(keys[13], (H * HD, D), ((TOK_DEV * N_CTX) ** 0.5 * (2 * H * HD) ** -0.5), 6.0, ((0, 2), (1, 16)), jnp.float32)
    gain_moment = bell_draw(keys[14], (2, D), ((TOK_DEV * N_FSDP * N_CTX) ** 0.5), 448.0, ((1, 16),), jnp.float32)
    gain_average = jnp.clip(1.0 + 0.1 * jax.random.normal(keys[15], (2, D), jnp.float32), 0.5, 1.5)
    in_moment = bell_draw(keys[16], (EXPERTS, 2, D, FF), (0.3 * (8 * TOK_DEV) ** 0.5), 96.0, ((0, 16), (3, 2)), jnp.float32)
    in_average = bell_draw(keys[17], (EXPERTS, 2, D, FF), D ** -0.5, 0.15625, ((0, 16), (3, 2)), jnp.float32)
    down_moment = bell_draw(keys[18], (EXPERTS, FF, D), (0.2 * (8 * TOK_DEV) ** 0.5), 64.0, ((0, 16), (1, 2)), jnp.float32)
    down_average = bell_draw(keys[19], (EXPERTS, FF, D), FF ** -0.5, 0.25, ((0, 16), (1, 2)), jnp.float32)
    return {"tokens": tokens, "out_grad": out_grad, "lengths": lengths, "routes": routes, "gate_weights": gate_weights, "qkv_weight": qkv_weight, "out_weight": out_weight, "norm_gains": norm_gains, "expert_in": expert_in, "expert_down": expert_down, "qkv_moment": qkv_moment, "qkv_average": qkv_average, "out_moment": out_moment, "out_average": out_average, "gain_moment": gain_moment, "gain_average": gain_average, "in_moment": in_moment, "in_average": in_average, "down_moment": down_moment, "down_average": down_average}


@jax.custom_vjp
def low(v):
    return lax.optimization_barrier(v.astype(jnp.bfloat16)).astype(jnp.float32)

@jax.custom_vjp
def low_back(v):
    return v

def low_keep(v):
    return (low(v), None)

def low_pass(kept, grad):
    return (grad,)

def back_keep(v):
    return (v, None)

def back_low(kept, grad):
    return (low(grad),)
low.defvjp(low_keep, low_pass)
low_back.defvjp(back_keep, back_low)
EPSILON = 1e-05
ROPE_BASE = 10000.0
MOMENTUM = 0.9
AVERAGE = 0.7
RATE_QKV = 7e-05
RATE_OUT = 0.15
RATE_GAIN = 0.0005
RATE_IN = 0.0004
RATE_DOWN = 0.001

def highest(left_mat, right_mat):
    return jnp.dot(left_mat, right_mat, precision=lax.Precision.HIGHEST)

def rotate(values, position, direction):
    half_width = values.shape[-1] // 2
    frequency = jnp.exp(jnp.arange(half_width, dtype=jnp.float32) * (-2.0 * math.log(ROPE_BASE) / values.shape[-1]))
    angles = position.astype(jnp.float32)[:, None] * frequency[None, :]
    cosine = jnp.cos(angles)[:, None, :]
    sine_part = direction * jnp.sin(angles)[:, None, :]
    first_half = values[..., :half_width]
    second = values[..., half_width:]
    return jnp.concatenate([first_half * cosine - second * sine_part, second * cosine + first_half * sine_part], axis=-1)

def doc_positions(lengths_row, places):
    doc_ends = jnp.cumsum(lengths_row).astype(jnp.int32)
    passed = places[:, None] >= doc_ends[None, :]
    segment = lax.optimization_barrier(jnp.sum(passed.astype(jnp.int32), axis=1))
    doc_start = lax.optimization_barrier(jnp.sum(jnp.where(passed, lengths_row[None, :], 0), axis=1)).astype(jnp.int32)
    return (segment, places - doc_start)

def normalize(hidden, gain_row):
    return hidden * lax.rsqrt(lax.optimization_barrier(jnp.mean(hidden * hidden, axis=-1, keepdims=True)) + EPSILON) * gain_row

def stream_attention(operands):
    projected, lengths_row = operands
    places = jnp.arange(SEQ, dtype=jnp.int32)
    segment, position = doc_positions(lengths_row, places)
    pieces = projected.reshape(SEQ, KV, GROUP + 2, HD)
    queries = low(rotate(pieces[:, :, :GROUP, :].reshape(SEQ, H, HD), position, 1.0))
    keys_rot = low(rotate(pieces[:, :, GROUP, :], position, 1.0))
    values_low = low(pieces[:, :, GROUP + 1, :])
    allowed = (segment[:, None] == segment[None, :]) & (places[None, :] <= places[:, None])
    query_heads = jnp.transpose(queries, (1, 0, 2))
    key_heads = jnp.repeat(jnp.transpose(keys_rot, (1, 0, 2)), GROUP, axis=0)
    value_heads = jnp.repeat(jnp.transpose(values_low, (1, 0, 2)), GROUP, axis=0)

    def one_head(head_operands):
        query_head, key_head, value_head = head_operands
        scores = low_back(highest(query_head, key_head.T) * HD ** (-0.5))
        scores = jnp.where(allowed, scores, -1e+30)
        top_score = lax.optimization_barrier(jnp.max(scores, axis=-1, keepdims=True))
        exponent = jnp.exp(scores - top_score)
        soft_probs = exponent / lax.optimization_barrier(jnp.sum(exponent, axis=-1, keepdims=True))
        return highest(low(soft_probs), value_head)
    attended = lax.map(jax.checkpoint(one_head), (query_heads, key_heads, value_heads))
    return jnp.transpose(attended, (1, 0, 2)).reshape(SEQ, H * HD)

def expert_block(expert_weights, operands):
    gate_low, up_low, down_low = expert_weights
    block_rows, block_routes, block_gates = operands
    flat_routes = block_routes.reshape(-1)
    chosen = (flat_routes[:, None] == jnp.arange(EXPERTS, dtype=jnp.int32)[None, :]).astype(jnp.int32)
    slot_rank = lax.optimization_barrier(jnp.sum((jnp.cumsum(chosen, axis=0) - chosen) * chosen, axis=1)).astype(jnp.int32)
    slot_flat = flat_routes * CAP + slot_rank
    token_of = jnp.arange(TOK_DEV * TOP, dtype=jnp.int32) // TOP
    buffer = jnp.zeros((EXPERTS * CAP, D), jnp.float32).at[slot_flat].set(block_rows[token_of])
    buffer = low_back(buffer).reshape(EXPERTS, CAP, D)
    gate_pre = low_back(jnp.einsum('ecd,edf->ecf', buffer, gate_low, precision=lax.Precision.HIGHEST))
    up_pre = low_back(jnp.einsum('ecd,edf->ecf', buffer, up_low, precision=lax.Precision.HIGHEST))
    activated = low(jax.nn.silu(gate_pre) * up_pre)
    expert_out = low_back(low(jnp.einsum('ecf,efd->ecd', activated, down_low, precision=lax.Precision.HIGHEST)))
    picked = expert_out.reshape(EXPERTS * CAP, D)[slot_flat].reshape(TOK_DEV, TOP, D)
    return lax.optimization_barrier(jnp.sum(picked * block_gates[:, :, None], axis=1))

def forward(lengths, routes, gate_weights, inputs, qkv_weight, out_weight, norm_gains, expert_in, expert_down):
    gains_low = low(norm_gains)
    normed_low = low(normalize(inputs, gains_low[0]))
    projected = low_back(highest(normed_low, low(qkv_weight)))
    head_out = lax.map(jax.checkpoint(stream_attention), (projected.reshape(N_FSDP, SEQ, (H + 2 * KV) * HD), lengths))
    head_out = low_back(low(head_out.reshape(TOKENS, H * HD)))
    hidden_one = inputs + low_back(highest(head_out, low(out_weight)))
    normed_two = low(normalize(hidden_one, gains_low[1]))
    expert_weights = (low(expert_in[:, 0]), low(expert_in[:, 1]), low(expert_down))
    blocks = TOKENS // TOK_DEV
    mixture = lax.map(jax.checkpoint(functools.partial(expert_block, expert_weights)), (normed_two.reshape(blocks, TOK_DEV, D), routes.reshape(blocks, TOK_DEV, TOP), gate_weights.reshape(blocks, TOK_DEV, TOP)))
    return hidden_one + mixture.reshape(TOKENS, D)

def advance(weight, gradient, moment, average, step_rate):
    moment_new = MOMENTUM * moment + gradient
    weight_new = weight - step_rate * (gradient + MOMENTUM * moment_new)
    average_new = AVERAGE * average + (1.0 - AVERAGE) * weight_new
    return (moment_new, average_new, weight_new)

def reference(tokens, out_grad, lengths, routes, gate_weights, qkv_weight, out_weight, norm_gains, expert_in, expert_down, qkv_moment, qkv_average, out_moment, out_average, gain_moment, gain_average, in_moment, in_average, down_moment, down_average):
    inputs = tokens.astype(jnp.float32)
    fixed = functools.partial(forward, lengths, routes, gate_weights)
    result, pull_back = jax.vjp(fixed, inputs, qkv_weight, out_weight, norm_gains, expert_in, expert_down)
    gradients = pull_back(out_grad.astype(jnp.float32))
    qkv_new = advance(qkv_weight, gradients[1], qkv_moment, qkv_average, RATE_QKV)
    out_new = advance(out_weight, gradients[2], out_moment, out_average, RATE_OUT)
    gain_new = advance(norm_gains, gradients[3], gain_moment, gain_average, RATE_GAIN)
    in_new = advance(expert_in, gradients[4], in_moment, in_average, RATE_IN)
    down_new = advance(expert_down, gradients[5], down_moment, down_average, RATE_DOWN)
    return (result.astype(jnp.bfloat16), gradients[0].astype(jnp.bfloat16), qkv_new[0], qkv_new[1], qkv_new[2], out_new[0], out_new[1], out_new[2], gain_new[0], gain_new[1], gain_new[2], in_new[0], in_new[1], in_new[2], down_new[0], down_new[1], down_new[2])
```

```python
import functools
import math

import jax
import jax.numpy as jnp
from jax import lax
from jax.experimental import pallas as pl
from jax.experimental.pallas import tpu as pltpu
from jax.sharding import PartitionSpec as P

HD = 64
GROUP = 3


EPSILON = 1e-05
ROPE_BASE = 10000.0
MOMENTUM = 0.9
AVERAGE = 0.7
RATE_QKV = 7e-05
RATE_OUT = 0.15
RATE_GAIN = 0.0005
RATE_IN = 0.0004
RATE_DOWN = 0.001


def rotate(values, position, direction):
    half_width = values.shape[-1] // 2
    frequency = jnp.exp(
        jnp.arange(half_width, dtype=jnp.float32) * (-2.0 * math.log(ROPE_BASE) / values.shape[-1])
    )
    angles = position.astype(jnp.float32)[:, None] * frequency[None, :]
    cosine = jnp.cos(angles)[:, None, :]
    sine_part = direction * jnp.sin(angles)[:, None, :]
    first_half = values[..., :half_width]
    second = values[..., half_width:]
    return jnp.concatenate(
        [first_half * cosine - second * sine_part, second * cosine + first_half * sine_part],
        axis=-1,
    )


def doc_positions(lengths_row, places):
    doc_ends = jnp.cumsum(lengths_row)
    passed = places[:, None] >= doc_ends[None, :]
    segment = jnp.sum(passed.astype(jnp.int32), axis=1)
    doc_start = jnp.sum(jnp.where(passed, lengths_row[None, :], 0), axis=1)
    return (segment, places - doc_start)


def contract_rows(left_mat, right_mat):
    return lax.dot_general(
        left_mat, right_mat, (((0,), (0,)), ((), ())), preferred_element_type=jnp.float32
    )


def contract_cols(left_mat, right_mat):
    return lax.dot_general(
        left_mat, right_mat, (((1,), (1,)), ((), ())), preferred_element_type=jnp.float32
    )


def norm_back(grad_out, normed, inverse, gain_row):
    scaled = grad_out * gain_row
    return inverse * (scaled - normed * jnp.mean(scaled * normed, axis=-1, keepdims=True))


F_MASKS = (0, 2, 1, 3)
VMEM_LIMIT = 60 * 1024 * 1024


def swap(value, axis, mask):
    size = lax.axis_size(axis)
    return lax.ppermute(value, axis, [(i, i ^ mask) for i in range(size)])


def gather_pieces(own_in, own_down):
    over_tp = range(lax.axis_size("tp"))
    far_in = swap(own_in, "fsdp", 2)
    downs_near = [own_down] + [swap(own_down, "tp", m) for m in over_tp[1:]]
    ins_near = [own_in] + [swap(own_in, "tp", m) for m in over_tp[1:]]
    downs_far = [swap(piece, "fsdp", 2) for piece in downs_near]
    ins_far = [far_in] + [swap(far_in, "tp", m) for m in over_tp[1:]]
    ins, downs = ins_near + ins_far, downs_near + downs_far
    ins += [swap(piece, "fsdp", 1) for piece in ins]
    downs += [swap(piece, "fsdp", 1) for piece in downs]
    return ins, downs


def nt_dot(left_mat, right_mat):
    return lax.dot_general(
        left_mat, right_mat, (((1,), (1,)), ((), ())), preferred_element_type=jnp.float32
    )


def expert_kernel(blocks, pieces, *refs):
    x_refs, refs = refs[:blocks], refs[blocks:]
    og_refs, refs = refs[:blocks], refs[blocks:]
    gate_refs, refs = refs[:blocks], refs[blocks:]
    in_refs, refs = refs[:pieces], refs[pieces:]
    down_refs, refs = refs[:pieces], refs[pieces:]
    gx_refs, refs = refs[:blocks], refs[blocks:]
    act_ref, gg_ref, gu_ref, w_in, w_down, x_all, og_all, gates, total, sem_in, sem_down = refs
    for p in range(pieces):
        pltpu.make_async_copy(in_refs[p], w_in.at[p], sem_in.at[p]).start()
        pltpu.make_async_copy(down_refs[p], w_down.at[p], sem_down.at[p]).start()
    rows = x_refs[0].shape[0]
    width = w_down.shape[1]
    for b in range(blocks):
        x_all[b * rows : (b + 1) * rows] = x_refs[b][...]
        og_all[b * rows : (b + 1) * rows] = og_refs[b][...]
        for m in range(len(F_MASKS)):
            gates[m, b * rows : (b + 1) * rows] = gate_refs[b][m]
    total[...] = jnp.zeros_like(total)

    @pl.loop(0, pieces)
    def _(p):
        pltpu.make_async_copy(w_in.at[p], w_in.at[p], sem_in.at[p]).wait()
        pltpu.make_async_copy(w_down.at[p], w_down.at[p], sem_down.at[p]).wait()
        x = x_all[...]
        gate = jnp.dot(x, w_in[p, 0], preferred_element_type=jnp.float32)
        up = jnp.dot(x, w_in[p, 1], preferred_element_type=jnp.float32)
        back = nt_dot(og_all[...], w_down[p])
        weight = gates[p // (pieces // len(F_MASKS))]
        sig = jax.nn.sigmoid(gate)
        silu = gate * sig
        back = back * weight
        cols = pl.ds(pl.multiple_of(p * width, width), width)
        act_ref[:, cols] = (silu * up * weight).astype(jnp.bfloat16)
        grad_gate = (back * up * (sig * (1.0 + gate * (1.0 - sig)))).astype(jnp.bfloat16)
        grad_up = (back * silu).astype(jnp.bfloat16)
        gg_ref[:, cols] = grad_gate
        gu_ref[:, cols] = grad_up
        total[...] += nt_dot(grad_gate, w_in[p, 0]) + nt_dot(grad_up, w_in[p, 1])

    for b in range(blocks):
        gx_refs[b][...] = total[b * rows : (b + 1) * rows].astype(jnp.bfloat16)


def expert_rows(xs, ogs, gates, ins, downs):
    blocks, (rows, width), hidden = len(xs), xs[0].shape, downs[0].shape[0]
    pieces = len(ins)
    vmem = pl.BlockSpec(memory_space=pltpu.VMEM)
    anywhere = pl.BlockSpec(memory_space=pl.ANY)
    low = jnp.bfloat16
    wide = jax.ShapeDtypeStruct((blocks * rows, pieces * hidden), low)
    flops = 2 * 5 * blocks * rows * width * pieces * hidden
    outs = pl.pallas_call(
        functools.partial(expert_kernel, blocks, pieces),
        out_shape=[jax.ShapeDtypeStruct((rows, width), low)] * blocks + [wide] * 3,
        in_specs=[vmem] * (3 * blocks) + [anywhere] * (2 * pieces),
        out_specs=[vmem] * (blocks + 3),
        scratch_shapes=[
            pltpu.VMEM((pieces, 2, width, hidden), low),
            pltpu.VMEM((pieces, hidden, width), low),
            pltpu.VMEM((blocks * rows, width), low),
            pltpu.VMEM((blocks * rows, width), low),
            pltpu.VMEM((len(F_MASKS), blocks * rows, 1), jnp.float32),
            pltpu.VMEM((blocks * rows, width), jnp.float32),
            pltpu.SemaphoreType.DMA((pieces,)),
            pltpu.SemaphoreType.DMA((pieces,)),
        ],
        compiler_params=pltpu.CompilerParams(vmem_limit_bytes=VMEM_LIMIT),
        cost_estimate=pl.CostEstimate(flops=flops, bytes_accessed=25 << 20, transcendentals=0),
        name="expert_rows",
    )(*xs, *ogs, *gates, *ins, *downs)
    return outs[:blocks], outs[blocks:]


def mix_kernel(blocks, calls, pieces, *refs):
    act_refs, refs = refs[:calls], refs[calls:]
    down_refs, refs = refs[:pieces], refs[pieces:]
    mix_refs, refs = refs[:blocks], refs[blocks:]
    w_down, sem = refs
    hidden = down_refs[0].shape[0]
    for p in range(pieces):
        pltpu.make_async_copy(
            down_refs[p], w_down.at[p * hidden : (p + 1) * hidden], sem.at[p]
        ).start()
    for p in range(pieces):
        pltpu.make_async_copy(
            down_refs[p], w_down.at[p * hidden : (p + 1) * hidden], sem.at[p]
        ).wait()
    rows = mix_refs[0].shape[0]
    per_call = blocks // calls
    for b in range(blocks):
        at = (b % per_call) * rows
        mix_refs[b][...] = jnp.dot(
            act_refs[b // per_call][at : at + rows], w_down[...], preferred_element_type=jnp.float32
        ).astype(jnp.bfloat16)


def mix_rows(acts, downs, blocks):
    hidden, width = downs[0].shape
    pieces, calls = len(downs), len(acts)
    rows = acts[0].shape[0] * calls // blocks
    vmem = pl.BlockSpec(memory_space=pltpu.VMEM)
    anywhere = pl.BlockSpec(memory_space=pl.ANY)
    return pl.pallas_call(
        functools.partial(mix_kernel, blocks, calls, pieces),
        out_shape=[jax.ShapeDtypeStruct((rows, width), jnp.bfloat16)] * blocks,
        in_specs=[vmem] * calls + [anywhere] * pieces,
        out_specs=[vmem] * blocks,
        scratch_shapes=[
            pltpu.VMEM((pieces * hidden, width), jnp.bfloat16),
            pltpu.SemaphoreType.DMA((pieces,)),
        ],
        compiler_params=pltpu.CompilerParams(vmem_limit_bytes=VMEM_LIMIT),
        cost_estimate=pl.CostEstimate(
            flops=2 * blocks * rows * width * pieces * hidden, bytes_accessed=12 << 20, transcendentals=0
        ),
        name="mix_rows",
    )(*acts, *downs)


def weight_kernel(blocks, calls, *refs):
    x_refs, refs = refs[:blocks], refs[blocks:]
    og_refs, refs = refs[:blocks], refs[blocks:]
    act_refs, refs = refs[:calls], refs[calls:]
    gg_refs, refs = refs[:calls], refs[calls:]
    gu_refs, refs = refs[:calls], refs[calls:]
    in_ref, down_ref, x_t, og_all, act_all, gg_all, gu_all = refs
    rows = x_refs[0].shape[0]

    @pl.when(pl.program_id(0) == 0)
    def _():
        for b in range(blocks):
            x_t[:, b * rows : (b + 1) * rows] = x_refs[b][...].T
            og_all[b * rows : (b + 1) * rows] = og_refs[b][...]

    some = act_refs[0].shape[0]
    for i in range(calls):
        act_all[i * some : (i + 1) * some] = act_refs[i][...]
        gg_all[i * some : (i + 1) * some] = gg_refs[i][...]
        gu_all[i * some : (i + 1) * some] = gu_refs[i][...]
    in_ref[0, 0] = jnp.dot(x_t[...], gg_all[...], preferred_element_type=jnp.float32).astype(jnp.bfloat16)
    in_ref[0, 1] = jnp.dot(x_t[...], gu_all[...], preferred_element_type=jnp.float32).astype(jnp.bfloat16)
    down_ref[0] = jnp.dot(
        act_all[...].T, og_all[...], preferred_element_type=jnp.float32
    ).astype(jnp.bfloat16)


def weight_grads(xs, ogs, acts, ggs, gus, hidden, first, count):
    blocks, calls, (rows, width) = len(xs), len(acts), xs[0].shape
    some = acts[0].shape[0]
    vmem = pl.BlockSpec(memory_space=pltpu.VMEM)
    column = pl.BlockSpec((some, hidden), lambda i: (0, first + i))
    low = jnp.bfloat16
    total = blocks * rows
    return pl.pallas_call(
        functools.partial(weight_kernel, blocks, calls),
        grid=(count,),
        out_shape=[
            jax.ShapeDtypeStruct((count, 2, width, hidden), low),
            jax.ShapeDtypeStruct((count, hidden, width), low),
        ],
        in_specs=[vmem] * (2 * blocks) + [column] * (3 * calls),
        out_specs=[
            pl.BlockSpec((1, 2, width, hidden), lambda i: (i, 0, 0, 0)),
            pl.BlockSpec((1, hidden, width), lambda i: (i, 0, 0)),
        ],
        scratch_shapes=[
            pltpu.VMEM((width, total), low),
            pltpu.VMEM((total, width), low),
            pltpu.VMEM((total, hidden), low),
            pltpu.VMEM((total, hidden), low),
            pltpu.VMEM((total, hidden), low),
        ],
        compiler_params=pltpu.CompilerParams(vmem_limit_bytes=VMEM_LIMIT),
        cost_estimate=pl.CostEstimate(
            flops=2 * 3 * total * width * count * hidden, bytes_accessed=20 << 20, transcendentals=0
        ),
        name="weight_grads",
    )(*xs, *ogs, *acts, *ggs, *gus)


def added(left_mat, right_mat):
    return (left_mat.astype(jnp.float32) + right_mat.astype(jnp.float32)).astype(jnp.bfloat16)


def scatter_pieces(kept, sent):
    back_in, back_down = swap(sent[0], "fsdp", 1), swap(sent[1], "fsdp", 1)
    count = lax.axis_size("tp")
    ins = [added(kept[0][i], back_in[i]) for i in range(2 * count)]
    downs = [added(kept[1][i], back_down[i]) for i in range(2 * count)]
    downs = [added(downs[i], swap(downs[count + i], "fsdp", 2)) for i in range(count)]
    far_in, own_in = ins[count], ins[0]
    for m in range(1, count):
        far_in = added(far_in, swap(ins[count + m], "tp", m))
        own_in = added(own_in, swap(ins[m], "tp", m))
    f32 = jnp.float32
    own_down = downs[0].astype(f32)
    for m in range(1, count):
        own_down += swap(downs[m], "tp", m).astype(f32)
    return own_in.astype(f32) + swap(far_in, "fsdp", 2).astype(f32), own_down


def advance(weight, gradient, moment, average, step_rate):
    moment_new = MOMENTUM * moment + gradient
    weight_new = weight - step_rate * (gradient + MOMENTUM * moment_new)
    average_new = AVERAGE * average + (1.0 - AVERAGE) * weight_new
    return (moment_new, average_new, weight_new)


def per_device(
    tokens,
    out_grad,
    lengths,
    routes,
    gate_weights,
    qkv_weight,
    out_weight,
    norm_gains,
    expert_in,
    expert_down,
    qkv_moment,
    qkv_average,
    out_moment,
    out_average,
    gain_moment,
    gain_average,
    in_moment,
    in_average,
    down_moment,
    down_average,
):
    tok_rows = tokens.shape[0]
    n_ctx = lax.axis_size("ctx")
    experts = lax.axis_size(("fsdp", "ctx"))
    seq_len = tok_rows * n_ctx
    score_scale = HD ** (-0.5)
    qkv_local, out_local, gain_local = (
        lax.all_gather(qkv_weight.astype(jnp.bfloat16), ("fsdp", "ctx"), axis=0, tiled=True),
        lax.all_gather(out_weight.astype(jnp.bfloat16), ("fsdp", "ctx"), axis=1, tiled=True),
        lax.all_gather(norm_gains.astype(jnp.bfloat16), ("fsdp", "ctx"), axis=1, tiled=True),
    )
    gain_one = gain_local[0].astype(jnp.float32)
    gain_two = gain_local[1].astype(jnp.float32)
    places = jnp.arange(seq_len, dtype=jnp.int32)
    seg_all, pos_all = doc_positions(lengths[0], places)
    first_row = lax.axis_index("ctx") * tok_rows
    seg_query = lax.dynamic_slice_in_dim(seg_all, first_row, tok_rows)
    pos_query = lax.dynamic_slice_in_dim(pos_all, first_row, tok_rows)
    place_query = first_row + jnp.arange(tok_rows, dtype=jnp.int32)
    allowed = (seg_query[:, None] == seg_all[None, :]) & (places[None, :] <= place_query[:, None])
    inputs = tokens.astype(jnp.float32)
    inverse_one = lax.rsqrt(jnp.mean(inputs * inputs, axis=-1, keepdims=True) + EPSILON)
    normed_one = inputs * inverse_one
    normed_low = (normed_one * gain_one).astype(jnp.bfloat16)
    projected = jnp.dot(normed_low, qkv_local, preferred_element_type=jnp.float32)
    kv_local = projected.shape[1] // ((GROUP + 2) * HD)
    heads_local = kv_local * GROUP
    pieces = projected.reshape(tok_rows, kv_local, GROUP + 2, HD)
    queries = rotate(
        pieces[:, :, :GROUP, :].reshape(tok_rows, heads_local, HD), pos_query, 1.0
    ).astype(jnp.bfloat16)
    keys_own = rotate(pieces[:, :, GROUP, :], pos_query, 1.0).astype(jnp.bfloat16)
    values_own = pieces[:, :, GROUP + 1, :].astype(jnp.bfloat16)
    keys_all, values_all = (
        lax.all_gather(keys_own.reshape(tok_rows, kv_local * HD), "ctx", axis=0, tiled=True),
        lax.all_gather(values_own.reshape(tok_rows, kv_local * HD), "ctx", axis=0, tiled=True),
    )
    key_heads = jnp.transpose(keys_all.reshape(seq_len, kv_local, HD), (1, 0, 2))
    value_heads = jnp.transpose(values_all.reshape(seq_len, kv_local, HD), (1, 0, 2))
    query_heads = jnp.transpose(queries, (1, 0, 2))
    kv_of_head = jnp.arange(heads_local, dtype=jnp.int32) // GROUP

    def scores_of(query_head, kv_index):
        raw_scores = contract_cols(query_head, key_heads[kv_index]) * score_scale
        return jnp.where(allowed, raw_scores, -1e30)

    def attend(operands):
        query_head, kv_index = operands
        masked = scores_of(query_head, kv_index)
        top_score = jnp.max(masked, axis=-1, keepdims=True)
        exponent = jnp.exp(masked - top_score)
        row_total = jnp.sum(exponent, axis=-1, keepdims=True)
        soft_low = (exponent / row_total).astype(jnp.bfloat16)
        attended = jnp.dot(soft_low, value_heads[kv_index], preferred_element_type=jnp.float32)
        return (attended, (top_score + jnp.log(row_total))[:, 0])

    attended_all, log_totals = lax.map(attend, (query_heads, kv_of_head))
    head_out = (
        jnp.transpose(attended_all, (1, 0, 2))
        .reshape(tok_rows, heads_local * HD)
        .astype(jnp.bfloat16)
    )
    attn_part = jnp.dot(head_out, out_local, preferred_element_type=jnp.float32)
    half_rows = tok_rows // lax.axis_size("tp")
    tp_index = lax.axis_index("tp")
    fsdp_index, ctx_index = lax.axis_index("fsdp"), lax.axis_index("ctx")

    over_tp = range(lax.axis_size("tp"))

    def part_of(value, mask):
        return lax.dynamic_slice_in_dim(value, (tp_index ^ mask) * half_rows, half_rows)

    def own_half(value):
        return part_of(value, 0)

    def sum_own(value):
        total = own_half(value)
        for m in over_tp[1:]:
            total += swap(part_of(value, m).astype(jnp.bfloat16), "tp", m).astype(jnp.float32)
        return total

    def both_halves(own):
        parts = [own] + [swap(own, "tp", m) for m in over_tp[1:]]
        ordered = []
        for at in over_tp:
            chosen = parts[0]
            for m in over_tp[1:]:
                chosen = jnp.where(tp_index ^ m == at, parts[m], chosen)
            ordered.append(chosen)
        return jnp.concatenate(ordered, axis=0)

    attn_sum = sum_own(attn_part)
    hidden_one = own_half(inputs) + attn_sum
    inverse_two = lax.rsqrt(jnp.mean(hidden_one * hidden_one, axis=-1, keepdims=True) + EPSILON)
    normed_two = hidden_one * inverse_two
    normed_two_low = (normed_two * gain_two).astype(jnp.bfloat16)

    ins, downs = gather_pieces(expert_in[0].astype(jnp.bfloat16), expert_down[0].astype(jnp.bfloat16))
    expert_ids = jnp.arange(experts, dtype=jnp.int32)
    dense_gates = jnp.sum(
        jnp.where(
            own_half(routes)[:, :, None] == expert_ids[None, None, :],
            own_half(gate_weights)[:, :, None],
            0.0,
        ),
        axis=1,
    )
    grad_own = own_half(out_grad)
    xs = [normed_two_low] + [swap(normed_two_low, "ctx", m) for m in range(1, n_ctx)]
    ogs = [grad_own] + [swap(grad_own, "ctx", m) for m in range(1, n_ctx)]
    all_gates = [dense_gates] + [swap(dense_gates, "ctx", m) for m in range(1, n_ctx)]

    def of_pieces(block_gates):
        columns = []
        for f_mask in F_MASKS:
            expert = (fsdp_index ^ f_mask) * n_ctx + ctx_index
            columns.append(
                jnp.sum(jnp.where(expert_ids[None, :] == expert, block_gates, 0.0), axis=1)
            )
        return jnp.stack(columns)[:, :, None]

    all_gates = [of_pieces(g) for g in all_gates]
    grads_x, acts, ggs, gus = [], [], [], []
    for at in range(0, n_ctx, 2):
        some_x, (act, gg, gu) = expert_rows(
            xs[at : at + 2], ogs[at : at + 2], all_gates[at : at + 2], ins, downs
        )
        grads_x += some_x
        acts.append(act)
        ggs.append(gg)
        gus.append(gu)
    grad_normed_two = grads_x[0].astype(jnp.float32)
    for m in range(1, n_ctx):
        grad_normed_two += swap(grads_x[m], "ctx", m).astype(jnp.float32)
    mixes = mix_rows(acts, downs, n_ctx)
    mixture = mixes[0].astype(jnp.float32)
    for m in range(1, n_ctx):
        mixture += swap(mixes[m], "ctx", m).astype(jnp.float32)
    block_out = both_halves((hidden_one + mixture).astype(jnp.bfloat16))
    hidden, near = downs[0].shape[0], len(downs) // 2
    sent = weight_grads(xs, ogs, acts, ggs, gus, hidden, near, near)
    kept = weight_grads(xs, ogs, acts, ggs, gus, hidden, 0, near)
    in_grad_sum, down_grad_sum = scatter_pieces(kept, sent)

    gain_grad_two = jnp.sum(grad_normed_two * normed_two, axis=0)
    grad_hidden_half = grad_own.astype(jnp.float32) + norm_back(
        grad_normed_two, normed_two, inverse_two, gain_two
    )
    grad_attn = both_halves(grad_hidden_half.astype(jnp.bfloat16))
    out_weight_grad = contract_rows(head_out, grad_attn)
    head_grad = contract_cols(grad_attn, out_local).astype(jnp.bfloat16)
    grad_heads = jnp.transpose(head_grad.reshape(tok_rows, heads_local, HD), (1, 0, 2))

    def attend_back(operands):
        query_head, kv_index, grad_head, log_total = operands
        masked = scores_of(query_head, kv_index)
        soft_probs = jnp.exp(masked - log_total[:, None])
        grad_probs = contract_cols(grad_head, value_heads[kv_index])
        inner_sum = jnp.sum(soft_probs * grad_probs, axis=-1, keepdims=True)
        grad_scores = (soft_probs * (grad_probs - inner_sum)).astype(jnp.bfloat16)
        grad_query = (
            jnp.dot(grad_scores, key_heads[kv_index], preferred_element_type=jnp.float32)
            * score_scale
        )
        grad_key = contract_rows(grad_scores, query_head) * score_scale
        grad_value = contract_rows(soft_probs.astype(jnp.bfloat16), grad_head)
        return (grad_query, grad_key, grad_value)

    grad_query_all, grad_key_all, grad_value_all = lax.map(
        attend_back, (query_heads, kv_of_head, grad_heads, log_totals)
    )
    grad_key_all = jnp.sum(grad_key_all.reshape(kv_local, GROUP, seq_len, HD), axis=1)
    grad_value_all = jnp.sum(grad_value_all.reshape(kv_local, GROUP, seq_len, HD), axis=1)
    grad_key_own, grad_value_own = (
        lax.psum_scatter(
            jnp.transpose(grad_key_all, (1, 0, 2))
            .reshape(seq_len, kv_local * HD)
            .astype(jnp.bfloat16),
            "ctx",
            scatter_dimension=0,
            tiled=True,
        ).astype(jnp.float32),
        lax.psum_scatter(
            jnp.transpose(grad_value_all, (1, 0, 2))
            .reshape(seq_len, kv_local * HD)
            .astype(jnp.bfloat16),
            "ctx",
            scatter_dimension=0,
            tiled=True,
        ).astype(jnp.float32),
    )
    grad_query_pre = rotate(jnp.transpose(grad_query_all, (1, 0, 2)), pos_query, -1.0)
    grad_key_pre = rotate(grad_key_own.reshape(tok_rows, kv_local, HD), pos_query, -1.0)
    grad_projected = (
        jnp.concatenate(
            [
                grad_query_pre.reshape(tok_rows, kv_local, GROUP, HD),
                grad_key_pre[:, :, None, :],
                grad_value_own.reshape(tok_rows, kv_local, 1, HD),
            ],
            axis=2,
        )
        .reshape(tok_rows, -1)
        .astype(jnp.bfloat16)
    )
    qkv_grad_part = contract_rows(normed_low, grad_projected)
    grad_normed_part = contract_cols(grad_projected, qkv_local)
    grad_normed_one = sum_own(grad_normed_part)
    normed_one_half = own_half(normed_one)
    gain_grad_one = jnp.sum(grad_normed_one * normed_one_half, axis=0)
    in_grad = both_halves(
        (
            grad_hidden_half
            + norm_back(grad_normed_one, normed_one_half, own_half(inverse_one), gain_one)
        ).astype(jnp.bfloat16)
    )
    qkv_grad, out_grad_sum, gains_grad = (
        lax.psum_scatter(
            qkv_grad_part.astype(jnp.bfloat16), ("fsdp", "ctx"), scatter_dimension=0, tiled=True
        ).astype(jnp.float32),
        lax.psum_scatter(
            out_weight_grad.astype(jnp.bfloat16), ("fsdp", "ctx"), scatter_dimension=1, tiled=True
        ).astype(jnp.float32),
        lax.psum_scatter(
            jnp.stack([gain_grad_one, gain_grad_two]).astype(jnp.bfloat16),
            ("fsdp", "ctx"),
            scatter_dimension=1,
            tiled=True,
        ).astype(jnp.float32),
    )
    gains_grad = lax.psum(gains_grad, "tp")
    in_grad_local = in_grad_sum[None]
    down_grad_local = down_grad_sum[None]
    qkv_new = advance(qkv_weight, qkv_grad, qkv_moment, qkv_average, RATE_QKV)
    out_new = advance(out_weight, out_grad_sum, out_moment, out_average, RATE_OUT)
    gain_new = advance(norm_gains, gains_grad, gain_moment, gain_average, RATE_GAIN)
    in_new = advance(expert_in, in_grad_local, in_moment, in_average, RATE_IN)
    down_new = advance(expert_down, down_grad_local, down_moment, down_average, RATE_DOWN)
    return (
        block_out,
        in_grad,
        qkv_new[0],
        qkv_new[1],
        qkv_new[2],
        out_new[0],
        out_new[1],
        out_new[2],
        gain_new[0],
        gain_new[1],
        gain_new[2],
        in_new[0],
        in_new[1],
        in_new[2],
        down_new[0],
        down_new[1],
        down_new[2],
    )


def solution(mesh):
    return jax.shard_map(
        per_device,
        mesh=mesh,
        in_specs=(
            P(("fsdp", "ctx"), None),
            P(("fsdp", "ctx"), None),
            P("fsdp", None),
            P(("fsdp", "ctx"), None),
            P(("fsdp", "ctx"), None),
            P(("fsdp", "ctx"), "tp"),
            P("tp", ("fsdp", "ctx")),
            P(None, ("fsdp", "ctx")),
            P(("fsdp", "ctx"), None, None, "tp"),
            P(("fsdp", "ctx"), "tp", None),
            P(("fsdp", "ctx"), "tp"),
            P(("fsdp", "ctx"), "tp"),
            P("tp", ("fsdp", "ctx")),
            P("tp", ("fsdp", "ctx")),
            P(None, ("fsdp", "ctx")),
            P(None, ("fsdp", "ctx")),
            P(("fsdp", "ctx"), None, None, "tp"),
            P(("fsdp", "ctx"), None, None, "tp"),
            P(("fsdp", "ctx"), "tp", None),
            P(("fsdp", "ctx"), "tp", None),
        ),
        out_specs=(
            P(("fsdp", "ctx"), None),
            P(("fsdp", "ctx"), None),
            P(("fsdp", "ctx"), "tp"),
            P(("fsdp", "ctx"), "tp"),
            P(("fsdp", "ctx"), "tp"),
            P("tp", ("fsdp", "ctx")),
            P("tp", ("fsdp", "ctx")),
            P("tp", ("fsdp", "ctx")),
            P(None, ("fsdp", "ctx")),
            P(None, ("fsdp", "ctx")),
            P(None, ("fsdp", "ctx")),
            P(("fsdp", "ctx"), None, None, "tp"),
            P(("fsdp", "ctx"), None, None, "tp"),
            P(("fsdp", "ctx"), None, None, "tp"),
            P(("fsdp", "ctx"), "tp", None),
            P(("fsdp", "ctx"), "tp", None),
            P(("fsdp", "ctx"), "tp", None),
        ),
        check_vma=False,
    )
```

```python
import functools
import math

import jax
import jax.numpy as jnp
from jax import lax
from jax.experimental import pallas as pl
from jax.experimental.pallas import tpu as pltpu
from jax.sharding import PartitionSpec as P

HD = 64
GROUP = 3


EPSILON = 1e-05
ROPE_BASE = 10000.0
MOMENTUM = 0.9
AVERAGE = 0.7
RATE_QKV = 7e-05
RATE_OUT = 0.15
RATE_GAIN = 0.0005
RATE_IN = 0.0004
RATE_DOWN = 0.001


def doc_positions(lengths_row, places):
    doc_ends = jnp.cumsum(lengths_row)
    passed = places[:, None] >= doc_ends[None, :]
    segment = jnp.sum(passed.astype(jnp.int32), axis=1)
    doc_start = jnp.sum(jnp.where(passed, lengths_row[None, :], 0), axis=1)
    return (segment, places - doc_start)


def norm_back(grad_out, normed, inverse, gain_row):
    scaled = grad_out * gain_row
    return inverse * (scaled - normed * jnp.mean(scaled * normed, axis=-1, keepdims=True))


F_MASKS = (0, 2, 1, 3)
VMEM_LIMIT = 60 * 1024 * 1024


def swap(value, axis, mask):
    size = lax.axis_size(axis)
    return lax.ppermute(value, axis, [(i, i ^ mask) for i in range(size)])


def gather_pieces(own_in, own_down):
    over_tp = range(lax.axis_size("tp"))
    far_in = swap(own_in, "fsdp", 2)
    downs_near = [own_down] + [swap(own_down, "tp", m) for m in over_tp[1:]]
    ins_near = [own_in] + [swap(own_in, "tp", m) for m in over_tp[1:]]
    downs_far = [swap(piece, "fsdp", 2) for piece in downs_near]
    ins_far = [far_in] + [swap(far_in, "tp", m) for m in over_tp[1:]]
    ins, downs = ins_near + ins_far, downs_near + downs_far
    ins += [swap(piece, "fsdp", 1) for piece in ins]
    downs += [swap(piece, "fsdp", 1) for piece in downs]
    return ins, downs


def nt_dot(left_mat, right_mat):
    return lax.dot_general(
        left_mat, right_mat, (((1,), (1,)), ((), ())), preferred_element_type=jnp.float32
    )


def expert_kernel(blocks, pieces, *refs):
    x_refs, refs = refs[:blocks], refs[blocks:]
    og_refs, refs = refs[:blocks], refs[blocks:]
    gate_refs, refs = refs[:blocks], refs[blocks:]
    in_refs, refs = refs[:pieces], refs[pieces:]
    down_refs, refs = refs[:pieces], refs[pieces:]
    gx_refs, refs = refs[:blocks], refs[blocks:]
    act_ref, gg_ref, gu_ref, w_in, w_down, x_all, og_all, gates, total, sem_in, sem_down = refs
    for p in range(pieces):
        pltpu.make_async_copy(in_refs[p], w_in.at[p], sem_in.at[p]).start()
        pltpu.make_async_copy(down_refs[p], w_down.at[p], sem_down.at[p]).start()
    rows = x_refs[0].shape[0]
    width = w_down.shape[1]
    for b in range(blocks):
        x_all[b * rows : (b + 1) * rows] = x_refs[b][...]
        og_all[b * rows : (b + 1) * rows] = og_refs[b][...]
        for m in range(len(F_MASKS)):
            gates[m, b * rows : (b + 1) * rows] = gate_refs[b][m]
    total[...] = jnp.zeros_like(total)

    @pl.loop(0, pieces)
    def _(p):
        pltpu.make_async_copy(w_in.at[p], w_in.at[p], sem_in.at[p]).wait()
        pltpu.make_async_copy(w_down.at[p], w_down.at[p], sem_down.at[p]).wait()
        x = x_all[...]
        gate = jnp.dot(x, w_in[p, 0], preferred_element_type=jnp.float32)
        up = jnp.dot(x, w_in[p, 1], preferred_element_type=jnp.float32)
        back = nt_dot(og_all[...], w_down[p])
        weight = gates[p // (pieces // len(F_MASKS))]
        sig = jax.nn.sigmoid(gate)
        silu = gate * sig
        back = back * weight
        cols = pl.ds(pl.multiple_of(p * width, width), width)
        act_ref[:, cols] = (silu * up * weight).astype(jnp.bfloat16)
        grad_gate = (back * up * (sig * (1.0 + gate * (1.0 - sig)))).astype(jnp.bfloat16)
        grad_up = (back * silu).astype(jnp.bfloat16)
        gg_ref[:, cols] = grad_gate
        gu_ref[:, cols] = grad_up
        total[...] += nt_dot(grad_gate, w_in[p, 0]) + nt_dot(grad_up, w_in[p, 1])

    for b in range(blocks):
        gx_refs[b][...] = total[b * rows : (b + 1) * rows].astype(jnp.bfloat16)


def expert_rows(xs, ogs, gates, ins, downs):
    blocks, (rows, width), hidden = len(xs), xs[0].shape, downs[0].shape[0]
    pieces = len(ins)
    vmem = pl.BlockSpec(memory_space=pltpu.VMEM)
    anywhere = pl.BlockSpec(memory_space=pl.ANY)
    low = jnp.bfloat16
    wide = jax.ShapeDtypeStruct((blocks * rows, pieces * hidden), low)
    flops = 2 * 5 * blocks * rows * width * pieces * hidden
    outs = pl.pallas_call(
        functools.partial(expert_kernel, blocks, pieces),
        out_shape=[jax.ShapeDtypeStruct((rows, width), low)] * blocks + [wide] * 3,
        in_specs=[vmem] * (3 * blocks) + [anywhere] * (2 * pieces),
        out_specs=[vmem] * (blocks + 3),
        scratch_shapes=[
            pltpu.VMEM((pieces, 2, width, hidden), low),
            pltpu.VMEM((pieces, hidden, width), low),
            pltpu.VMEM((blocks * rows, width), low),
            pltpu.VMEM((blocks * rows, width), low),
            pltpu.VMEM((len(F_MASKS), blocks * rows, 1), jnp.float32),
            pltpu.VMEM((blocks * rows, width), jnp.float32),
            pltpu.SemaphoreType.DMA((pieces,)),
            pltpu.SemaphoreType.DMA((pieces,)),
        ],
        compiler_params=pltpu.CompilerParams(vmem_limit_bytes=VMEM_LIMIT),
        cost_estimate=pl.CostEstimate(flops=flops, bytes_accessed=25 << 20, transcendentals=0),
        name="expert_rows",
    )(*xs, *ogs, *gates, *ins, *downs)
    return outs[:blocks], outs[blocks:]


def mix_kernel(blocks, calls, pieces, *refs):
    act_refs, refs = refs[:calls], refs[calls:]
    down_refs, refs = refs[:pieces], refs[pieces:]
    mix_refs, refs = refs[:blocks], refs[blocks:]
    w_down, sem = refs
    hidden = down_refs[0].shape[0]
    for p in range(pieces):
        pltpu.make_async_copy(
            down_refs[p], w_down.at[p * hidden : (p + 1) * hidden], sem.at[p]
        ).start()
    for p in range(pieces):
        pltpu.make_async_copy(
            down_refs[p], w_down.at[p * hidden : (p + 1) * hidden], sem.at[p]
        ).wait()
    rows = mix_refs[0].shape[0]
    per_call = blocks // calls
    for b in range(blocks):
        at = (b % per_call) * rows
        mix_refs[b][...] = jnp.dot(
            act_refs[b // per_call][at : at + rows], w_down[...], preferred_element_type=jnp.float32
        ).astype(jnp.bfloat16)


def mix_rows(acts, downs, blocks):
    hidden, width = downs[0].shape
    pieces, calls = len(downs), len(acts)
    rows = acts[0].shape[0] * calls // blocks
    vmem = pl.BlockSpec(memory_space=pltpu.VMEM)
    anywhere = pl.BlockSpec(memory_space=pl.ANY)
    return pl.pallas_call(
        functools.partial(mix_kernel, blocks, calls, pieces),
        out_shape=[jax.ShapeDtypeStruct((rows, width), jnp.bfloat16)] * blocks,
        in_specs=[vmem] * calls + [anywhere] * pieces,
        out_specs=[vmem] * blocks,
        scratch_shapes=[
            pltpu.VMEM((pieces * hidden, width), jnp.bfloat16),
            pltpu.SemaphoreType.DMA((pieces,)),
        ],
        compiler_params=pltpu.CompilerParams(vmem_limit_bytes=VMEM_LIMIT),
        cost_estimate=pl.CostEstimate(
            flops=2 * blocks * rows * width * pieces * hidden, bytes_accessed=12 << 20, transcendentals=0
        ),
        name="mix_rows",
    )(*acts, *downs)


def weight_kernel(blocks, calls, *refs):
    x_refs, refs = refs[:blocks], refs[blocks:]
    og_refs, refs = refs[:blocks], refs[blocks:]
    act_refs, refs = refs[:calls], refs[calls:]
    gg_refs, refs = refs[:calls], refs[calls:]
    gu_refs, refs = refs[:calls], refs[calls:]
    in_ref, down_ref, x_t, og_all, act_all, gg_all, gu_all = refs
    rows = x_refs[0].shape[0]

    @pl.when(pl.program_id(0) == 0)
    def _():
        for b in range(blocks):
            x_t[:, b * rows : (b + 1) * rows] = x_refs[b][...].T
            og_all[b * rows : (b + 1) * rows] = og_refs[b][...]

    some = act_refs[0].shape[0]
    for i in range(calls):
        act_all[i * some : (i + 1) * some] = act_refs[i][...]
        gg_all[i * some : (i + 1) * some] = gg_refs[i][...]
        gu_all[i * some : (i + 1) * some] = gu_refs[i][...]
    in_ref[0, 0] = jnp.dot(x_t[...], gg_all[...], preferred_element_type=jnp.float32).astype(jnp.bfloat16)
    in_ref[0, 1] = jnp.dot(x_t[...], gu_all[...], preferred_element_type=jnp.float32).astype(jnp.bfloat16)
    down_ref[0] = jnp.dot(
        act_all[...].T, og_all[...], preferred_element_type=jnp.float32
    ).astype(jnp.bfloat16)


def weight_grads(xs, ogs, acts, ggs, gus, hidden, first, count):
    blocks, calls, (rows, width) = len(xs), len(acts), xs[0].shape
    some = acts[0].shape[0]
    vmem = pl.BlockSpec(memory_space=pltpu.VMEM)
    column = pl.BlockSpec((some, hidden), lambda i: (0, first + i))
    low = jnp.bfloat16
    total = blocks * rows
    return pl.pallas_call(
        functools.partial(weight_kernel, blocks, calls),
        grid=(count,),
        out_shape=[
            jax.ShapeDtypeStruct((count, 2, width, hidden), low),
            jax.ShapeDtypeStruct((count, hidden, width), low),
        ],
        in_specs=[vmem] * (2 * blocks) + [column] * (3 * calls),
        out_specs=[
            pl.BlockSpec((1, 2, width, hidden), lambda i: (i, 0, 0, 0)),
            pl.BlockSpec((1, hidden, width), lambda i: (i, 0, 0)),
        ],
        scratch_shapes=[
            pltpu.VMEM((width, total), low),
            pltpu.VMEM((total, width), low),
            pltpu.VMEM((total, hidden), low),
            pltpu.VMEM((total, hidden), low),
            pltpu.VMEM((total, hidden), low),
        ],
        compiler_params=pltpu.CompilerParams(vmem_limit_bytes=VMEM_LIMIT),
        cost_estimate=pl.CostEstimate(
            flops=2 * 3 * total * width * count * hidden, bytes_accessed=20 << 20, transcendentals=0
        ),
        name="weight_grads",
    )(*xs, *ogs, *acts, *ggs, *gus)


def added(left_mat, right_mat):
    return (left_mat.astype(jnp.float32) + right_mat.astype(jnp.float32)).astype(jnp.bfloat16)


def scatter_pieces(kept, sent):
    back_in, back_down = swap(sent[0], "fsdp", 1), swap(sent[1], "fsdp", 1)
    count = lax.axis_size("tp")
    ins = [added(kept[0][i], back_in[i]) for i in range(2 * count)]
    downs = [added(kept[1][i], back_down[i]) for i in range(2 * count)]
    downs = [added(downs[i], swap(downs[count + i], "fsdp", 2)) for i in range(count)]
    far_in, own_in = ins[count], ins[0]
    for m in range(1, count):
        far_in = added(far_in, swap(ins[count + m], "tp", m))
        own_in = added(own_in, swap(ins[m], "tp", m))
    f32 = jnp.float32
    own_down = downs[0].astype(f32)
    for m in range(1, count):
        own_down += swap(downs[m], "tp", m).astype(f32)
    return own_in.astype(f32) + swap(far_in, "fsdp", 2).astype(f32), own_down


def gather_shards(own):
    near = [own] + [swap(own, "ctx", m) for m in range(1, lax.axis_size("ctx"))]
    near = near + [swap(piece, "fsdp", 2) for piece in near]
    return near + [swap(piece, "fsdp", 1) for piece in near]


def load_shards(place_ref, shard_refs, whole, sems, n_ctx):
    rows = shard_refs[0].shape[0]
    copies = []
    for i, shard in enumerate(shard_refs):
        index = (place_ref[0] ^ F_MASKS[i // n_ctx]) * n_ctx + (place_ref[1] ^ (i % n_ctx))
        at = pl.multiple_of(index * rows, rows)
        copies.append(pltpu.make_async_copy(shard, whole.at[pl.ds(at, rows)], sems.at[i]))
    return copies


def turn(first, second, cosine, sine):
    return first * cosine - second * sine, second * cosine + first * sine


def project_kernel(n_ctx, shards, q_rows, k_rows, v_rows, *refs):
    place, tok, cos_ref, sin_ref = refs[:4]
    shard_refs, refs = refs[4 : 4 + shards], refs[4 + shards :]
    q_ref, kv_ref, norm_t, whole, gain_ref, sems = refs
    copies = load_shards(place, shard_refs, whole, sems, n_ctx)
    for copy in copies:
        copy.start()
    x = tok[...].astype(jnp.float32)
    hat = x * lax.rsqrt(jnp.mean(x * x, axis=-1, keepdims=True) + EPSILON)
    for copy in copies:
        copy.wait()
    columns = q_rows + k_rows + v_rows
    gains = whole[:, columns:].astype(jnp.float32).T
    gain_ref[...] = gains[:8]
    normed = (hat * gains[:1]).astype(jnp.bfloat16)
    norm_t[...] = normed.T
    cosine, sine = cos_ref[...], sin_ref[...]
    half = HD // 2
    heads = jnp.dot(normed, whole[:, :columns], preferred_element_type=jnp.float32).T
    for at in range(0, q_rows, HD):
        a, b = turn(heads[at : at + half], heads[at + half : at + HD], cosine, sine)
        q_ref[at : at + half] = a.astype(jnp.bfloat16) * jnp.bfloat16(HD**-0.5)
        q_ref[at + half : at + HD] = b.astype(jnp.bfloat16) * jnp.bfloat16(HD**-0.5)
    for at in range(0, k_rows, HD):
        here = q_rows + at
        a, b = turn(heads[here : here + half], heads[here + half : here + HD], cosine, sine)
        kv_ref[at : at + half] = a.astype(jnp.bfloat16)
        kv_ref[at + half : at + HD] = b.astype(jnp.bfloat16)
    kv_ref[k_rows:] = heads[q_rows + k_rows :].astype(jnp.bfloat16)


def vmem_spec():
    return pl.BlockSpec(memory_space=pltpu.VMEM)


def any_spec():
    return pl.BlockSpec(memory_space=pl.ANY)


def smem_spec():
    return pl.BlockSpec(memory_space=pltpu.SMEM)


def project(place, tokens, cosine, sine, shards, q_rows, k_rows):
    n_ctx = lax.axis_size("ctx")
    rows, width = tokens.shape
    low = jnp.bfloat16
    columns = shards[0].shape[1]
    return pl.pallas_call(
        functools.partial(project_kernel, n_ctx, len(shards), q_rows, k_rows, k_rows),
        out_shape=[
            jax.ShapeDtypeStruct((q_rows, rows), low),
            jax.ShapeDtypeStruct((2 * k_rows, rows), low),
            jax.ShapeDtypeStruct((width, rows), low),
            jax.ShapeDtypeStruct((width, columns), low),
            jax.ShapeDtypeStruct((8, width), jnp.float32),
        ],
        in_specs=[smem_spec()] + [vmem_spec()] * 3 + [any_spec()] * len(shards),
        out_specs=[vmem_spec()] * 5,
        scratch_shapes=[pltpu.SemaphoreType.DMA((len(shards),))],
        compiler_params=pltpu.CompilerParams(vmem_limit_bytes=VMEM_LIMIT),
        cost_estimate=pl.CostEstimate(
            flops=2 * rows * width * columns, bytes_accessed=12 << 20, transcendentals=0
        ),
        name="project",
    )(place, tokens, cosine, sine, *shards)


def attend_kernel(n_ctx, shards, *refs):
    place, start_ref, q_ref = refs[:3]
    piece_refs, refs = refs[3 : 3 + n_ctx], refs[3 + n_ctx :]
    shard_refs, refs = refs[:shards], refs[shards:]
    p_ref, head_ref, part_ref, kv_all, out_t, bias, scores, q3, sems = refs
    rows = q_ref.shape[1]
    half_kv = kv_all.shape[0] // 2
    step = pl.program_id(0)
    copies = load_shards(place, shard_refs, out_t, sems, n_ctx)

    @pl.when(step == 0)
    def _():
        for copy in copies:
            copy.start()
        key_at = lax.broadcasted_iota(jnp.int32, (rows, rows), 0)
        query_at = lax.broadcasted_iota(jnp.int32, (rows, rows), 1)
        for j in range(n_ctx):
            kv_all[:, j * rows : (j + 1) * rows] = piece_refs[j][...]
            allowed = key_at + (place[1] - j) * rows >= start_ref[...]
            if j == 0:
                allowed = allowed & (key_at <= query_at)
            bias[j * rows : (j + 1) * rows] = jnp.where(allowed, 0.0, -1e30)

    for h in range(GROUP):
        q3[:, h * rows : (h + 1) * rows] = q_ref[h * HD : (h + 1) * HD]
    keys = kv_all[pl.ds(pl.multiple_of(step * HD, HD), HD)]
    values = kv_all[pl.ds(pl.multiple_of(half_kv + step * HD, HD), HD)]
    scores[...] = jnp.dot(keys.T, q3[...], preferred_element_type=jnp.float32)
    for h in range(GROUP):
        cols = slice(h * rows, (h + 1) * rows)
        masked = scores[:, cols] + bias[...]
        exponent = jnp.exp(masked - jnp.max(masked, axis=0, keepdims=True))
        inverse = 1.0 / jnp.sum(exponent, axis=0, keepdims=True)
        p_ref[0, :, cols] = (exponent * inverse).astype(jnp.bfloat16)
    attended = jnp.dot(values, p_ref[0], preferred_element_type=jnp.float32).astype(jnp.bfloat16)
    for h in range(GROUP):
        at = pl.multiple_of((step * GROUP + h) * HD, HD)
        head_ref[pl.ds(at, HD)] = attended[:, h * rows : (h + 1) * rows]

    @pl.when(step == pl.num_programs(0) - 1)
    def _():
        for copy in copies:
            copy.wait()
        part_ref[...] = nt_dot(head_ref[...].T, out_t[...])


def attend(place, starts, q_t, pieces, shards):
    n_ctx = lax.axis_size("ctx")
    q_rows, rows = q_t.shape
    kv = q_rows // (GROUP * HD)
    width = shards[0].shape[0] * len(shards)
    seq = rows * n_ctx
    low = jnp.bfloat16
    return pl.pallas_call(
        functools.partial(attend_kernel, n_ctx, len(shards)),
        grid=(kv,),
        out_shape=[
            jax.ShapeDtypeStruct((kv, seq, GROUP * rows), low),
            jax.ShapeDtypeStruct((q_rows, rows), low),
            jax.ShapeDtypeStruct((rows, width), jnp.float32),
            jax.ShapeDtypeStruct((2 * kv * HD, seq), low),
            jax.ShapeDtypeStruct((width, q_rows), low),
        ],
        in_specs=[smem_spec(), vmem_spec(), pl.BlockSpec((GROUP * HD, rows), lambda i: (i, 0))]
        + [vmem_spec()] * n_ctx
        + [any_spec()] * len(shards),
        out_specs=[pl.BlockSpec((1, seq, GROUP * rows), lambda i: (i, 0, 0))] + [vmem_spec()] * 4,
        scratch_shapes=[
            pltpu.VMEM((seq, rows), jnp.float32),
            pltpu.VMEM((seq, GROUP * rows), jnp.float32),
            pltpu.VMEM((HD, GROUP * rows), low),
            pltpu.SemaphoreType.DMA((len(shards),)),
        ],
        compiler_params=pltpu.CompilerParams(vmem_limit_bytes=VMEM_LIMIT),
        cost_estimate=pl.CostEstimate(
            flops=2 * q_rows * rows * (2 * seq + width), bytes_accessed=20 << 20, transcendentals=0
        ),
        name="attend",
    )(place, starts, q_t, *pieces, *shards)


def attend_back_kernel(n_ctx, *refs):
    p_ref, q_ref, kv_all, grad_ref, out_t, cos_ref, sin_ref = refs[:7]
    dq_ref, own_ref = refs[7:9]
    piece_refs, refs = refs[9 : 8 + n_ctx], refs[8 + n_ctx :]
    grads, q3, g3 = refs
    rows = q_ref.shape[1]
    half_kv = kv_all.shape[0] // 2
    step = pl.program_id(0)

    @pl.when(step == 0)
    def _():
        back = jnp.dot(grad_ref[...], out_t[...], preferred_element_type=jnp.float32)
        grads[...] = back.astype(jnp.bfloat16).T

    for h in range(GROUP):
        cols = slice(h * rows, (h + 1) * rows)
        q3[:, cols] = q_ref[h * HD : (h + 1) * HD]
        g3[:, cols] = grads[pl.ds(pl.multiple_of((step * GROUP + h) * HD, HD), HD)]
    keys = kv_all[pl.ds(pl.multiple_of(step * HD, HD), HD)]
    values = kv_all[pl.ds(pl.multiple_of(half_kv + step * HD, HD), HD)]
    probs = p_ref[0].astype(jnp.float32)
    grad_probs = jnp.dot(values.T, g3[...], preferred_element_type=jnp.float32)
    inner = jnp.sum(probs * grad_probs, axis=0, keepdims=True)
    grad_scores = (probs * (grad_probs - inner)).astype(jnp.bfloat16)
    grad_query = jnp.dot(keys, grad_scores, preferred_element_type=jnp.float32) * HD**-0.5
    grad_key = nt_dot(grad_scores, q3[...]).T
    grad_value = nt_dot(p_ref[0], g3[...]).T
    half = HD // 2
    cosine, sine = cos_ref[...], -sin_ref[...]
    for h in range(GROUP):
        cols = slice(h * rows, (h + 1) * rows)
        a, b = turn(grad_query[:half, cols], grad_query[half:, cols], cosine, sine)
        dq_ref[h * HD : h * HD + half] = a.astype(jnp.bfloat16)
        dq_ref[h * HD + half : (h + 1) * HD] = b.astype(jnp.bfloat16)
    key_at = pl.ds(pl.multiple_of(step * HD, HD), HD)
    value_at = pl.ds(pl.multiple_of(half_kv + step * HD, HD), HD)
    own_ref[key_at] = grad_key[:, :rows]
    own_ref[value_at] = grad_value[:, :rows]
    for j in range(1, n_ctx):
        cols = slice(j * rows, (j + 1) * rows)
        piece_refs[j - 1][key_at] = grad_key[:, cols].astype(jnp.bfloat16)
        piece_refs[j - 1][value_at] = grad_value[:, cols].astype(jnp.bfloat16)


def attend_back(probs, q_t, kv_all, grad_attn, out_t, cosine, sine):
    n_ctx = lax.axis_size("ctx")
    q_rows, rows = q_t.shape
    kv, seq = probs.shape[:2]
    low = jnp.bfloat16
    block = pl.BlockSpec((GROUP * HD, rows), lambda i: (i, 0))
    return pl.pallas_call(
        functools.partial(attend_back_kernel, n_ctx),
        grid=(kv,),
        out_shape=[
            jax.ShapeDtypeStruct((q_rows, rows), low),
            jax.ShapeDtypeStruct((2 * kv * HD, rows), jnp.float32),
        ]
        + [jax.ShapeDtypeStruct((2 * kv * HD, rows), low)] * (n_ctx - 1),
        in_specs=[pl.BlockSpec((1, seq, GROUP * rows), lambda i: (i, 0, 0)), block] + [vmem_spec()] * 5,
        out_specs=[block] + [vmem_spec()] * n_ctx,
        scratch_shapes=[
            pltpu.VMEM((q_rows, rows), low),
            pltpu.VMEM((HD, GROUP * rows), low),
            pltpu.VMEM((HD, GROUP * rows), low),
        ],
        compiler_params=pltpu.CompilerParams(vmem_limit_bytes=VMEM_LIMIT),
        cost_estimate=pl.CostEstimate(
            flops=2 * q_rows * rows * (4 * seq + out_t.shape[0]), bytes_accessed=20 << 20, transcendentals=0
        ),
        name="attend_back",
    )(probs, q_t, kv_all, grad_attn, out_t, cosine, sine)


def store_products(place, left_t, right, out_refs):
    rows = out_refs[0].shape[0]
    for mask, out in zip(F_MASKS, out_refs):
        at = pl.multiple_of((place[0] ^ mask) * rows, rows)
        out[...] = jnp.dot(
            left_t[pl.ds(at, rows)], right, preferred_element_type=jnp.float32
        ).astype(jnp.bfloat16)


def out_grad_kernel(place, grad_ref, head_ref, *refs):
    out_refs, grad_t = refs[:-1], refs[-1]
    grad_t[...] = grad_ref[...].T
    store_products(place, grad_t, head_ref[...].T, out_refs)


def out_weight_grads(place, grad_attn, head_t):
    rows, width = grad_attn.shape
    parts = len(F_MASKS)
    return pl.pallas_call(
        out_grad_kernel,
        out_shape=[jax.ShapeDtypeStruct((width // parts, head_t.shape[0]), jnp.bfloat16)] * parts,
        in_specs=[smem_spec()] + [vmem_spec()] * 2,
        out_specs=[vmem_spec()] * parts,
        scratch_shapes=[pltpu.VMEM((width, rows), jnp.bfloat16)],
        compiler_params=pltpu.CompilerParams(vmem_limit_bytes=VMEM_LIMIT),
        cost_estimate=pl.CostEstimate(
            flops=2 * rows * width * head_t.shape[0], bytes_accessed=5 << 20, transcendentals=0
        ),
        name="out_weight_grads",
    )(place, grad_attn, head_t)


def query_grad_kernel(place, dq_ref, norm_t, whole, *refs):
    out_refs, part_ref = refs[:-1], refs[-1]
    back = dq_ref[...].T
    store_products(place, norm_t, back, out_refs)
    part_ref[...] = nt_dot(back, whole[:, : back.shape[1]])


def query_grads(place, dq_t, norm_t, whole):
    q_rows, rows = dq_t.shape
    width = norm_t.shape[0]
    parts = len(F_MASKS)
    outs = pl.pallas_call(
        query_grad_kernel,
        out_shape=[jax.ShapeDtypeStruct((width // parts, q_rows), jnp.bfloat16)] * parts
        + [jax.ShapeDtypeStruct((rows, width), jnp.float32)],
        in_specs=[smem_spec()] + [vmem_spec()] * 3,
        out_specs=[vmem_spec()] * (parts + 1),
        compiler_params=pltpu.CompilerParams(vmem_limit_bytes=VMEM_LIMIT),
        cost_estimate=pl.CostEstimate(
            flops=4 * rows * width * q_rows, bytes_accessed=10 << 20, transcendentals=0
        ),
        name="query_grads",
    )(place, dq_t, norm_t, whole)
    return outs[:parts], outs[parts]


def key_grad_kernel(n_ctx, q_rows, *refs):
    place, own_ref = refs[:2]
    piece_refs, refs = refs[2 : 1 + n_ctx], refs[1 + n_ctx :]
    cos_ref, sin_ref, norm_t, whole, tok, query_part, gain_two_ref = refs[:7]
    out_refs, part_ref, back_t, right = refs[7:-3], refs[-3], refs[-2], refs[-1]
    kv_rows, rows = own_ref.shape
    total = own_ref[...]
    for piece in piece_refs:
        total += piece[...].astype(jnp.float32)
    cosine, sine = cos_ref[...], -sin_ref[...]
    half = HD // 2
    for at in range(0, kv_rows // 2, HD):
        a, b = turn(total[at : at + half], total[at + half : at + HD], cosine, sine)
        back_t[at : at + half] = a.astype(jnp.bfloat16)
        back_t[at + half : at + HD] = b.astype(jnp.bfloat16)
    back_t[kv_rows // 2 :] = total[kv_rows // 2 :].astype(jnp.bfloat16)
    back = back_t[...].T
    part = query_part[...] + nt_dot(back, whole[:, q_rows : q_rows + kv_rows])
    part_ref[...] = part
    store_products(place, norm_t, back, [out.at[:, :kv_rows] for out in out_refs])
    x = tok[...].astype(jnp.float32)
    hat = x * lax.rsqrt(jnp.mean(x * x, axis=-1, keepdims=True) + EPSILON)
    gain_one = jnp.sum(part * hat, axis=0, keepdims=True)
    row = lax.broadcasted_iota(jnp.int32, (128, x.shape[1]), 0)
    columns = jnp.where(row == 0, gain_one, jnp.where(row == 1, gain_two_ref[...], 0.0))
    right[...] = columns.T
    count = out_refs[0].shape[0]
    for mask, out in zip(F_MASKS, out_refs):
        at = pl.multiple_of((place[0] ^ mask) * count, count)
        out[:, kv_rows:] = right[pl.ds(at, count)].astype(jnp.bfloat16)


def key_grads(place, own, pieces, cosine, sine, norm_t, whole, tokens, query_part, gain_two, q_rows):
    n_ctx = lax.axis_size("ctx")
    kv_rows, rows = own.shape
    width = norm_t.shape[0]
    parts = len(F_MASKS)
    outs = pl.pallas_call(
        functools.partial(key_grad_kernel, n_ctx, q_rows),
        out_shape=[jax.ShapeDtypeStruct((width // parts, kv_rows + 128), jnp.bfloat16)] * parts
        + [jax.ShapeDtypeStruct((rows, width), jnp.float32)],
        in_specs=[smem_spec()] + [vmem_spec()] * (n_ctx + 7),
        out_specs=[vmem_spec()] * (parts + 1),
        scratch_shapes=[
            pltpu.VMEM((kv_rows, rows), jnp.bfloat16),
            pltpu.VMEM((width, 128), jnp.float32),
        ],
        compiler_params=pltpu.CompilerParams(vmem_limit_bytes=VMEM_LIMIT),
        cost_estimate=pl.CostEstimate(
            flops=4 * rows * width * kv_rows, bytes_accessed=12 << 20, transcendentals=0
        ),
        name="key_grads",
    )(place, own, *pieces, cosine, sine, norm_t, whole, tokens, query_part, gain_two)
    return outs[:parts], outs[parts]


def scatter_rows(parts):
    n_ctx = lax.axis_size("ctx")
    ctx_index = lax.axis_index("ctx")
    near, far, near_core, far_core = parts
    far = added(far, swap(far_core, "fsdp", 1))
    near = added(near, swap(near_core, "fsdp", 1))
    near = added(near, swap(far, "fsdp", 2))
    rows = near.shape[0] // n_ctx

    def block(mask):
        return lax.dynamic_slice_in_dim(near, (ctx_index ^ mask) * rows, rows)

    total = block(0).astype(jnp.float32)
    for m in range(1, n_ctx):
        total += swap(block(m), "ctx", m).astype(jnp.float32)
    return total


def shift(value, distance):
    size = lax.axis_size("ctx")
    pairs = [(i, i - distance) for i in range(size) if 0 <= i - distance < size]
    return lax.ppermute(value, "ctx", pairs)


def advance(weight, gradient, moment, average, step_rate):
    moment_new = MOMENTUM * moment + gradient
    weight_new = weight - step_rate * (gradient + MOMENTUM * moment_new)
    average_new = AVERAGE * average + (1.0 - AVERAGE) * weight_new
    return (moment_new, average_new, weight_new)


def per_device(
    tokens,
    out_grad,
    lengths,
    routes,
    gate_weights,
    qkv_weight,
    out_weight,
    norm_gains,
    expert_in,
    expert_down,
    qkv_moment,
    qkv_average,
    out_moment,
    out_average,
    gain_moment,
    gain_average,
    in_moment,
    in_average,
    down_moment,
    down_average,
):
    tok_rows = tokens.shape[0]
    n_ctx = lax.axis_size("ctx")
    experts = lax.axis_size(("fsdp", "ctx"))
    fsdp_index, ctx_index = lax.axis_index("fsdp"), lax.axis_index("ctx")
    place = jnp.stack([fsdp_index, ctx_index]).astype(jnp.int32)
    low = jnp.bfloat16
    shard_rows, qkv_columns = qkv_weight.shape
    kv_local = qkv_columns // ((GROUP + 2) * HD)
    q_rows, k_rows = kv_local * GROUP * HD, kv_local * HD
    by_head = qkv_weight.astype(low).reshape(shard_rows, kv_local, GROUP + 2, HD)
    gain_columns = jnp.pad(norm_gains.astype(low).T, ((0, 0), (0, 126)))
    qkv_own = jnp.concatenate(
        [
            by_head[:, :, :GROUP].reshape(shard_rows, q_rows),
            by_head[:, :, GROUP].reshape(shard_rows, k_rows),
            by_head[:, :, GROUP + 1].reshape(shard_rows, k_rows),
            gain_columns,
        ],
        axis=1,
    )
    qkv_shards = gather_shards(qkv_own)
    out_shards = gather_shards(out_weight.astype(low).T)
    places = ctx_index * tok_rows + jnp.arange(tok_rows, dtype=jnp.int32)
    _, position = doc_positions(lengths[0], places)
    starts = (places - position)[None, :]
    frequency = jnp.exp(
        jnp.arange(HD // 2, dtype=jnp.float32) * (-2.0 * math.log(ROPE_BASE) / HD)
    )
    angles = frequency[:, None] * position.astype(jnp.float32)[None, :]
    cosine, sine = jnp.cos(angles), jnp.sin(angles)
    inputs = tokens.astype(jnp.float32)
    inverse_one = lax.rsqrt(jnp.mean(inputs * inputs, axis=-1, keepdims=True) + EPSILON)
    normed_one = inputs * inverse_one
    q_t, kv_t, norm_t, qkv_whole, gains = project(
        place, tokens, cosine, sine, qkv_shards, q_rows, k_rows
    )
    gain_one, gain_two = gains[0], gains[1]
    kv_pieces = [kv_t] + [shift(kv_t, -j) for j in range(1, n_ctx)]
    probs, head_t, attn_part, kv_all, out_t = attend(place, starts, q_t, kv_pieces, out_shards)
    half_rows = tok_rows // lax.axis_size("tp")
    tp_index = lax.axis_index("tp")
    fsdp_index, ctx_index = lax.axis_index("fsdp"), lax.axis_index("ctx")

    over_tp = range(lax.axis_size("tp"))

    def part_of(value, mask):
        return lax.dynamic_slice_in_dim(value, (tp_index ^ mask) * half_rows, half_rows)

    def own_half(value):
        return part_of(value, 0)

    def sum_own(value):
        total = own_half(value)
        for m in over_tp[1:]:
            total += swap(part_of(value, m).astype(jnp.bfloat16), "tp", m).astype(jnp.float32)
        return total

    def both_halves(own):
        parts = [own] + [swap(own, "tp", m) for m in over_tp[1:]]
        ordered = []
        for at in over_tp:
            chosen = parts[0]
            for m in over_tp[1:]:
                chosen = jnp.where(tp_index ^ m == at, parts[m], chosen)
            ordered.append(chosen)
        return jnp.concatenate(ordered, axis=0)

    attn_sum = sum_own(attn_part)
    hidden_one = own_half(inputs) + attn_sum
    inverse_two = lax.rsqrt(jnp.mean(hidden_one * hidden_one, axis=-1, keepdims=True) + EPSILON)
    normed_two = hidden_one * inverse_two
    normed_two_low = (normed_two * gain_two).astype(jnp.bfloat16)

    ins, downs = gather_pieces(expert_in[0].astype(jnp.bfloat16), expert_down[0].astype(jnp.bfloat16))
    expert_ids = jnp.arange(experts, dtype=jnp.int32)
    dense_gates = jnp.sum(
        jnp.where(
            own_half(routes)[:, :, None] == expert_ids[None, None, :],
            own_half(gate_weights)[:, :, None],
            0.0,
        ),
        axis=1,
    )
    grad_own = own_half(out_grad)
    xs = [normed_two_low] + [swap(normed_two_low, "ctx", m) for m in range(1, n_ctx)]
    ogs = [grad_own] + [swap(grad_own, "ctx", m) for m in range(1, n_ctx)]
    all_gates = [dense_gates] + [swap(dense_gates, "ctx", m) for m in range(1, n_ctx)]

    def of_pieces(block_gates):
        columns = []
        for f_mask in F_MASKS:
            expert = (fsdp_index ^ f_mask) * n_ctx + ctx_index
            columns.append(
                jnp.sum(jnp.where(expert_ids[None, :] == expert, block_gates, 0.0), axis=1)
            )
        return jnp.stack(columns)[:, :, None]

    all_gates = [of_pieces(g) for g in all_gates]
    grads_x, acts, ggs, gus = [], [], [], []
    for at in range(0, n_ctx, 2):
        some_x, (act, gg, gu) = expert_rows(
            xs[at : at + 2], ogs[at : at + 2], all_gates[at : at + 2], ins, downs
        )
        grads_x += some_x
        acts.append(act)
        ggs.append(gg)
        gus.append(gu)
    grad_normed_two = grads_x[0].astype(jnp.float32)
    for m in range(1, n_ctx):
        grad_normed_two += swap(grads_x[m], "ctx", m).astype(jnp.float32)
    mixes = mix_rows(acts, downs, n_ctx)
    mixture = mixes[0].astype(jnp.float32)
    for m in range(1, n_ctx):
        mixture += swap(mixes[m], "ctx", m).astype(jnp.float32)
    block_out = both_halves((hidden_one + mixture).astype(jnp.bfloat16))
    hidden, near = downs[0].shape[0], len(downs) // 2
    sent = weight_grads(xs, ogs, acts, ggs, gus, hidden, near, near)
    kept = weight_grads(xs, ogs, acts, ggs, gus, hidden, 0, near)
    in_grad_sum, down_grad_sum = scatter_pieces(kept, sent)

    gain_grad_two = jnp.sum(grad_normed_two * normed_two, axis=0)
    grad_hidden_half = grad_own.astype(jnp.float32) + norm_back(
        grad_normed_two, normed_two, inverse_two, gain_two
    )
    grad_attn = both_halves(grad_hidden_half.astype(jnp.bfloat16))
    out_parts = out_weight_grads(place, grad_attn, head_t)
    out_grad_sum = scatter_rows(out_parts).T
    dq_t, own_grads, *far_grads = attend_back(probs, q_t, kv_all, grad_attn, out_t, cosine, sine)
    query_parts, query_part = query_grads(place, dq_t, norm_t, qkv_whole)
    come = [shift(far_grads[j - 1], j) for j in range(1, n_ctx)]
    key_parts, grad_normed_part = key_grads(
        place, own_grads, come, cosine, sine, norm_t, qkv_whole, tokens, query_part,
        gain_grad_two[None], q_rows,
    )
    grad_normed_one = sum_own(grad_normed_part)
    normed_one_half = own_half(normed_one)
    in_grad = both_halves(
        (
            grad_hidden_half
            + norm_back(grad_normed_one, normed_one_half, own_half(inverse_one), gain_one)
        ).astype(jnp.bfloat16)
    )
    query_grad, key_grad = scatter_rows(query_parts), scatter_rows(key_parts)
    gains_grad = key_grad[:, 2 * k_rows : 2 * k_rows + 2].T
    gains_grad = gains_grad + sum(swap(gains_grad, "tp", m) for m in over_tp[1:])
    qkv_grad = jnp.concatenate(
        [
            query_grad.reshape(shard_rows, kv_local, GROUP, HD),
            key_grad[:, :k_rows].reshape(shard_rows, kv_local, 1, HD),
            key_grad[:, k_rows : 2 * k_rows].reshape(shard_rows, kv_local, 1, HD),
        ],
        axis=2,
    ).reshape(shard_rows, qkv_columns)
    in_grad_local = in_grad_sum[None]
    down_grad_local = down_grad_sum[None]
    qkv_new = advance(qkv_weight, qkv_grad, qkv_moment, qkv_average, RATE_QKV)
    out_new = advance(out_weight, out_grad_sum, out_moment, out_average, RATE_OUT)
    gain_new = advance(norm_gains, gains_grad, gain_moment, gain_average, RATE_GAIN)
    in_new = advance(expert_in, in_grad_local, in_moment, in_average, RATE_IN)
    down_new = advance(expert_down, down_grad_local, down_moment, down_average, RATE_DOWN)
    return (
        block_out,
        in_grad,
        qkv_new[0],
        qkv_new[1],
        qkv_new[2],
        out_new[0],
        out_new[1],
        out_new[2],
        gain_new[0],
        gain_new[1],
        gain_new[2],
        in_new[0],
        in_new[1],
        in_new[2],
        down_new[0],
        down_new[1],
        down_new[2],
    )


def solution(mesh):
    return jax.shard_map(
        per_device,
        mesh=mesh,
        in_specs=(
            P(("fsdp", "ctx"), None),
            P(("fsdp", "ctx"), None),
            P("fsdp", None),
            P(("fsdp", "ctx"), None),
            P(("fsdp", "ctx"), None),
            P(("fsdp", "ctx"), "tp"),
            P("tp", ("fsdp", "ctx")),
            P(None, ("fsdp", "ctx")),
            P(("fsdp", "ctx"), None, None, "tp"),
            P(("fsdp", "ctx"), "tp", None),
            P(("fsdp", "ctx"), "tp"),
            P(("fsdp", "ctx"), "tp"),
            P("tp", ("fsdp", "ctx")),
            P("tp", ("fsdp", "ctx")),
            P(None, ("fsdp", "ctx")),
            P(None, ("fsdp", "ctx")),
            P(("fsdp", "ctx"), None, None, "tp"),
            P(("fsdp", "ctx"), None, None, "tp"),
            P(("fsdp", "ctx"), "tp", None),
            P(("fsdp", "ctx"), "tp", None),
        ),
        out_specs=(
            P(("fsdp", "ctx"), None),
            P(("fsdp", "ctx"), None),
            P(("fsdp", "ctx"), "tp"),
            P(("fsdp", "ctx"), "tp"),
            P(("fsdp", "ctx"), "tp"),
            P("tp", ("fsdp", "ctx")),
            P("tp", ("fsdp", "ctx")),
            P("tp", ("fsdp", "ctx")),
            P(None, ("fsdp", "ctx")),
            P(None, ("fsdp", "ctx")),
            P(None, ("fsdp", "ctx")),
            P(("fsdp", "ctx"), None, None, "tp"),
            P(("fsdp", "ctx"), None, None, "tp"),
            P(("fsdp", "ctx"), None, None, "tp"),
            P(("fsdp", "ctx"), "tp", None),
            P(("fsdp", "ctx"), "tp", None),
            P(("fsdp", "ctx"), "tp", None),
        ),
        check_vma=False,
    )
```

```python
import functools
import math

import jax
import jax.numpy as jnp
from jax import lax
from jax.experimental import pallas as pl
from jax.experimental.pallas import tpu as pltpu
from jax.sharding import PartitionSpec as P

HD = 64
GROUP = 3


EPSILON = 1e-05
ROPE_BASE = 10000.0
MOMENTUM = 0.9
AVERAGE = 0.7
RATE_QKV = 7e-05
RATE_OUT = 0.15
RATE_GAIN = 0.0005
RATE_IN = 0.0004
RATE_DOWN = 0.001


def doc_positions(lengths_row, places):
    doc_ends = jnp.cumsum(lengths_row)
    passed = places[:, None] >= doc_ends[None, :]
    segment = jnp.sum(passed.astype(jnp.int32), axis=1)
    doc_start = jnp.sum(jnp.where(passed, lengths_row[None, :], 0), axis=1)
    return (segment, places - doc_start)


def norm_back(grad_out, normed, inverse, gain_row):
    scaled = grad_out * gain_row
    return inverse * (scaled - normed * jnp.mean(scaled * normed, axis=-1, keepdims=True))


F_MASKS = (0, 2, 1, 3)
VMEM_LIMIT = 60 * 1024 * 1024


def advance(weight, gradient, moment, average, step_rate):
    moment_new = MOMENTUM * moment + gradient
    weight_new = weight - step_rate * (gradient + MOMENTUM * moment_new)
    average_new = AVERAGE * average + (1.0 - AVERAGE) * weight_new
    return (moment_new, average_new, weight_new)


def swap(value, axis, mask):
    size = lax.axis_size(axis)
    return lax.ppermute(value, axis, [(i, i ^ mask) for i in range(size)])


def after(value, *others):
    return lax.optimization_barrier((value, *others))[0]


def nt_dot(left_mat, right_mat):
    return lax.dot_general(
        left_mat, right_mat, (((1,), (1,)), ((), ())), preferred_element_type=jnp.float32
    )


def vmem_spec():
    return pl.BlockSpec(memory_space=pltpu.VMEM)


def any_spec():
    return pl.BlockSpec(memory_space=pl.ANY)


def smem_spec():
    return pl.BlockSpec(memory_space=pltpu.SMEM)


def added(left_mat, right_mat):
    return (left_mat.astype(jnp.float32) + right_mat.astype(jnp.float32)).astype(jnp.bfloat16)


def params():
    return pltpu.CompilerParams(vmem_limit_bytes=VMEM_LIMIT)


def cost(flops, mib):
    return pl.CostEstimate(flops=1, bytes_accessed=1, transcendentals=0)


def spread(blocks):
    return lax.all_to_all(blocks, "ctx", split_axis=0, concat_axis=0, tiled=True)


def gather_along_ctx(own):
    return spread(jnp.broadcast_to(own[None], (lax.axis_size("ctx"), *own.shape)))


def load_shards(place_ref, shard_refs, whole, sems, first=0):
    cols = slice(first, first + whole.shape[1])
    rows = shard_refs[0].shape[0]
    copies = []
    for i, shard in enumerate(shard_refs):
        at = pl.multiple_of((place_ref[0] ^ F_MASKS[i]) * rows, rows)
        copies.append(pltpu.make_async_copy(shard.at[:, cols], whole.at[pl.ds(at, rows)], sems.at[i]))
    return copies


def turn(first, second, cosine, sine):
    return first * cosine - second * sine, second * cosine + first * sine


def project_keys_kernel(k_rows, *refs):
    place, tok, cos_ref, sin_ref = refs[:4]
    shard_refs, refs = refs[4 : 4 + len(F_MASKS)], refs[4 + len(F_MASKS) :]
    kv_ref, norm_ref, norm_t, whole, gain_ref, sems = refs
    copies = load_shards(place, shard_refs, whole, sems)
    for copy in copies:
        copy.start()
    x = tok[...].astype(jnp.float32)
    hat = x * lax.rsqrt(jnp.mean(x * x, axis=-1, keepdims=True) + EPSILON)
    for copy in copies:
        copy.wait()
    gains = whole[:, 2 * k_rows :].astype(jnp.float32).T
    gain_ref[...] = gains[:8]
    normed = (hat * gains[:1]).astype(jnp.bfloat16)
    norm_ref[...] = normed
    norm_t[...] = normed.T
    cosine, sine = cos_ref[...], sin_ref[...]
    half = HD // 2
    heads = jnp.dot(normed, whole[:, : 2 * k_rows], preferred_element_type=jnp.float32).T
    for at in range(0, k_rows, HD):
        a, b = turn(heads[at : at + half], heads[at + half : at + HD], cosine, sine)
        kv_ref[at : at + half] = a.astype(jnp.bfloat16)
        kv_ref[at + half : at + HD] = b.astype(jnp.bfloat16)
    kv_ref[k_rows:] = heads[k_rows:].astype(jnp.bfloat16)


def project_keys(place, tokens, cosine, sine, shards, k_rows):
    rows, width = tokens.shape
    low = jnp.bfloat16
    columns = shards[0].shape[1]
    return pl.pallas_call(
        functools.partial(project_keys_kernel, k_rows),
        out_shape=[
            jax.ShapeDtypeStruct((2 * k_rows, rows), low),
            jax.ShapeDtypeStruct((rows, width), low),
            jax.ShapeDtypeStruct((width, rows), low),
            jax.ShapeDtypeStruct((width, columns), low),
            jax.ShapeDtypeStruct((8, width), jnp.float32),
        ],
        in_specs=[smem_spec()] + [vmem_spec()] * 3 + [any_spec()] * len(shards),
        out_specs=[vmem_spec()] * 5,
        scratch_shapes=[pltpu.SemaphoreType.DMA((len(shards),))],
        compiler_params=params(),
        cost_estimate=cost(2 * rows * width * columns, 8),
        name="project_keys",
    )(place, tokens, cosine, sine, *shards)


def project_queries_kernel(*refs):
    place, norm_ref, cos_ref, sin_ref = refs[:4]
    shard_refs, refs = refs[4 : 4 + len(F_MASKS)], refs[4 + len(F_MASKS) :]
    q_ref, whole, sems = refs
    copies = load_shards(place, shard_refs, whole, sems)
    for copy in copies:
        copy.start()
    for copy in copies:
        copy.wait()
    cosine, sine = cos_ref[...], sin_ref[...]
    half = HD // 2
    heads = jnp.dot(norm_ref[...], whole[...], preferred_element_type=jnp.float32).T
    scale = jnp.bfloat16(HD**-0.5)
    for at in range(0, q_ref.shape[0], HD):
        a, b = turn(heads[at : at + half], heads[at + half : at + HD], cosine, sine)
        q_ref[at : at + half] = a.astype(jnp.bfloat16) * scale
        q_ref[at + half : at + HD] = b.astype(jnp.bfloat16) * scale


def project_queries(place, normed, cosine, sine, shards):
    rows, width = normed.shape
    low = jnp.bfloat16
    columns = shards[0].shape[1] // 2
    return pl.pallas_call(
        project_queries_kernel,
        out_shape=[
            jax.ShapeDtypeStruct((columns, rows), low),
            jax.ShapeDtypeStruct((width, columns), low),
        ],
        in_specs=[smem_spec()] + [vmem_spec()] * 3 + [any_spec()] * len(shards),
        out_specs=[vmem_spec()] * 2,
        scratch_shapes=[pltpu.SemaphoreType.DMA((len(shards),))],
        compiler_params=params(),
        cost_estimate=cost(2 * rows * width * columns, 8),
        name="project_queries",
    )(place, normed, cosine, sine, *shards)


def attend_kernel(n_ctx, *refs):
    place, start_ref, q_ref, piece_ref = refs[:4]
    refs = refs[4:]
    shard_refs, refs = refs[: len(F_MASKS)], refs[len(F_MASKS) :]
    p_ref, head_ref, part_ref, kv_all, out_t, bias, scores, q3, sems = refs
    rows = q_ref.shape[1]
    half_kv = kv_all.shape[0] // 2
    step = pl.program_id(0)
    copies = load_shards(place, shard_refs, out_t, sems, out_t.shape[1])

    @pl.when(step == 0)
    def _():
        for copy in copies:
            copy.start()
        key_at = lax.broadcasted_iota(jnp.int32, (rows, rows), 0)
        query_at = lax.broadcasted_iota(jnp.int32, (rows, rows), 1)
        for j in range(n_ctx):
            kv_all[:, j * rows : (j + 1) * rows] = piece_ref[j]
            allowed = key_at + j * rows >= start_ref[...]
            allowed = allowed & (key_at + j * rows <= query_at + place[1] * rows)
            bias[j * rows : (j + 1) * rows] = jnp.where(allowed, 0.0, -1e30)

    for h in range(GROUP):
        q3[:, h * rows : (h + 1) * rows] = q_ref[h * HD : (h + 1) * HD]
    keys = kv_all[pl.ds(pl.multiple_of(step * HD, HD), HD)]
    values = kv_all[pl.ds(pl.multiple_of(half_kv + step * HD, HD), HD)]
    scores[...] = jnp.dot(keys.T, q3[...], preferred_element_type=jnp.float32)
    for h in range(GROUP):
        cols = slice(h * rows, (h + 1) * rows)
        masked = scores[:, cols] + bias[...]
        exponent = jnp.exp(masked - jnp.max(masked, axis=0, keepdims=True))
        inverse = 1.0 / jnp.sum(exponent, axis=0, keepdims=True)
        p_ref[0, :, cols] = (exponent * inverse).astype(jnp.bfloat16)
    attended = jnp.dot(values, p_ref[0], preferred_element_type=jnp.float32).astype(jnp.bfloat16)
    for h in range(GROUP):
        at = pl.multiple_of((step * GROUP + h) * HD, HD)
        head_ref[pl.ds(at, HD)] = attended[:, h * rows : (h + 1) * rows]

    @pl.when(step == pl.num_programs(0) - 1)
    def _():
        for copy in copies:
            copy.wait()
        part_ref[...] = nt_dot(head_ref[...].T, out_t[...])


def attend(place, starts, q_t, pieces, shards):
    n_ctx = lax.axis_size("ctx")
    q_rows, rows = q_t.shape
    kv = q_rows // (GROUP * HD)
    width = shards[0].shape[0] * len(shards)
    seq = rows * n_ctx
    low = jnp.bfloat16
    return pl.pallas_call(
        functools.partial(attend_kernel, n_ctx),
        grid=(kv,),
        out_shape=[
            jax.ShapeDtypeStruct((kv, seq, GROUP * rows), low),
            jax.ShapeDtypeStruct((q_rows, rows), low),
            jax.ShapeDtypeStruct((rows, width), jnp.float32),
            jax.ShapeDtypeStruct((2 * kv * HD, seq), low),
            jax.ShapeDtypeStruct((width, q_rows), low),
        ],
        in_specs=[smem_spec(), vmem_spec(), pl.BlockSpec((GROUP * HD, rows), lambda i: (i, 0))]
        + [vmem_spec()]
        + [any_spec()] * len(shards),
        out_specs=[pl.BlockSpec((1, seq, GROUP * rows), lambda i: (i, 0, 0))] + [vmem_spec()] * 4,
        scratch_shapes=[
            pltpu.VMEM((seq, rows), jnp.float32),
            pltpu.VMEM((seq, GROUP * rows), jnp.float32),
            pltpu.VMEM((HD, GROUP * rows), low),
            pltpu.SemaphoreType.DMA((len(shards),)),
        ],
        compiler_params=pltpu.CompilerParams(vmem_limit_bytes=VMEM_LIMIT),
        cost_estimate=pl.CostEstimate(
            flops=2 * q_rows * rows * (2 * seq + width), bytes_accessed=20 << 20, transcendentals=0
        ),
        name="attend",
    )(place, starts, q_t, pieces, *shards)


def attend_back_kernel(n_ctx, *refs):
    p_ref, q_ref, kv_all, grad_ref, out_t, cos_ref, sin_ref = refs[:7]
    dq_ref, piece_ref, grads, q3, g3 = refs[7:]
    rows = q_ref.shape[1]
    half_kv = kv_all.shape[0] // 2
    step = pl.program_id(0)

    @pl.when(step == 0)
    def _():
        back = jnp.dot(grad_ref[...], out_t[...], preferred_element_type=jnp.float32)
        grads[...] = back.astype(jnp.bfloat16).T

    for h in range(GROUP):
        cols = slice(h * rows, (h + 1) * rows)
        q3[:, cols] = q_ref[h * HD : (h + 1) * HD]
        g3[:, cols] = grads[pl.ds(pl.multiple_of((step * GROUP + h) * HD, HD), HD)]
    keys = kv_all[pl.ds(pl.multiple_of(step * HD, HD), HD)]
    values = kv_all[pl.ds(pl.multiple_of(half_kv + step * HD, HD), HD)]
    probs = p_ref[0].astype(jnp.float32)
    grad_probs = jnp.dot(values.T, g3[...], preferred_element_type=jnp.float32)
    inner = jnp.sum(probs * grad_probs, axis=0, keepdims=True)
    grad_scores = (probs * (grad_probs - inner)).astype(jnp.bfloat16)
    grad_query = jnp.dot(keys, grad_scores, preferred_element_type=jnp.float32) * HD**-0.5
    grad_key = nt_dot(grad_scores, q3[...]).T
    grad_value = nt_dot(p_ref[0], g3[...]).T
    half = HD // 2
    cosine, sine = cos_ref[...], -sin_ref[...]
    for h in range(GROUP):
        cols = slice(h * rows, (h + 1) * rows)
        a, b = turn(grad_query[:half, cols], grad_query[half:, cols], cosine, sine)
        dq_ref[h * HD : h * HD + half] = a.astype(jnp.bfloat16)
        dq_ref[h * HD + half : (h + 1) * HD] = b.astype(jnp.bfloat16)
    key_at = pl.ds(pl.multiple_of(step * HD, HD), HD)
    value_at = pl.ds(pl.multiple_of(half_kv + step * HD, HD), HD)
    for j in range(n_ctx):
        cols = slice(j * rows, (j + 1) * rows)
        piece_ref[j, key_at] = grad_key[:, cols].astype(jnp.bfloat16)
        piece_ref[j, value_at] = grad_value[:, cols].astype(jnp.bfloat16)


def attend_back(probs, q_t, kv_all, grad_attn, out_t, cosine, sine):
    n_ctx = lax.axis_size("ctx")
    q_rows, rows = q_t.shape
    kv, seq = probs.shape[:2]
    low = jnp.bfloat16
    block = pl.BlockSpec((GROUP * HD, rows), lambda i: (i, 0))
    return pl.pallas_call(
        functools.partial(attend_back_kernel, n_ctx),
        grid=(kv,),
        out_shape=[
            jax.ShapeDtypeStruct((q_rows, rows), low),
            jax.ShapeDtypeStruct((n_ctx, 2 * kv * HD, rows), low),
        ],
        in_specs=[pl.BlockSpec((1, seq, GROUP * rows), lambda i: (i, 0, 0)), block] + [vmem_spec()] * 5,
        out_specs=[block, vmem_spec()],
        scratch_shapes=[
            pltpu.VMEM((q_rows, rows), low),
            pltpu.VMEM((HD, GROUP * rows), low),
            pltpu.VMEM((HD, GROUP * rows), low),
        ],
        compiler_params=pltpu.CompilerParams(vmem_limit_bytes=VMEM_LIMIT),
        cost_estimate=pl.CostEstimate(
            flops=2 * q_rows * rows * (4 * seq + out_t.shape[0]), bytes_accessed=20 << 20, transcendentals=0
        ),
        name="attend_back",
    )(probs, q_t, kv_all, grad_attn, out_t, cosine, sine)


def store_products(place, left_t, right, out_refs):
    rows = out_refs[0].shape[0]
    for mask, out in zip(F_MASKS, out_refs):
        at = pl.multiple_of((place[0] ^ mask) * rows, rows)
        out[...] = jnp.dot(
            left_t[pl.ds(at, rows)], right, preferred_element_type=jnp.float32
        ).astype(jnp.bfloat16)


def query_grad_kernel(place, dq_ref, norm_t, whole, grad_ref, head_ref, near, far, core, part_ref, grad_t):
    columns = whole.shape[1]
    back = dq_ref[...].T
    outs = [near, far, core.at[0], core.at[1]]
    store_products(place, norm_t, back, [out.at[:, :columns] for out in outs])
    grad_t[...] = grad_ref[...].T
    store_products(place, grad_t, head_ref[...].T, [out.at[:, columns:] for out in outs])
    part_ref[...] = nt_dot(back, whole[...])


def row_parts(rows, columns):
    low = jnp.bfloat16
    return [
        jax.ShapeDtypeStruct((rows, columns), low),
        jax.ShapeDtypeStruct((rows, columns), low),
        jax.ShapeDtypeStruct((2, rows, columns), low),
    ]


def query_grads(place, dq_t, norm_t, whole, grad_attn, head_t):
    q_rows, rows = dq_t.shape
    width = norm_t.shape[0]
    outs = pl.pallas_call(
        query_grad_kernel,
        out_shape=row_parts(width // len(F_MASKS), 2 * q_rows)
        + [jax.ShapeDtypeStruct((rows, width), jnp.float32)],
        in_specs=[smem_spec()] + [vmem_spec()] * 5,
        out_specs=[vmem_spec()] * 4,
        scratch_shapes=[pltpu.VMEM((width, rows), jnp.bfloat16)],
        compiler_params=params(),
        cost_estimate=cost(6 * rows * width * q_rows, 15),
        name="query_grads",
    )(place, dq_t, norm_t, whole, grad_attn, head_t)
    return outs[:3], outs[3]


def key_grad_kernel(n_ctx, *refs):
    place, piece_ref = refs[:2]
    refs = refs[2:]
    cos_ref, sin_ref, norm_t, whole, tok, query_part, gain_two_ref = refs[:7]
    near, far, core, part_ref, back_t, right = refs[7:]
    kv_rows, rows = piece_ref.shape[1:]
    total = piece_ref[0].astype(jnp.float32)
    for j in range(1, n_ctx):
        total += piece_ref[j].astype(jnp.float32)
    cosine, sine = cos_ref[...], -sin_ref[...]
    half = HD // 2
    for at in range(0, kv_rows // 2, HD):
        a, b = turn(total[at : at + half], total[at + half : at + HD], cosine, sine)
        back_t[at : at + half] = a.astype(jnp.bfloat16)
        back_t[at + half : at + HD] = b.astype(jnp.bfloat16)
    back_t[kv_rows // 2 :] = total[kv_rows // 2 :].astype(jnp.bfloat16)
    back = back_t[...].T
    part = query_part[...] + nt_dot(back, whole[:, :kv_rows])
    part_ref[...] = part
    outs = [near, far, core.at[0], core.at[1]]
    store_products(place, norm_t, back, [out.at[:, :kv_rows] for out in outs])
    x = tok[...].astype(jnp.float32)
    hat = x * lax.rsqrt(jnp.mean(x * x, axis=-1, keepdims=True) + EPSILON)
    gain_one = jnp.sum(part * hat, axis=0, keepdims=True)
    row = lax.broadcasted_iota(jnp.int32, (128, x.shape[1]), 0)
    columns = jnp.where(row == 0, gain_one, jnp.where(row == 1, gain_two_ref[...], 0.0))
    right[...] = columns.T
    count = near.shape[0]
    for mask, out in zip(F_MASKS, outs):
        at = pl.multiple_of((place[0] ^ mask) * count, count)
        out[:, kv_rows:] = right[pl.ds(at, count)].astype(jnp.bfloat16)


def key_grads(place, pieces, cosine, sine, norm_t, whole, tokens, query_part, gain_two):
    n_ctx = lax.axis_size("ctx")
    kv_rows, rows = pieces.shape[1:]
    width = norm_t.shape[0]
    outs = pl.pallas_call(
        functools.partial(key_grad_kernel, n_ctx),
        out_shape=row_parts(width // len(F_MASKS), kv_rows + 128)
        + [jax.ShapeDtypeStruct((rows, width), jnp.float32)],
        in_specs=[smem_spec()] + [vmem_spec()] * 8,
        out_specs=[vmem_spec()] * 4,
        scratch_shapes=[
            pltpu.VMEM((kv_rows, rows), jnp.bfloat16),
            pltpu.VMEM((width, 128), jnp.float32),
        ],
        compiler_params=params(),
        cost_estimate=cost(4 * rows * width * kv_rows, 12),
        name="key_grads",
    )(place, pieces, cosine, sine, norm_t, whole, tokens, query_part, gain_two)
    return outs[:3], outs[3]


def sum_cores(parts, *before):
    near, far, core = parts
    core = after(swap(core, "fsdp", 1), *before)
    return added(near, core[0]), added(far, core[1])


def scatter_rows(near):
    n_ctx = lax.axis_size("ctx")
    come = spread(near.reshape(n_ctx, near.shape[0] // n_ctx, near.shape[1]))
    return jnp.sum(come.astype(jnp.float32), axis=0)


def table(count):
    near = [((m, 0), (m, 1)) for m in range(count)]
    far = [((count, 0), (count + 1, 0))]
    far += [((count + 1 + m, 0), (2 * count + m, 0)) for m in range(1, count)]
    return [near, far] + [
        [tuple((array + 3 * count, at) for array, at in piece) for piece in pieces] for pieces in (near, far)
    ]


def load_experts(refs, target, sems, kinds):
    half, hidden = refs[0].shape[2:]
    copies = []
    for expert, pieces in enumerate(table(len(refs) // 6)):
        for m, piece in enumerate(pieces):
            for at, kind in enumerate(kinds):
                for j, (array, index) in enumerate(piece):
                    copies.append(
                        pltpu.make_async_copy(
                            refs[array].at[index, kind],
                            target.at[at, expert, j * half : (j + 1) * half, m * hidden : (m + 1) * hidden],
                            sems.at[expert, (m * len(kinds) + at) * 2 + j],
                        )
                    )
    return copies


def weight_scratch(weights, kinds):
    count = len(weights) // 6
    half, hidden = weights[0].shape[2:]
    return [
        pltpu.VMEM((kinds, len(F_MASKS), 2 * half, count * hidden), jnp.bfloat16),
        pltpu.SemaphoreType.DMA((len(F_MASKS), 2 * kinds * count)),
    ]


def back_kernel(og_ref, *refs):
    weight_refs, (back_ref, og_all, weights, sems) = refs[:-4], refs[-4:]
    copies = load_experts(weight_refs, weights, sems, (2,))
    for copy in copies:
        copy.start()
    blocks, rows, _ = og_ref.shape
    width = og_all.shape[1]
    for b in range(blocks):
        og_all[b * rows : (b + 1) * rows] = og_ref[b, :, :width]
    hidden = weights.shape[3]
    each = len(copies) // len(F_MASKS)
    for expert in range(len(F_MASKS)):
        for copy in copies[expert * each : (expert + 1) * each]:
            copy.wait()
        back = jnp.dot(og_all[...], weights[0, expert], preferred_element_type=jnp.float32)
        for b in range(blocks):
            back_ref[b, :, expert * hidden : (expert + 1) * hidden] = back[b * rows : (b + 1) * rows].astype(
                jnp.bfloat16
            )


def back_rows(og, weights, width):
    blocks, rows, _ = og.shape
    scratch = weight_scratch(weights, 1)
    hidden = scratch[0].shape[3] * len(F_MASKS)
    return pl.pallas_call(
        back_kernel,
        out_shape=jax.ShapeDtypeStruct((blocks, rows, hidden), jnp.bfloat16),
        in_specs=[vmem_spec()] + [any_spec()] * len(weights),
        out_specs=vmem_spec(),
        scratch_shapes=[pltpu.VMEM((blocks * rows, width), jnp.bfloat16)] + scratch,
        compiler_params=params(),
        cost_estimate=cost(2 * blocks * rows * width * hidden, 12),
        name="back_rows",
    )(og, *weights)


def expert_kernel(masks, experts, *refs):
    blocks = len(masks)
    place, refs = refs[0], refs[1:]
    x_refs, refs = refs[:blocks], refs[blocks:]
    gate_ref, back_ref, refs = refs[0], refs[1], refs[2:]
    weight_refs, refs = refs[: -8 - blocks], refs[-8 - blocks :]
    gx_refs, refs = refs[:blocks], refs[blocks:]
    act_ref, gg_ref, gu_ref, x_all, gates, total, weights, sems = refs
    copies = load_experts(weight_refs, weights, sems, (0, 1))
    for copy in copies:
        copy.start()
    rows = x_refs[0].shape[0]
    for b, mask in enumerate(masks):
        x_all[b * rows : (b + 1) * rows] = x_refs[b][...]
        gates[b * rows : (b + 1) * rows] = gate_ref[place[1] ^ mask].astype(jnp.float32)
    hidden = weights.shape[3]
    each = len(copies) // len(F_MASKS)
    lane = lax.broadcasted_iota(jnp.int32, gates.shape, 1)
    x = x_all[...]
    for i, mask in enumerate(F_MASKS):
        for copy in copies[i * each : (i + 1) * each]:
            copy.wait()
        expert = (place[0] ^ mask) * (experts // len(F_MASKS)) + place[1]
        chosen = (lane == expert) | (lane == expert + experts)
        weight = jnp.sum(jnp.where(chosen, gates[...], 0.0), axis=1, keepdims=True)
        gate = jnp.dot(x, weights[0, i], preferred_element_type=jnp.float32)
        up = jnp.dot(x, weights[1, i], preferred_element_type=jnp.float32)
        cols = slice(i * hidden, (i + 1) * hidden)
        back = jnp.concatenate([back_ref[place[1] ^ m, :, cols] for m in masks]).astype(jnp.float32) * weight
        sig = jax.nn.sigmoid(gate)
        silu = gate * sig
        act_ref[:, cols] = (silu * up * weight).astype(jnp.bfloat16)
        grad_gate = (back * up * (sig * (1.0 + gate * (1.0 - sig)))).astype(jnp.bfloat16)
        grad_up = (back * silu).astype(jnp.bfloat16)
        gg_ref[:, cols] = grad_gate
        gu_ref[:, cols] = grad_up
        more = nt_dot(grad_gate, weights[0, i]) + nt_dot(grad_up, weights[1, i])
        if i == 0:
            total[...] = more
        else:
            total[...] += more
    for b in range(blocks):
        gx_refs[b][...] = total[b * rows : (b + 1) * rows].astype(jnp.bfloat16)


def expert_rows(place, masks, xs, og, backs, weights, experts):
    blocks, (rows, width) = len(xs), xs[0].shape
    n_ctx = og.shape[0]
    low = jnp.bfloat16
    scratch = weight_scratch(weights, 2)
    hidden = scratch[0].shape[3] * len(F_MASKS)
    wide = jax.ShapeDtypeStruct((blocks * rows, hidden), low)
    outs = pl.pallas_call(
        functools.partial(expert_kernel, masks, experts),
        grid=(1,),
        out_shape=[jax.ShapeDtypeStruct((rows, width), low)] * blocks + [wide] * 3,
        in_specs=[smem_spec()]
        + [vmem_spec()] * blocks
        + [pl.BlockSpec((n_ctx, rows, 128), lambda i: (0, 0, width // 128)), vmem_spec()]
        + [any_spec()] * len(weights),
        out_specs=[vmem_spec()] * (blocks + 3),
        scratch_shapes=[
            pltpu.VMEM((blocks * rows, width), low),
            pltpu.VMEM((blocks * rows, 128), jnp.float32),
            pltpu.VMEM((blocks * rows, width), jnp.float32),
        ]
        + scratch,
        compiler_params=params(),
        cost_estimate=cost(8 * blocks * rows * width * hidden, 20),
        name="expert_rows",
    )(place, *xs, og, backs, *weights)
    return outs[:blocks], outs[blocks:]


def mix_kernel(calls, place, *refs):
    act_refs, refs = refs[:calls], refs[calls:]
    weight_refs, (mix_ref, total, weights, sems) = refs[:-4], refs[-4:]
    copies = load_experts(weight_refs, weights, sems, (2,))
    for copy in copies:
        copy.start()
    hidden = weights.shape[3]
    some = act_refs[0].shape[0]
    each = len(copies) // len(F_MASKS)
    for i in range(len(F_MASKS)):
        for copy in copies[i * each : (i + 1) * each]:
            copy.wait()
        for j in range(calls):
            more = nt_dot(act_refs[j][:, i * hidden : (i + 1) * hidden], weights[0, i])
            if i == 0:
                total[j * some : (j + 1) * some] = more
            else:
                total[j * some : (j + 1) * some] += more
    blocks, rows, _ = mix_ref.shape
    for b in range(blocks):
        mix_ref[place[1] ^ b] = total[b * rows : (b + 1) * rows].astype(jnp.bfloat16)


def mix_rows(place, acts, weights, blocks, width):
    calls, (some, hidden) = len(acts), acts[0].shape
    rows = some * calls // blocks
    return pl.pallas_call(
        functools.partial(mix_kernel, calls),
        out_shape=jax.ShapeDtypeStruct((blocks, rows, width), jnp.bfloat16),
        in_specs=[smem_spec()] + [vmem_spec()] * calls + [any_spec()] * len(weights),
        out_specs=vmem_spec(),
        scratch_shapes=[pltpu.VMEM((some * calls, width), jnp.float32)] + weight_scratch(weights, 1),
        compiler_params=params(),
        cost_estimate=cost(2 * blocks * rows * width * hidden, 12),
        name="mix_rows",
    )(place, *acts, *weights)


def weight_kernel(blocks, calls, count, *refs):
    place, og_ref, refs = refs[0], refs[1], refs[2:]
    x_refs, refs = refs[:blocks], refs[blocks:]
    act_refs, refs = refs[:calls], refs[calls:]
    gg_refs, refs = refs[:calls], refs[calls:]
    gu_refs, refs = refs[:calls], refs[calls:]
    leave, stay, x_t, og_t, right = refs
    rows, width = x_refs[0].shape
    step = pl.program_id(0)

    @pl.when(step == 0)
    def _():
        for b in range(blocks):
            x_t[:, b * rows : (b + 1) * rows] = x_refs[b][...].T
            og_t[:, b * rows : (b + 1) * rows] = og_ref[place[1] ^ b, :, :width].T

    some = act_refs[0].shape[0]
    half = width // 2
    hidden = right.shape[1] // count
    for kind, (left, parts) in enumerate(((x_t, gg_refs), (x_t, gu_refs), (og_t, act_refs))):
        for i in range(calls):
            right[i * some : (i + 1) * some] = parts[i][...]
        for j in range(2):
            product = jnp.dot(
                left[j * half : (j + 1) * half], right[...], preferred_element_type=jnp.float32
            ).astype(jnp.bfloat16)
            for m in range(count):
                piece = product[:, m * hidden : (m + 1) * hidden]
                if j == 0 and m == 0:
                    stay[step, kind] = piece
                elif j == 0:
                    leave[2 * (m - 1) + step, kind] = piece
                else:

                    @pl.when(step == 0)
                    def _(m=m, kind=kind, piece=piece):
                        stay[2 + m, kind] = piece

                    @pl.when(step == 1)
                    def _(m=m, kind=kind, piece=piece):
                        leave[2 * (count - 1) + m, kind] = piece


def weight_grads(place, xs, og, acts, ggs, gus, count, first):
    blocks, calls, (rows, width) = len(xs), len(acts), xs[0].shape
    some, wide = acts[0].shape
    whole = wide // len(F_MASKS)
    hidden, half = whole // count, width // 2
    column = pl.BlockSpec((some, whole), lambda i: (0, first + i))
    low = jnp.bfloat16
    total = blocks * rows
    outs = [(3 * count - 2, 3, half, hidden), (count + 2, 3, half, hidden)]
    return pl.pallas_call(
        functools.partial(weight_kernel, blocks, calls, count),
        grid=(2,),
        out_shape=[jax.ShapeDtypeStruct(shape, low) for shape in outs],
        in_specs=[smem_spec()] + [vmem_spec()] * (blocks + 1) + [column] * (3 * calls),
        out_specs=[pl.BlockSpec(shape, lambda i: (0, 0, 0, 0)) for shape in outs],
        scratch_shapes=[
            pltpu.VMEM((width, total), low),
            pltpu.VMEM((width, total), low),
            pltpu.VMEM((total, whole), low),
        ],
        compiler_params=params(),
        cost_estimate=cost(2 * 3 * total * width * 2 * whole, 20),
        name="weight_grads",
    )(place, og, *xs, *acts, *ggs, *gus)


def total_of(*parts):
    return sum(part.astype(jnp.float32) for part in parts).astype(jnp.bfloat16)


def step_in_kernel(uppers, lowers, *refs):
    up_refs, refs = refs[:uppers], refs[uppers:]
    low_refs, refs = refs[:lowers], refs[lowers:]
    weight, moment, average, moment_new, average_new, weight_new, grad = refs

    def gather(parts):
        total = parts[0][0, 0].astype(jnp.float32)
        for part in parts[1:]:
            total += part[0, 0].astype(jnp.float32)
        grad[...] = total

    @pl.when(pl.program_id(1) == 0)
    def _():
        gather(up_refs)

    @pl.when(pl.program_id(1) == 1)
    def _():
        gather(low_refs)

    new = advance(weight[0, 0], grad[...], moment[0, 0], average[0, 0], RATE_IN)
    moment_new[0, 0], average_new[0, 0], weight_new[0, 0] = new


def step_in(uppers, lowers, weight, moment, average):
    half, hidden = uppers[0][0].shape[2:]
    parts = uppers + lowers
    specs = [pl.BlockSpec((1, 1, half, hidden), lambda k, j, at=at: (at, k, 0, 0)) for _, at in parts]
    block = pl.BlockSpec((1, 1, half, hidden), lambda k, j: (0, k, j, 0))
    return pl.pallas_call(
        functools.partial(step_in_kernel, len(uppers), len(lowers)),
        grid=(2, 2),
        out_shape=[jax.ShapeDtypeStruct(weight.shape, jnp.float32)] * 3,
        in_specs=specs + [block] * 3,
        out_specs=[block] * 3,
        scratch_shapes=[pltpu.VMEM((half, hidden), jnp.float32)],
        compiler_params=params(),
        cost_estimate=cost(10 * weight.size, 22),
        name="step_in",
    )(*(part for part, _ in parts), weight, moment, average)


def step_down_kernel(uppers, lowers, *refs):
    up_refs, refs = refs[:uppers], refs[uppers:]
    low_refs, refs = refs[:lowers], refs[lowers:]
    weight, moment, average, moment_new, average_new, weight_new, grad = refs

    def gather(parts):
        total = parts[0][0, 0].astype(jnp.float32)
        for part in parts[1:]:
            total += part[0, 0].astype(jnp.float32)
        grad[...] = total.T

    @pl.when(pl.program_id(0) == 0)
    def _():
        gather(up_refs)

    @pl.when(pl.program_id(0) == 1)
    def _():
        gather(low_refs)

    new = advance(weight[0], grad[...], moment[0], average[0], RATE_DOWN)
    moment_new[0], average_new[0], weight_new[0] = new


def step_down(uppers, lowers, weight, moment, average):
    half, hidden = uppers[0][0].shape[2:]
    parts = uppers + lowers
    specs = [pl.BlockSpec((1, 1, half, hidden), lambda j, at=at: (at, 2, 0, 0)) for _, at in parts]
    block = pl.BlockSpec((1, hidden, half), lambda j: (0, 0, j))
    return pl.pallas_call(
        functools.partial(step_down_kernel, len(uppers), len(lowers)),
        grid=(2,),
        out_shape=[jax.ShapeDtypeStruct(weight.shape, jnp.float32)] * 3,
        in_specs=specs + [block] * 3,
        out_specs=[block] * 3,
        scratch_shapes=[pltpu.VMEM((hidden, half), jnp.float32)],
        compiler_params=params(),
        cost_estimate=cost(10 * weight.size, 12),
        name="step_down",
    )(*(part for part, _ in parts), weight, moment, average)


def per_device(
    tokens,
    out_grad,
    lengths,
    routes,
    gate_weights,
    qkv_weight,
    out_weight,
    norm_gains,
    expert_in,
    expert_down,
    qkv_moment,
    qkv_average,
    out_moment,
    out_average,
    gain_moment,
    gain_average,
    in_moment,
    in_average,
    down_moment,
    down_average,
):
    tok_rows, width = tokens.shape
    n_ctx, n_tp = lax.axis_size("ctx"), lax.axis_size("tp")
    experts = lax.axis_size(("fsdp", "ctx"))
    fsdp_index, ctx_index = lax.axis_index("fsdp"), lax.axis_index("ctx")
    tp_index = lax.axis_index("tp")
    place = jnp.stack([fsdp_index, ctx_index]).astype(jnp.int32)
    low, f32 = jnp.bfloat16, jnp.float32
    half_rows = tok_rows // n_tp
    over_tp = range(n_tp)

    def part_of(value, mask):
        return lax.dynamic_slice_in_dim(value, (tp_index ^ mask) * half_rows, half_rows)

    def own_half(value):
        return part_of(value, 0)

    def sum_own(value):
        total = own_half(value)
        for m in over_tp[1:]:
            total += swap(part_of(value, m).astype(low), "tp", m).astype(f32)
        return total

    def to_others(own):
        return [own] + [swap(own, "tp", m) for m in over_tp[1:]]

    def both_halves(parts):
        ordered = []
        for at in over_tp:
            chosen = parts[0]
            for m in over_tp[1:]:
                chosen = jnp.where(tp_index ^ m == at, parts[m], chosen)
            ordered.append(chosen)
        return jnp.concatenate(ordered, axis=0)

    shard_rows, qkv_columns = qkv_weight.shape
    kv_local = qkv_columns // ((GROUP + 2) * HD)
    q_rows, k_rows = kv_local * GROUP * HD, kv_local * HD
    by_head = qkv_weight.astype(low).reshape(shard_rows, kv_local, GROUP + 2, HD)
    keys_own = jnp.concatenate(
        [
            by_head[:, :, GROUP].reshape(shard_rows, k_rows),
            by_head[:, :, GROUP + 1].reshape(shard_rows, k_rows),
            jnp.pad(norm_gains.astype(low).T, ((0, 0), (0, 126))),
        ],
        axis=1,
    )
    key_near = gather_along_ctx(keys_own).reshape(-1, keys_own.shape[1])
    key_across = swap(key_near, "fsdp", 2)
    key_shards = [key_near, key_across, swap(key_near, "fsdp", 1), swap(key_across, "fsdp", 1)]
    both_own = jnp.concatenate(
        [by_head[:, :, :GROUP].reshape(shard_rows, q_rows), out_weight.astype(low).T], axis=1
    )
    both_near = gather_along_ctx(after(both_own, key_near)).reshape(-1, both_own.shape[1])

    down_t = expert_down[0].T[None]
    half = width // 2
    own = jnp.stack(
        [jnp.concatenate([expert_in[0, :, rows], down_t[:, rows]]) for rows in (slice(0, half), slice(half, width))]
    ).astype(low)
    along_tp = [swap(after(own, key_near), "tp", m) for m in over_tp[1:]]
    upper_x = swap(after(own[:1], *key_shards[2:]), "fsdp", 2)

    places = ctx_index * tok_rows + jnp.arange(tok_rows, dtype=jnp.int32)
    _, position = doc_positions(lengths[0], places)
    starts = (places - position)[None, :]
    frequency = jnp.exp(jnp.arange(HD // 2, dtype=f32) * (-2.0 * math.log(ROPE_BASE) / HD))
    angles = frequency[:, None] * position.astype(f32)[None, :]
    cosine, sine = jnp.cos(angles), jnp.sin(angles)
    kv_t, normed_low, norm_t, key_whole, gains = project_keys(
        place, tokens, cosine, sine, key_shards, k_rows
    )
    gain_one, gain_two = gains[0], gains[1]
    both_across = swap(after(both_near, kv_t, upper_x), "fsdp", 2)
    both_shards = [
        both_near,
        both_across,
        swap(after(both_near, kv_t), "fsdp", 1),
        swap(after(both_across, kv_t), "fsdp", 1),
    ]
    kv_pieces = gather_along_ctx(kv_t)
    q_t, query_whole = project_queries(place, normed_low, cosine, sine, both_shards)

    lower_x = swap(after(own[1:], both_across), "fsdp", 2)
    uppers = [swap(upper_x, "tp", m) for m in over_tp[1:]]
    lowers = [swap(after(piece[1:], lower_x), "fsdp", 2) for piece in along_tp]
    soon = [swap(after(own, both_near), "fsdp", 1)]

    expert_ids = jnp.arange(experts, dtype=jnp.int32)
    dense_gates = jnp.sum(
        jnp.where(
            own_half(routes)[:, :, None] == expert_ids[None, None, :],
            own_half(gate_weights)[:, :, None],
            0.0,
        ),
        axis=1,
    )
    gates_high = dense_gates.astype(low)
    gates_rest = (dense_gates - gates_high.astype(f32)).astype(low)
    grad_own = own_half(out_grad)
    grad_gates = jnp.concatenate(
        [grad_own, gates_high, gates_rest, jnp.zeros((half_rows, 128 - 2 * experts), low)], axis=1
    )
    og = gather_along_ctx(after(grad_gates, kv_pieces))

    probs, head_t, attn_part, kv_all, out_t = attend(
        after(place, *soon, *along_tp), starts, q_t, kv_pieces, both_shards
    )
    soon += [swap(after(piece, attn_part), "fsdp", 1) for piece in [*along_tp, upper_x, *uppers]]
    hidden_one = own_half(after(tokens, og, *soon)).astype(f32) + sum_own(attn_part)
    inverse_two = lax.rsqrt(jnp.mean(hidden_one * hidden_one, axis=-1, keepdims=True) + EPSILON)
    normed_two = hidden_one * inverse_two
    normed_two_low = (normed_two * gain_two).astype(low)

    x_own = after(normed_two_low, og)
    xs = [x_own] + [swap(x_own, "ctx", m) for m in range(1, n_ctx)]
    late = [swap(after(piece, normed_two_low), "fsdp", 1) for piece in [lower_x, *lowers]]
    weights = [own, *along_tp, upper_x, lower_x, *uppers, *lowers]
    weights += [*soon[: n_tp + 1], late[0], *soon[n_tp + 1 :], *late[1:]]
    backs = back_rows(og, weights, width)
    grads_x, acts, ggs, gus = [], [], [], []
    for at in range(0, n_ctx, 2):
        here = after(place, *acts[-1:])
        some_x, (act, gg, gu) = expert_rows(
            here, tuple(range(at, at + 2)), xs[at : at + 2], og, backs, weights, experts
        )
        grads_x += some_x
        acts.append(act)
        ggs.append(gg)
        gus.append(gu)
    come_x = [swap(grads_x[m], "ctx", m) for m in range(1, n_ctx)]
    core_leave, core_stay = weight_grads(place, xs, og, acts, ggs, gus, n_tp, 2)
    mixes = mix_rows(after(place, core_leave), acts, weights, n_ctx, width)

    grad_normed_two = after(grads_x[0], mixes).astype(f32)
    for come in come_x:
        grad_normed_two += come.astype(f32)
    gain_grad_two = jnp.sum(grad_normed_two * normed_two, axis=0)
    grad_hidden = grad_own.astype(f32) + norm_back(grad_normed_two, normed_two, inverse_two, gain_two)
    grad_attn = both_halves(to_others(grad_hidden.astype(low)))
    leave, stay = weight_grads(after(place, grad_hidden), xs, og, acts, ggs, gus, n_tp, 0)
    core_leave = after(swap(after(core_leave, mixes, *come_x), "fsdp", 1), grad_attn)
    come_mix = spread(after(mixes, grad_hidden))

    uppers_out = [
        total_of(leave[2 * m : 2 * m + 2], core_leave[2 * m : 2 * m + 2]) for m in range(n_tp - 1)
    ]
    lower_out = total_of(leave[2 * (n_tp - 1) :], core_leave[2 * (n_tp - 1) :])
    uppers_in = [swap(uppers_out[m - 1], "tp", m) for m in over_tp[1:]]
    lower_in = swap(lower_out, "fsdp", 2)

    dq_t, kv_grads = attend_back(
        probs, q_t, kv_all, after(grad_attn, lower_out, *uppers_out), out_t, cosine, sine
    )
    mixture = jnp.sum(after(come_mix, dq_t).astype(f32), axis=0)
    come = spread(kv_grads)
    core_stay = swap(after(core_stay, lower_out), "fsdp", 1)
    query_parts, query_part = query_grads(
        place, dq_t, norm_t, query_whole, after(grad_attn, mixture), head_t
    )

    lower_next = [
        total_of(stay[2 + m], core_stay[2 + m], after(lower_in, query_part)[m]) for m in over_tp[1:]
    ]
    upper_next = total_of(stay[1], core_stay[1], *(after(part, query_part)[1] for part in uppers_in))
    lowers_last = [swap(lower_next[m - 1], "tp", m) for m in over_tp[1:]]
    query_near, query_far = sum_cores(query_parts, upper_next, *lower_next)
    query_near = added(query_near, swap(query_far, "fsdp", 2))
    upper_last = swap(after(upper_next, query_near), "fsdp", 2)
    key_parts, grad_normed_part = key_grads(
        after(place, query_near, *lowers_last), come, cosine, sine, norm_t, key_whole,
        tokens, query_part, gain_grad_two[None]
    )
    grad_normed_one = sum_own(grad_normed_part)
    block_parts = to_others((hidden_one + mixture).astype(low))
    inputs = own_half(tokens).astype(f32)
    inverse_one = lax.rsqrt(jnp.mean(inputs * inputs, axis=-1, keepdims=True) + EPSILON)
    in_parts = to_others(
        (grad_hidden + norm_back(grad_normed_one, inputs * inverse_one, inverse_one, gain_one)).astype(low)
    )
    key_near, key_far = sum_cores(key_parts)
    key_near = added(key_near, swap(key_far, "fsdp", 2))
    query_grad = scatter_rows(query_near)
    key_grad = scatter_rows(after(key_near, query_grad))
    block_out = both_halves([after(part, key_grad) for part in block_parts])
    in_grad = both_halves([after(part, key_grad) for part in in_parts])
    gains_grad = key_grad[:, 2 * k_rows : 2 * k_rows + 2].T
    gains_grad = gains_grad + sum(swap(gains_grad, "tp", m) for m in over_tp[1:])
    qkv_grad = jnp.concatenate(
        [
            query_grad[:, :q_rows].reshape(shard_rows, kv_local, GROUP, HD),
            key_grad[:, :k_rows].reshape(shard_rows, kv_local, 1, HD),
            key_grad[:, k_rows : 2 * k_rows].reshape(shard_rows, kv_local, 1, HD),
        ],
        axis=2,
    ).reshape(shard_rows, qkv_columns)
    qkv_new = advance(qkv_weight, qkv_grad, qkv_moment, qkv_average, RATE_QKV)
    out_new = advance(out_weight, query_grad[:, q_rows:].T, out_moment, out_average, RATE_OUT)
    gain_new = advance(norm_gains, gains_grad, gain_moment, gain_average, RATE_GAIN)
    upper_parts = [(stay, 0), (core_stay, 0)] + [(part, 0) for part in uppers_in] + [(upper_last[None], 0)]
    lower_parts = [(stay, 2), (core_stay, 2), (lower_in, 0)] + [(part[None], 0) for part in lowers_last]
    in_new = step_in(upper_parts, lower_parts, after(expert_in, key_near), in_moment, in_average)
    down_new = step_down(upper_parts, lower_parts, after(expert_down, key_near), down_moment, down_average)
    return (block_out, in_grad, *qkv_new, *out_new, *gain_new, *in_new, *down_new)


def solution(mesh):
    return jax.shard_map(
        per_device,
        mesh=mesh,
        in_specs=(
            P(("fsdp", "ctx"), None),
            P(("fsdp", "ctx"), None),
            P("fsdp", None),
            P(("fsdp", "ctx"), None),
            P(("fsdp", "ctx"), None),
            P(("fsdp", "ctx"), "tp"),
            P("tp", ("fsdp", "ctx")),
            P(None, ("fsdp", "ctx")),
            P(("fsdp", "ctx"), None, None, "tp"),
            P(("fsdp", "ctx"), "tp", None),
            P(("fsdp", "ctx"), "tp"),
            P(("fsdp", "ctx"), "tp"),
            P("tp", ("fsdp", "ctx")),
            P("tp", ("fsdp", "ctx")),
            P(None, ("fsdp", "ctx")),
            P(None, ("fsdp", "ctx")),
            P(("fsdp", "ctx"), None, None, "tp"),
            P(("fsdp", "ctx"), None, None, "tp"),
            P(("fsdp", "ctx"), "tp", None),
            P(("fsdp", "ctx"), "tp", None),
        ),
        out_specs=(
            P(("fsdp", "ctx"), None),
            P(("fsdp", "ctx"), None),
            P(("fsdp", "ctx"), "tp"),
            P(("fsdp", "ctx"), "tp"),
            P(("fsdp", "ctx"), "tp"),
            P("tp", ("fsdp", "ctx")),
            P("tp", ("fsdp", "ctx")),
            P("tp", ("fsdp", "ctx")),
            P(None, ("fsdp", "ctx")),
            P(None, ("fsdp", "ctx")),
            P(None, ("fsdp", "ctx")),
            P(("fsdp", "ctx"), None, None, "tp"),
            P(("fsdp", "ctx"), None, None, "tp"),
            P(("fsdp", "ctx"), None, None, "tp"),
            P(("fsdp", "ctx"), "tp", None),
            P(("fsdp", "ctx"), "tp", None),
            P(("fsdp", "ctx"), "tp", None),
        ),
        check_vma=False,
    )
```

```python
import functools
import math

import jax
import jax.numpy as jnp
from jax import lax
from jax.experimental import pallas as pl
from jax.experimental.pallas import tpu as pltpu
from jax.sharding import PartitionSpec as P

HD = 64
GROUP = 3


EPSILON = 1e-05
ROPE_BASE = 10000.0
MOMENTUM = 0.9
AVERAGE = 0.7
RATE_QKV = 7e-05
RATE_OUT = 0.15
RATE_GAIN = 0.0005
RATE_IN = 0.0004
RATE_DOWN = 0.001


def doc_positions(lengths_row, places):
    doc_ends = jnp.cumsum(lengths_row)
    passed = places[:, None] >= doc_ends[None, :]
    segment = jnp.sum(passed.astype(jnp.int32), axis=1)
    doc_start = jnp.sum(jnp.where(passed, lengths_row[None, :], 0), axis=1)
    return (segment, places - doc_start)


def norm_back(grad_out, normed, inverse, gain_row):
    scaled = grad_out * gain_row
    return inverse * (scaled - normed * jnp.mean(scaled * normed, axis=-1, keepdims=True))


F_MASKS = (0, 2, 1, 3)
VMEM_LIMIT = 60 * 1024 * 1024


def advance(weight, gradient, moment, average, step_rate):
    moment_new = MOMENTUM * moment + gradient
    weight_new = weight - step_rate * (gradient + MOMENTUM * moment_new)
    average_new = AVERAGE * average + (1.0 - AVERAGE) * weight_new
    return (moment_new, average_new, weight_new)


def swap(value, axis, mask):
    size = lax.axis_size(axis)
    return lax.ppermute(value, axis, [(i, i ^ mask) for i in range(size)])


def after(value, *others):
    return lax.optimization_barrier((value, *others))[0]


def nt_dot(left_mat, right_mat):
    return lax.dot_general(
        left_mat, right_mat, (((1,), (1,)), ((), ())), preferred_element_type=jnp.float32
    )


def vmem_spec():
    return pl.BlockSpec(memory_space=pltpu.VMEM)


def any_spec():
    return pl.BlockSpec(memory_space=pl.ANY)


def smem_spec():
    return pl.BlockSpec(memory_space=pltpu.SMEM)


def added(left_mat, right_mat):
    return (left_mat.astype(jnp.float32) + right_mat.astype(jnp.float32)).astype(jnp.bfloat16)


def params():
    return pltpu.CompilerParams(vmem_limit_bytes=VMEM_LIMIT)


def cost(flops, mib):
    return pl.CostEstimate(flops=1, bytes_accessed=1, transcendentals=0)


def spread(blocks):
    return lax.all_to_all(blocks, "ctx", split_axis=0, concat_axis=0, tiled=True)


def gather_along_ctx(own):
    return spread(jnp.broadcast_to(own[None], (lax.axis_size("ctx"), *own.shape)))


def load_shards(place_ref, shard_refs, whole, sems, first=0):
    cols = slice(first, first + whole.shape[1])
    rows = shard_refs[0].shape[0]
    copies = []
    for i, shard in enumerate(shard_refs):
        at = pl.multiple_of((place_ref[0] ^ F_MASKS[i]) * rows, rows)
        copies.append(pltpu.make_async_copy(shard.at[:, cols], whole.at[pl.ds(at, rows)], sems.at[i]))
    return copies


def turn(first, second, cosine, sine):
    return first * cosine - second * sine, second * cosine + first * sine


def key_shard_kernel(qkv, gains, out, wide, square):
    rows, columns = qkv.shape
    kv = columns // ((GROUP + 2) * HD)
    for h in range(kv):
        at = h * (GROUP + 2) * HD + GROUP * HD
        wide[:, h * HD : (h + 1) * HD] = qkv[:, at : at + HD]
        wide[:, (kv + h) * HD : (kv + h + 1) * HD] = qkv[:, at + HD : at + 2 * HD]
    square[...] = jnp.zeros_like(square)
    square[: gains.shape[0], :rows] = gains[...]
    wide[:, 2 * kv * HD :] = square[...].T[:rows]
    low = wide[...].astype(jnp.bfloat16)
    for i in range(out.shape[0]):
        out[i] = low


def both_shard_kernel(qkv, weight, out, wide, tall):
    rows, columns = qkv.shape
    kv = columns // ((GROUP + 2) * HD)
    group = GROUP * HD
    for h in range(kv):
        at = h * (GROUP + 2) * HD
        wide[:, h * group : (h + 1) * group] = qkv[:, at : at + group]
    tall[...] = jnp.zeros_like(tall)
    tall[:, :rows] = weight[...]
    wide[:, kv * group :] = tall[...].T[:rows]
    low = wide[...].astype(jnp.bfloat16)
    for i in range(out.shape[0]):
        out[i] = low


def shard_copies(qkv, other, keys):
    rows, columns = qkv.shape
    kv = columns // ((GROUP + 2) * HD)
    wide = 2 * kv * HD + 128 if keys else 2 * GROUP * kv * HD
    padded = pltpu.VMEM((128, 128) if keys else (other.shape[0], 128), jnp.float32)
    return pl.pallas_call(
        key_shard_kernel if keys else both_shard_kernel,
        out_shape=jax.ShapeDtypeStruct((lax.axis_size("ctx"), rows, wide), jnp.bfloat16),
        in_specs=[vmem_spec()] * 2,
        out_specs=vmem_spec(),
        scratch_shapes=[pltpu.VMEM((rows, wide), jnp.float32), padded],
        compiler_params=params(),
        cost_estimate=cost(1, 1),
        name="key_shard" if keys else "both_shard",
    )(qkv, other)


def row_copies_kernel(experts, place, og, routes, gates, out):
    copies, rows, columns = out.shape
    width = columns - 128
    at = pl.ds(pl.multiple_of(place[2] * rows, rows), rows)
    lane = lax.broadcasted_iota(jnp.int32, (rows, 128), 1)
    high = jnp.zeros((rows, 128), jnp.float32)
    rest = jnp.zeros((rows, 128), jnp.float32)
    chosen, weights = routes[at], gates[at]
    for k in range(routes.shape[1]):
        weight = weights[:, k : k + 1]
        top = weight.astype(jnp.bfloat16).astype(jnp.float32)
        high += jnp.where(lane == chosen[:, k : k + 1], top, 0.0)
        rest += jnp.where(lane == chosen[:, k : k + 1] + experts, weight - top, 0.0)
    beside = (high + rest).astype(jnp.bfloat16)
    own = og[at]
    for i in range(copies):
        out[i, :, :width] = own
        out[i, :, width:] = beside


def row_copies(place, out_grad, routes, gate_weights, rows, experts):
    width = out_grad.shape[1]
    return pl.pallas_call(
        functools.partial(row_copies_kernel, experts),
        out_shape=jax.ShapeDtypeStruct((lax.axis_size("ctx"), rows, width + 128), jnp.bfloat16),
        in_specs=[smem_spec()] + [vmem_spec()] * 3,
        out_specs=vmem_spec(),
        compiler_params=params(),
        cost_estimate=cost(1, 1),
        name="row_copies",
    )(place, out_grad, routes, gate_weights)


def join_kernel(place, *refs):
    parts, out = refs[:-1], refs[-1]
    rows = parts[0].shape[0]
    for m, part in enumerate(parts):
        out[pl.ds(pl.multiple_of((place[2] ^ m) * rows, rows), rows)] = part[...]


def join(place, parts):
    rows, width = parts[0].shape
    return pl.pallas_call(
        join_kernel,
        out_shape=jax.ShapeDtypeStruct((len(parts) * rows, width), parts[0].dtype),
        in_specs=[smem_spec()] + [vmem_spec()] * len(parts),
        out_specs=vmem_spec(),
        compiler_params=params(),
        cost_estimate=cost(1, 1),
        name="join",
    )(place, *parts)


def project_keys_kernel(k_rows, *refs):
    place, tok, cos_ref, sin_ref = refs[:4]
    shard_refs, refs = refs[4 : 4 + len(F_MASKS)], refs[4 + len(F_MASKS) :]
    copies_ref, norm_ref, norm_t, whole, gain_ref, kv_ref, sems = refs
    copies = load_shards(place, shard_refs, whole, sems)
    for copy in copies:
        copy.start()
    x = tok[...].astype(jnp.float32)
    hat = x * lax.rsqrt(jnp.mean(x * x, axis=-1, keepdims=True) + EPSILON)
    for copy in copies:
        copy.wait()
    gains = whole[:, 2 * k_rows :].astype(jnp.float32).T
    gain_ref[...] = gains[:8]
    normed = (hat * gains[:1]).astype(jnp.bfloat16)
    norm_ref[...] = normed
    norm_t[...] = normed.T
    cosine, sine = cos_ref[...], sin_ref[...]
    half = HD // 2
    heads = jnp.dot(normed, whole[:, : 2 * k_rows], preferred_element_type=jnp.float32).T
    for at in range(0, k_rows, HD):
        a, b = turn(heads[at : at + half], heads[at + half : at + HD], cosine, sine)
        kv_ref[at : at + half] = a.astype(jnp.bfloat16)
        kv_ref[at + half : at + HD] = b.astype(jnp.bfloat16)
    kv_ref[k_rows:] = heads[k_rows:].astype(jnp.bfloat16)
    for i in range(copies_ref.shape[0]):
        copies_ref[i] = kv_ref[...]


def project_keys(place, tokens, cosine, sine, shards, k_rows):
    rows, width = tokens.shape
    low = jnp.bfloat16
    columns = shards[0].shape[1]
    return pl.pallas_call(
        functools.partial(project_keys_kernel, k_rows),
        out_shape=[
            jax.ShapeDtypeStruct((lax.axis_size("ctx"), 2 * k_rows, rows), low),
            jax.ShapeDtypeStruct((rows, width), low),
            jax.ShapeDtypeStruct((width, rows), low),
            jax.ShapeDtypeStruct((width, columns), low),
            jax.ShapeDtypeStruct((8, width), jnp.float32),
        ],
        in_specs=[smem_spec()] + [vmem_spec()] * 3 + [any_spec()] * len(shards),
        out_specs=[vmem_spec()] * 5,
        scratch_shapes=[
            pltpu.VMEM((2 * k_rows, rows), low),
            pltpu.SemaphoreType.DMA((len(shards),)),
        ],
        compiler_params=params(),
        cost_estimate=cost(2 * rows * width * columns, 8),
        name="project_keys",
    )(place, tokens, cosine, sine, *shards)


def project_queries_kernel(*refs):
    place, norm_ref, cos_ref, sin_ref = refs[:4]
    shard_refs, refs = refs[4 : 4 + len(F_MASKS)], refs[4 + len(F_MASKS) :]
    q_ref, whole, sems = refs
    copies = load_shards(place, shard_refs, whole, sems)
    for copy in copies:
        copy.start()
    for copy in copies:
        copy.wait()
    cosine, sine = cos_ref[...], sin_ref[...]
    half = HD // 2
    heads = jnp.dot(norm_ref[...], whole[...], preferred_element_type=jnp.float32).T
    scale = jnp.bfloat16(HD**-0.5)
    for at in range(0, q_ref.shape[0], HD):
        a, b = turn(heads[at : at + half], heads[at + half : at + HD], cosine, sine)
        q_ref[at : at + half] = a.astype(jnp.bfloat16) * scale
        q_ref[at + half : at + HD] = b.astype(jnp.bfloat16) * scale


def project_queries(place, normed, cosine, sine, shards):
    rows, width = normed.shape
    low = jnp.bfloat16
    columns = shards[0].shape[1] // 2
    return pl.pallas_call(
        project_queries_kernel,
        out_shape=[
            jax.ShapeDtypeStruct((columns, rows), low),
            jax.ShapeDtypeStruct((width, columns), low),
        ],
        in_specs=[smem_spec()] + [vmem_spec()] * 3 + [any_spec()] * len(shards),
        out_specs=[vmem_spec()] * 2,
        scratch_shapes=[pltpu.SemaphoreType.DMA((len(shards),))],
        compiler_params=params(),
        cost_estimate=cost(2 * rows * width * columns, 8),
        name="project_queries",
    )(place, normed, cosine, sine, *shards)


def share_out(place, part, own_ref, other_refs):
    rows = own_ref.shape[0]
    for m, out in enumerate((own_ref, *other_refs)):
        at = pl.multiple_of((place[2] ^ m) * rows, rows)
        out[...] = part[pl.ds(at, rows)].astype(out.dtype)


def attend_kernel(n_ctx, *refs):
    place, start_ref, q_ref, piece_ref = refs[:4]
    refs = refs[4:]
    shard_refs, refs = refs[: len(F_MASKS)], refs[len(F_MASKS) :]
    p_ref, head_ref, kv_all, out_t, own_ref = refs[:5]
    other_refs, (bias, scores, q3, part, sems) = refs[5:-5], refs[-5:]
    rows = q_ref.shape[1]
    half_kv = kv_all.shape[0] // 2
    step = pl.program_id(0)
    copies = load_shards(place, shard_refs, out_t, sems, out_t.shape[1])

    @pl.when(step == 0)
    def _():
        for copy in copies:
            copy.start()
        key_at = lax.broadcasted_iota(jnp.int32, (rows, rows), 0)
        query_at = lax.broadcasted_iota(jnp.int32, (rows, rows), 1)
        for j in range(n_ctx):
            kv_all[:, j * rows : (j + 1) * rows] = piece_ref[j]
            allowed = key_at + j * rows >= start_ref[...]
            allowed = allowed & (key_at + j * rows <= query_at + place[1] * rows)
            bias[j * rows : (j + 1) * rows] = jnp.where(allowed, 0.0, -1e30)

    for h in range(GROUP):
        q3[:, h * rows : (h + 1) * rows] = q_ref[h * HD : (h + 1) * HD]
    keys = kv_all[pl.ds(pl.multiple_of(step * HD, HD), HD)]
    values = kv_all[pl.ds(pl.multiple_of(half_kv + step * HD, HD), HD)]
    scores[...] = jnp.dot(keys.T, q3[...], preferred_element_type=jnp.float32)
    for h in range(GROUP):
        cols = slice(h * rows, (h + 1) * rows)
        masked = scores[:, cols] + bias[...]
        exponent = jnp.exp(masked - jnp.max(masked, axis=0, keepdims=True))
        inverse = 1.0 / jnp.sum(exponent, axis=0, keepdims=True)
        p_ref[0, :, cols] = (exponent * inverse).astype(jnp.bfloat16)
    attended = jnp.dot(values, p_ref[0], preferred_element_type=jnp.float32).astype(jnp.bfloat16)
    for h in range(GROUP):
        at = pl.multiple_of((step * GROUP + h) * HD, HD)
        head_ref[pl.ds(at, HD)] = attended[:, h * rows : (h + 1) * rows]

    @pl.when(step == pl.num_programs(0) - 1)
    def _():
        for copy in copies:
            copy.wait()
        part[...] = nt_dot(head_ref[...].T, out_t[...])
        share_out(place, part, own_ref, other_refs)


def attend(place, starts, q_t, pieces, shards):
    n_ctx, n_tp = lax.axis_size("ctx"), lax.axis_size("tp")
    q_rows, rows = q_t.shape
    kv = q_rows // (GROUP * HD)
    width = shards[0].shape[0] * len(shards)
    seq = rows * n_ctx
    low = jnp.bfloat16
    return pl.pallas_call(
        functools.partial(attend_kernel, n_ctx),
        grid=(kv,),
        out_shape=[
            jax.ShapeDtypeStruct((kv, seq, GROUP * rows), low),
            jax.ShapeDtypeStruct((q_rows, rows), low),
            jax.ShapeDtypeStruct((2 * kv * HD, seq), low),
            jax.ShapeDtypeStruct((width, q_rows), low),
            jax.ShapeDtypeStruct((rows // n_tp, width), jnp.float32),
        ]
        + [jax.ShapeDtypeStruct((rows // n_tp, width), low)] * (n_tp - 1),
        in_specs=[smem_spec(), vmem_spec(), pl.BlockSpec((GROUP * HD, rows), lambda i: (i, 0))]
        + [vmem_spec()]
        + [any_spec()] * len(shards),
        out_specs=[pl.BlockSpec((1, seq, GROUP * rows), lambda i: (i, 0, 0))] + [vmem_spec()] * (3 + n_tp),
        scratch_shapes=[
            pltpu.VMEM((seq, rows), jnp.float32),
            pltpu.VMEM((seq, GROUP * rows), jnp.float32),
            pltpu.VMEM((HD, GROUP * rows), low),
            pltpu.VMEM((rows, width), jnp.float32),
            pltpu.SemaphoreType.DMA((len(shards),)),
        ],
        compiler_params=pltpu.CompilerParams(vmem_limit_bytes=VMEM_LIMIT),
        cost_estimate=pl.CostEstimate(
            flops=2 * q_rows * rows * (2 * seq + width), bytes_accessed=20 << 20, transcendentals=0
        ),
        name="attend",
    )(place, starts, q_t, pieces, *shards)


def attend_back_kernel(n_ctx, *refs):
    place, p_ref, q_ref, kv_all, out_t, cos_ref, sin_ref = refs[:7]
    grad_refs, (dq_ref, piece_ref, grad_all, grads, q3, g3) = refs[7:-6], refs[-6:]
    rows = q_ref.shape[1]
    half_kv = kv_all.shape[0] // 2
    step = pl.program_id(0)

    @pl.when(step == 0)
    def _():
        join_kernel(place, *grad_refs, grad_all)
        back = jnp.dot(grad_all[...], out_t[...], preferred_element_type=jnp.float32)
        grads[...] = back.astype(jnp.bfloat16).T

    for h in range(GROUP):
        cols = slice(h * rows, (h + 1) * rows)
        q3[:, cols] = q_ref[h * HD : (h + 1) * HD]
        g3[:, cols] = grads[pl.ds(pl.multiple_of((step * GROUP + h) * HD, HD), HD)]
    keys = kv_all[pl.ds(pl.multiple_of(step * HD, HD), HD)]
    values = kv_all[pl.ds(pl.multiple_of(half_kv + step * HD, HD), HD)]
    probs = p_ref[0].astype(jnp.float32)
    grad_probs = jnp.dot(values.T, g3[...], preferred_element_type=jnp.float32)
    inner = jnp.sum(probs * grad_probs, axis=0, keepdims=True)
    grad_scores = (probs * (grad_probs - inner)).astype(jnp.bfloat16)
    grad_query = jnp.dot(keys, grad_scores, preferred_element_type=jnp.float32) * HD**-0.5
    grad_key = nt_dot(grad_scores, q3[...]).T
    grad_value = nt_dot(p_ref[0], g3[...]).T
    half = HD // 2
    cosine, sine = cos_ref[...], -sin_ref[...]
    for h in range(GROUP):
        cols = slice(h * rows, (h + 1) * rows)
        a, b = turn(grad_query[:half, cols], grad_query[half:, cols], cosine, sine)
        dq_ref[h * HD : h * HD + half] = a.astype(jnp.bfloat16)
        dq_ref[h * HD + half : (h + 1) * HD] = b.astype(jnp.bfloat16)
    key_at = pl.ds(pl.multiple_of(step * HD, HD), HD)
    value_at = pl.ds(pl.multiple_of(half_kv + step * HD, HD), HD)
    for j in range(n_ctx):
        cols = slice(j * rows, (j + 1) * rows)
        piece_ref[j, key_at] = grad_key[:, cols].astype(jnp.bfloat16)
        piece_ref[j, value_at] = grad_value[:, cols].astype(jnp.bfloat16)


def attend_back(place, probs, q_t, kv_all, grads, out_t, cosine, sine):
    n_ctx = lax.axis_size("ctx")
    q_rows, rows = q_t.shape
    kv, seq = probs.shape[:2]
    low = jnp.bfloat16
    block = pl.BlockSpec((GROUP * HD, rows), lambda i: (i, 0))
    return pl.pallas_call(
        functools.partial(attend_back_kernel, n_ctx),
        grid=(kv,),
        out_shape=[
            jax.ShapeDtypeStruct((q_rows, rows), low),
            jax.ShapeDtypeStruct((n_ctx, 2 * kv * HD, rows), low),
        ],
        in_specs=[smem_spec(), pl.BlockSpec((1, seq, GROUP * rows), lambda i: (i, 0, 0)), block]
        + [vmem_spec()] * (4 + len(grads)),
        out_specs=[block, vmem_spec()],
        scratch_shapes=[
            pltpu.VMEM((rows, out_t.shape[0]), low),
            pltpu.VMEM((q_rows, rows), low),
            pltpu.VMEM((HD, GROUP * rows), low),
            pltpu.VMEM((HD, GROUP * rows), low),
        ],
        compiler_params=pltpu.CompilerParams(vmem_limit_bytes=VMEM_LIMIT),
        cost_estimate=pl.CostEstimate(
            flops=2 * q_rows * rows * (4 * seq + out_t.shape[0]), bytes_accessed=20 << 20, transcendentals=0
        ),
        name="attend_back",
    )(place, probs, q_t, kv_all, out_t, cosine, sine, *grads)


def store_products(place, left_t, right, out_refs):
    rows = out_refs[0].shape[0]
    for mask, out in zip(F_MASKS, out_refs):
        at = pl.multiple_of((place[0] ^ mask) * rows, rows)
        out[...] = jnp.dot(
            left_t[pl.ds(at, rows)], right, preferred_element_type=jnp.float32
        ).astype(jnp.bfloat16)


def query_grad_kernel(place, dq_ref, norm_t, whole, head_ref, *refs):
    grad_refs, (near, far, core, part_ref, grad_all, grad_t) = refs[:-6], refs[-6:]
    columns = whole.shape[1]
    back = dq_ref[...].T
    outs = [near, far, core.at[0], core.at[1]]
    store_products(place, norm_t, back, [out.at[:, :columns] for out in outs])
    join_kernel(place, *grad_refs, grad_all)
    grad_t[...] = grad_all[...].T
    store_products(place, grad_t, head_ref[...].T, [out.at[:, columns:] for out in outs])
    part_ref[...] = nt_dot(back, whole[...])


def row_parts(rows, columns):
    low = jnp.bfloat16
    return [
        jax.ShapeDtypeStruct((rows, columns), low),
        jax.ShapeDtypeStruct((rows, columns), low),
        jax.ShapeDtypeStruct((2, rows, columns), low),
    ]


def query_grads(place, dq_t, norm_t, whole, grads, head_t):
    q_rows, rows = dq_t.shape
    width = norm_t.shape[0]
    outs = pl.pallas_call(
        query_grad_kernel,
        out_shape=row_parts(width // len(F_MASKS), 2 * q_rows)
        + [jax.ShapeDtypeStruct((rows, width), jnp.float32)],
        in_specs=[smem_spec()] + [vmem_spec()] * (4 + len(grads)),
        out_specs=[vmem_spec()] * 4,
        scratch_shapes=[pltpu.VMEM((rows, width), jnp.bfloat16), pltpu.VMEM((width, rows), jnp.bfloat16)],
        compiler_params=params(),
        cost_estimate=cost(6 * rows * width * q_rows, 15),
        name="query_grads",
    )(place, dq_t, norm_t, whole, head_t, *grads)
    return outs[:3], outs[3]


def key_grad_kernel(n_ctx, *refs):
    place, piece_ref = refs[:2]
    refs = refs[2:]
    cos_ref, sin_ref, norm_t, whole, tok, query_part, gain_two_ref = refs[:7]
    near, far, core, own_ref = refs[7:11]
    other_refs, (part_ref, back_t, right) = refs[11:-3], refs[-3:]
    kv_rows, rows = piece_ref.shape[1:]
    total = piece_ref[0].astype(jnp.float32)
    for j in range(1, n_ctx):
        total += piece_ref[j].astype(jnp.float32)
    cosine, sine = cos_ref[...], -sin_ref[...]
    half = HD // 2
    for at in range(0, kv_rows // 2, HD):
        a, b = turn(total[at : at + half], total[at + half : at + HD], cosine, sine)
        back_t[at : at + half] = a.astype(jnp.bfloat16)
        back_t[at + half : at + HD] = b.astype(jnp.bfloat16)
    back_t[kv_rows // 2 :] = total[kv_rows // 2 :].astype(jnp.bfloat16)
    back = back_t[...].T
    part = query_part[...] + nt_dot(back, whole[:, :kv_rows])
    part_ref[...] = part
    share_out(place, part_ref, own_ref, other_refs)
    outs = [near, far, core.at[0], core.at[1]]
    store_products(place, norm_t, back, [out.at[:, :kv_rows] for out in outs])
    x = tok[...].astype(jnp.float32)
    hat = x * lax.rsqrt(jnp.mean(x * x, axis=-1, keepdims=True) + EPSILON)
    gain_one = jnp.sum(part * hat, axis=0, keepdims=True)
    row = lax.broadcasted_iota(jnp.int32, (128, x.shape[1]), 0)
    columns = jnp.where(row == 0, gain_one, jnp.where(row == 1, gain_two_ref[...], 0.0))
    right[...] = columns.T
    count = near.shape[0]
    for mask, out in zip(F_MASKS, outs):
        at = pl.multiple_of((place[0] ^ mask) * count, count)
        out[:, kv_rows:] = right[pl.ds(at, count)].astype(jnp.bfloat16)


def key_grads(place, pieces, cosine, sine, norm_t, whole, tokens, query_part, gain_two):
    n_ctx, n_tp = lax.axis_size("ctx"), lax.axis_size("tp")
    kv_rows, rows = pieces.shape[1:]
    width = norm_t.shape[0]
    outs = pl.pallas_call(
        functools.partial(key_grad_kernel, n_ctx),
        out_shape=row_parts(width // len(F_MASKS), kv_rows + 128)
        + [jax.ShapeDtypeStruct((rows // n_tp, width), jnp.float32)]
        + [jax.ShapeDtypeStruct((rows // n_tp, width), jnp.bfloat16)] * (n_tp - 1),
        in_specs=[smem_spec()] + [vmem_spec()] * 8,
        out_specs=[vmem_spec()] * (3 + n_tp),
        scratch_shapes=[
            pltpu.VMEM((rows, width), jnp.float32),
            pltpu.VMEM((kv_rows, rows), jnp.bfloat16),
            pltpu.VMEM((width, 128), jnp.float32),
        ],
        compiler_params=params(),
        cost_estimate=cost(4 * rows * width * kv_rows, 12),
        name="key_grads",
    )(place, pieces, cosine, sine, norm_t, whole, tokens, query_part, gain_two)
    return outs[:3], outs[3:]


def sum_cores(parts, *before):
    near, far, core = parts
    core = after(swap(core, "fsdp", 1), *before)
    return added(near, core[0]), added(far, core[1])


def scatter_rows(near):
    n_ctx = lax.axis_size("ctx")
    return spread(near.reshape(n_ctx, near.shape[0] // n_ctx, near.shape[1]))


def table(count):
    near = [((m, 0), (m, 1)) for m in range(count)]
    far = [((count, 0), (count, 1))]
    far += [((count + m, 0), (2 * count - 1 + m, 0)) for m in range(1, count)]
    return [near, far] + [
        [tuple((array + 3 * count - 1, at) for array, at in piece) for piece in pieces] for pieces in (near, far)
    ]


def load_experts(refs, target, sems, kinds):
    half, hidden = refs[0].shape[2:]
    copies = []
    for expert, pieces in enumerate(table((len(refs) + 2) // 6)):
        for m, piece in enumerate(pieces):
            for at, kind in enumerate(kinds):
                for j, (array, index) in enumerate(piece):
                    copies.append(
                        pltpu.make_async_copy(
                            refs[array].at[index, kind],
                            target.at[at, expert, j * half : (j + 1) * half, m * hidden : (m + 1) * hidden],
                            sems.at[expert, (m * len(kinds) + at) * 2 + j],
                        )
                    )
    return copies


def weight_scratch(weights, kinds):
    count = (len(weights) + 2) // 6
    half, hidden = weights[0].shape[2:]
    return [
        pltpu.VMEM((kinds, len(F_MASKS), 2 * half, count * hidden), jnp.bfloat16),
        pltpu.SemaphoreType.DMA((len(F_MASKS), 2 * kinds * count)),
    ]


def back_kernel(og_ref, *refs):
    weight_refs, (back_ref, og_all, weights, sems) = refs[:-4], refs[-4:]
    copies = load_experts(weight_refs, weights, sems, (2,))
    for copy in copies:
        copy.start()
    blocks, rows, _ = og_ref.shape
    width = og_all.shape[1]
    for b in range(blocks):
        og_all[b * rows : (b + 1) * rows] = og_ref[b, :, :width]
    hidden = weights.shape[3]
    each = len(copies) // len(F_MASKS)
    for expert in range(len(F_MASKS)):
        for copy in copies[expert * each : (expert + 1) * each]:
            copy.wait()
        back = jnp.dot(og_all[...], weights[0, expert], preferred_element_type=jnp.float32)
        for b in range(blocks):
            back_ref[b, :, expert * hidden : (expert + 1) * hidden] = back[b * rows : (b + 1) * rows].astype(
                jnp.bfloat16
            )


def back_rows(og, weights, width):
    blocks, rows, _ = og.shape
    scratch = weight_scratch(weights, 1)
    hidden = scratch[0].shape[3] * len(F_MASKS)
    return pl.pallas_call(
        back_kernel,
        out_shape=jax.ShapeDtypeStruct((blocks, rows, hidden), jnp.bfloat16),
        in_specs=[vmem_spec()] + [any_spec()] * len(weights),
        out_specs=vmem_spec(),
        scratch_shapes=[pltpu.VMEM((blocks * rows, width), jnp.bfloat16)] + scratch,
        compiler_params=params(),
        cost_estimate=cost(2 * blocks * rows * width * hidden, 12),
        name="back_rows",
    )(og, *weights)


def expert_kernel(masks, experts, *refs):
    blocks = len(masks)
    place, refs = refs[0], refs[1:]
    x_refs, refs = refs[:blocks], refs[blocks:]
    gate_ref, back_ref, refs = refs[0], refs[1], refs[2:]
    weight_refs, refs = refs[: -8 - blocks], refs[-8 - blocks :]
    gx_refs, refs = refs[:blocks], refs[blocks:]
    act_ref, gg_ref, gu_ref, x_all, gates, total, weights, sems = refs
    copies = load_experts(weight_refs, weights, sems, (0, 1))
    for copy in copies:
        copy.start()
    rows = x_refs[0].shape[0]
    for b, mask in enumerate(masks):
        x_all[b * rows : (b + 1) * rows] = x_refs[b][...]
        gates[b * rows : (b + 1) * rows] = gate_ref[place[1] ^ mask].astype(jnp.float32)
    hidden = weights.shape[3]
    each = len(copies) // len(F_MASKS)
    lane = lax.broadcasted_iota(jnp.int32, gates.shape, 1)
    x = x_all[...]
    for i, mask in enumerate(F_MASKS):
        for copy in copies[i * each : (i + 1) * each]:
            copy.wait()
        expert = (place[0] ^ mask) * (experts // len(F_MASKS)) + place[1]
        chosen = (lane == expert) | (lane == expert + experts)
        weight = jnp.sum(jnp.where(chosen, gates[...], 0.0), axis=1, keepdims=True)
        gate = jnp.dot(x, weights[0, i], preferred_element_type=jnp.float32)
        up = jnp.dot(x, weights[1, i], preferred_element_type=jnp.float32)
        cols = slice(i * hidden, (i + 1) * hidden)
        back = jnp.concatenate([back_ref[place[1] ^ m, :, cols] for m in masks]).astype(jnp.float32) * weight
        sig = jax.nn.sigmoid(gate)
        silu = gate * sig
        act_ref[:, cols] = (silu * up * weight).astype(jnp.bfloat16)
        grad_gate = (back * up * (sig * (1.0 + gate * (1.0 - sig)))).astype(jnp.bfloat16)
        grad_up = (back * silu).astype(jnp.bfloat16)
        gg_ref[:, cols] = grad_gate
        gu_ref[:, cols] = grad_up
        more = nt_dot(grad_gate, weights[0, i]) + nt_dot(grad_up, weights[1, i])
        if i == 0:
            total[...] = more
        else:
            total[...] += more
    for b in range(blocks):
        gx_refs[b][...] = total[b * rows : (b + 1) * rows].astype(jnp.bfloat16)


def expert_rows(place, masks, xs, og, backs, weights, experts):
    blocks, (rows, width) = len(xs), xs[0].shape
    n_ctx = og.shape[0]
    low = jnp.bfloat16
    scratch = weight_scratch(weights, 2)
    hidden = scratch[0].shape[3] * len(F_MASKS)
    wide = jax.ShapeDtypeStruct((blocks * rows, hidden), low)
    outs = pl.pallas_call(
        functools.partial(expert_kernel, masks, experts),
        grid=(1,),
        out_shape=[jax.ShapeDtypeStruct((rows, width), low)] * blocks + [wide] * 3,
        in_specs=[smem_spec()]
        + [vmem_spec()] * blocks
        + [pl.BlockSpec((n_ctx, rows, 128), lambda i: (0, 0, width // 128)), vmem_spec()]
        + [any_spec()] * len(weights),
        out_specs=[vmem_spec()] * (blocks + 3),
        scratch_shapes=[
            pltpu.VMEM((blocks * rows, width), low),
            pltpu.VMEM((blocks * rows, 128), jnp.float32),
            pltpu.VMEM((blocks * rows, width), jnp.float32),
        ]
        + scratch,
        compiler_params=params(),
        cost_estimate=cost(8 * blocks * rows * width * hidden, 20),
        name="expert_rows",
    )(place, *xs, og, backs, *weights)
    return outs[:blocks], outs[blocks:]


def mix_kernel(calls, place, *refs):
    act_refs, refs = refs[:calls], refs[calls:]
    weight_refs, (mix_ref, total, weights, sems) = refs[:-4], refs[-4:]
    copies = load_experts(weight_refs, weights, sems, (2,))
    for copy in copies:
        copy.start()
    hidden = weights.shape[3]
    some = act_refs[0].shape[0]
    each = len(copies) // len(F_MASKS)
    for i in range(len(F_MASKS)):
        for copy in copies[i * each : (i + 1) * each]:
            copy.wait()
        for j in range(calls):
            more = nt_dot(act_refs[j][:, i * hidden : (i + 1) * hidden], weights[0, i])
            if i == 0:
                total[j * some : (j + 1) * some] = more
            else:
                total[j * some : (j + 1) * some] += more
    blocks, rows, _ = mix_ref.shape
    for b in range(blocks):
        mix_ref[place[1] ^ b] = total[b * rows : (b + 1) * rows].astype(jnp.bfloat16)


def mix_rows(place, acts, weights, blocks, width):
    calls, (some, hidden) = len(acts), acts[0].shape
    rows = some * calls // blocks
    return pl.pallas_call(
        functools.partial(mix_kernel, calls),
        out_shape=jax.ShapeDtypeStruct((blocks, rows, width), jnp.bfloat16),
        in_specs=[smem_spec()] + [vmem_spec()] * calls + [any_spec()] * len(weights),
        out_specs=vmem_spec(),
        scratch_shapes=[pltpu.VMEM((some * calls, width), jnp.float32)] + weight_scratch(weights, 1),
        compiler_params=params(),
        cost_estimate=cost(2 * blocks * rows * width * hidden, 12),
        name="mix_rows",
    )(place, *acts, *weights)


def weight_kernel(blocks, calls, count, *refs):
    place, og_ref, refs = refs[0], refs[1], refs[2:]
    x_refs, refs = refs[:blocks], refs[blocks:]
    act_refs, refs = refs[:calls], refs[calls:]
    gg_refs, refs = refs[:calls], refs[calls:]
    gu_refs, refs = refs[:calls], refs[calls:]
    leave, stay, x_t, og_t, right = refs
    rows, width = x_refs[0].shape
    step = pl.program_id(0)

    @pl.when(step == 0)
    def _():
        for b in range(blocks):
            x_t[:, b * rows : (b + 1) * rows] = x_refs[b][...].T
            og_t[:, b * rows : (b + 1) * rows] = og_ref[place[1] ^ b, :, :width].T

    some = act_refs[0].shape[0]
    half = width // 2
    hidden = right.shape[1] // count
    for kind, (left, parts) in enumerate(((x_t, gg_refs), (x_t, gu_refs), (og_t, act_refs))):
        for i in range(calls):
            right[i * some : (i + 1) * some] = parts[i][...]
        for j in range(2):
            product = jnp.dot(
                left[j * half : (j + 1) * half], right[...], preferred_element_type=jnp.float32
            ).astype(jnp.bfloat16)
            for m in range(count):
                piece = product[:, m * hidden : (m + 1) * hidden]
                if j == 0 and m == 0:
                    stay[step, kind] = piece
                elif j == 0:
                    leave[2 * (m - 1) + step, kind] = piece
                else:

                    @pl.when(step == 0)
                    def _(m=m, kind=kind, piece=piece):
                        stay[2 + m, kind] = piece

                    @pl.when(step == 1)
                    def _(m=m, kind=kind, piece=piece):
                        leave[2 * (count - 1) + m, kind] = piece


def weight_grads(place, xs, og, acts, ggs, gus, count, first):
    blocks, calls, (rows, width) = len(xs), len(acts), xs[0].shape
    some, wide = acts[0].shape
    whole = wide // len(F_MASKS)
    hidden, half = whole // count, width // 2
    column = pl.BlockSpec((some, whole), lambda i: (0, first + i))
    low = jnp.bfloat16
    total = blocks * rows
    outs = [(3 * count - 2, 3, half, hidden), (count + 2, 3, half, hidden)]
    return pl.pallas_call(
        functools.partial(weight_kernel, blocks, calls, count),
        grid=(2,),
        out_shape=[jax.ShapeDtypeStruct(shape, low) for shape in outs],
        in_specs=[smem_spec()] + [vmem_spec()] * (blocks + 1) + [column] * (3 * calls),
        out_specs=[pl.BlockSpec(shape, lambda i: (0, 0, 0, 0)) for shape in outs],
        scratch_shapes=[
            pltpu.VMEM((width, total), low),
            pltpu.VMEM((width, total), low),
            pltpu.VMEM((total, whole), low),
        ],
        compiler_params=params(),
        cost_estimate=cost(2 * 3 * total * width * 2 * whole, 20),
        name="weight_grads",
    )(place, og, *xs, *acts, *ggs, *gus)


def total_of(*parts):
    return sum(part.astype(jnp.float32) for part in parts).astype(jnp.bfloat16)


def step_in_kernel(uppers, lowers, *refs):
    up_refs, refs = refs[:uppers], refs[uppers:]
    low_refs, refs = refs[:lowers], refs[lowers:]
    weight, moment, average, moment_new, average_new, weight_new, grad = refs

    def gather(parts):
        total = parts[0][0, 0].astype(jnp.float32)
        for part in parts[1:]:
            total += part[0, 0].astype(jnp.float32)
        grad[...] = total

    @pl.when(pl.program_id(1) == 0)
    def _():
        gather(up_refs)

    @pl.when(pl.program_id(1) == 1)
    def _():
        gather(low_refs)

    new = advance(weight[0, 0], grad[...], moment[0, 0], average[0, 0], RATE_IN)
    moment_new[0, 0], average_new[0, 0], weight_new[0, 0] = new


def step_in(uppers, lowers, weight, moment, average):
    half, hidden = uppers[0][0].shape[2:]
    parts = uppers + lowers
    specs = [pl.BlockSpec((1, 1, half, hidden), lambda k, j, at=at: (at, k, 0, 0)) for _, at in parts]
    block = pl.BlockSpec((1, 1, half, hidden), lambda k, j: (0, k, j, 0))
    return pl.pallas_call(
        functools.partial(step_in_kernel, len(uppers), len(lowers)),
        grid=(2, 2),
        out_shape=[jax.ShapeDtypeStruct(weight.shape, jnp.float32)] * 3,
        in_specs=specs + [block] * 3,
        out_specs=[block] * 3,
        scratch_shapes=[pltpu.VMEM((half, hidden), jnp.float32)],
        compiler_params=params(),
        cost_estimate=cost(10 * weight.size, 22),
        name="step_in",
    )(*(part for part, _ in parts), weight, moment, average)


def step_down_kernel(uppers, lowers, *refs):
    up_refs, refs = refs[:uppers], refs[uppers:]
    low_refs, refs = refs[:lowers], refs[lowers:]
    weight, moment, average, moment_new, average_new, weight_new, grad = refs

    def gather(parts):
        total = parts[0][0, 0].astype(jnp.float32)
        for part in parts[1:]:
            total += part[0, 0].astype(jnp.float32)
        grad[...] = total.T

    @pl.when(pl.program_id(0) == 0)
    def _():
        gather(up_refs)

    @pl.when(pl.program_id(0) == 1)
    def _():
        gather(low_refs)

    new = advance(weight[0], grad[...], moment[0], average[0], RATE_DOWN)
    moment_new[0], average_new[0], weight_new[0] = new


def step_down(uppers, lowers, weight, moment, average):
    half, hidden = uppers[0][0].shape[2:]
    parts = uppers + lowers
    specs = [pl.BlockSpec((1, 1, half, hidden), lambda j, at=at: (at, 2, 0, 0)) for _, at in parts]
    block = pl.BlockSpec((1, hidden, half), lambda j: (0, 0, j))
    return pl.pallas_call(
        functools.partial(step_down_kernel, len(uppers), len(lowers)),
        grid=(2,),
        out_shape=[jax.ShapeDtypeStruct(weight.shape, jnp.float32)] * 3,
        in_specs=specs + [block] * 3,
        out_specs=[block] * 3,
        scratch_shapes=[pltpu.VMEM((hidden, half), jnp.float32)],
        compiler_params=params(),
        cost_estimate=cost(10 * weight.size, 12),
        name="step_down",
    )(*(part for part, _ in parts), weight, moment, average)


def sum_first(ref, cols):
    total = ref[0, :, cols].astype(jnp.float32)
    for i in range(1, ref.shape[0]):
        total += ref[i, :, cols].astype(jnp.float32)
    return total


def step_out_kernel(come, weight, moment, average, moment_new, average_new, weight_new, wide):
    rows = come.shape[1]
    wide[...] = jnp.zeros_like(wide)
    wide[:rows] = sum_first(come, slice(come.shape[2] // 2, come.shape[2]))
    new = advance(weight[...], wide[...].T[:, :rows], moment[...], average[...], RATE_OUT)
    moment_new[...], average_new[...], weight_new[...] = new


def step_out(come, weight, moment, average):
    return pl.pallas_call(
        step_out_kernel,
        out_shape=[jax.ShapeDtypeStruct(weight.shape, jnp.float32)] * 3,
        in_specs=[vmem_spec()] * 4,
        out_specs=[vmem_spec()] * 3,
        scratch_shapes=[pltpu.VMEM((128, weight.shape[0]), jnp.float32)],
        compiler_params=params(),
        cost_estimate=cost(1, 1),
        name="step_out",
    )(come, weight, moment, average)


def step_qkv_kernel(
    query_come, key_come, weight, moment, average, moment_new, average_new, weight_new, grad, wide
):
    kv = weight.shape[1] // ((GROUP + 2) * HD)
    group = GROUP * HD
    queries = sum_first(query_come, slice(0, kv * group))
    wide[...] = sum_first(key_come, slice(None))
    for h in range(kv):
        at = h * (GROUP + 2) * HD
        grad[:, at : at + group] = queries[:, h * group : (h + 1) * group]
        grad[:, at + group : at + group + HD] = wide[:, h * HD : (h + 1) * HD]
        grad[:, at + group + HD : at + group + 2 * HD] = wide[:, (kv + h) * HD : (kv + h + 1) * HD]
    new = advance(weight[...], grad[...], moment[...], average[...], RATE_QKV)
    moment_new[...], average_new[...], weight_new[...] = new


def step_qkv(query_come, key_come, weight, moment, average):
    return pl.pallas_call(
        step_qkv_kernel,
        out_shape=[jax.ShapeDtypeStruct(weight.shape, jnp.float32)] * 3,
        in_specs=[vmem_spec()] * 5,
        out_specs=[vmem_spec()] * 3,
        scratch_shapes=[
            pltpu.VMEM(weight.shape, jnp.float32),
            pltpu.VMEM(key_come.shape[1:], jnp.float32),
        ],
        compiler_params=params(),
        cost_estimate=cost(1, 1),
        name="step_qkv",
    )(query_come, key_come, weight, moment, average)


def per_device(
    tokens,
    out_grad,
    lengths,
    routes,
    gate_weights,
    qkv_weight,
    out_weight,
    norm_gains,
    expert_in,
    expert_down,
    qkv_moment,
    qkv_average,
    out_moment,
    out_average,
    gain_moment,
    gain_average,
    in_moment,
    in_average,
    down_moment,
    down_average,
):
    tok_rows, width = tokens.shape
    n_ctx, n_tp = lax.axis_size("ctx"), lax.axis_size("tp")
    experts = lax.axis_size(("fsdp", "ctx"))
    fsdp_index, ctx_index = lax.axis_index("fsdp"), lax.axis_index("ctx")
    tp_index = lax.axis_index("tp")
    place = jnp.stack([fsdp_index, ctx_index, tp_index]).astype(jnp.int32)
    low, f32 = jnp.bfloat16, jnp.float32
    half_rows = tok_rows // n_tp
    over_tp = range(n_tp)

    def part_of(value, mask):
        return lax.dynamic_slice_in_dim(value, (tp_index ^ mask) * half_rows, half_rows)

    def own_half(value):
        return part_of(value, 0)

    def sum_own(own, others):
        for m, other in enumerate(others, 1):
            own = own + swap(other, "tp", m).astype(f32)
        return own

    def to_others(own):
        return [own] + [swap(own, "tp", m) for m in over_tp[1:]]

    shard_rows, qkv_columns = qkv_weight.shape
    kv_local = qkv_columns // ((GROUP + 2) * HD)
    q_rows, k_rows = kv_local * GROUP * HD, kv_local * HD
    key_near = spread(shard_copies(qkv_weight, norm_gains, True)).reshape(-1, 2 * k_rows + 128)
    key_across = swap(key_near, "fsdp", 2)
    key_shards = [key_near, key_across, swap(key_near, "fsdp", 1), swap(key_across, "fsdp", 1)]
    both_near = spread(shard_copies(after(qkv_weight, key_near), out_weight, False)).reshape(-1, 2 * q_rows)

    down_t = expert_down[0].T[None]
    half = width // 2
    own = jnp.stack(
        [jnp.concatenate([expert_in[0, :, rows], down_t[:, rows]]) for rows in (slice(0, half), slice(half, width))]
    ).astype(low)
    along_tp = [swap(after(own, key_near), "tp", m) for m in over_tp[1:]]
    along_x = swap(after(own, *key_shards[2:]), "fsdp", 2)

    places = ctx_index * tok_rows + jnp.arange(tok_rows, dtype=jnp.int32)
    _, position = doc_positions(lengths[0], places)
    starts = (places - position)[None, :]
    frequency = jnp.exp(jnp.arange(HD // 2, dtype=f32) * (-2.0 * math.log(ROPE_BASE) / HD))
    angles = frequency[:, None] * position.astype(f32)[None, :]
    cosine, sine = jnp.cos(angles), jnp.sin(angles)
    kv_t, normed_low, norm_t, key_whole, gains = project_keys(
        place, tokens, cosine, sine, key_shards, k_rows
    )
    gain_one, gain_two = gains[0], gains[1]
    both_across = swap(after(both_near, kv_t, along_x), "fsdp", 2)
    both_shards = [
        both_near,
        both_across,
        swap(after(both_near, kv_t), "fsdp", 1),
        swap(after(both_across, kv_t), "fsdp", 1),
    ]
    kv_pieces = spread(kv_t)
    q_t, query_whole = project_queries(place, normed_low, cosine, sine, both_shards)

    uppers = [swap(along_x[:1], "tp", m) for m in over_tp[1:]]
    lowers = [swap(after(piece[1:], both_across), "fsdp", 2) for piece in along_tp]
    soon = [swap(after(own, both_near), "fsdp", 1)]

    grad_rows = row_copies(after(place, kv_t), out_grad, routes, gate_weights, half_rows, experts)
    og = spread(after(grad_rows, kv_pieces))

    probs, head_t, kv_all, out_t, attn_own, *attn_others = attend(
        after(place, *soon, *along_tp), starts, q_t, kv_pieces, both_shards
    )
    soon += [swap(after(piece, attn_own), "fsdp", 1) for piece in [*along_tp, along_x, *uppers, *lowers]]
    hidden_one = own_half(after(tokens, og, *soon)).astype(f32) + sum_own(attn_own, attn_others)
    inverse_two = lax.rsqrt(jnp.mean(hidden_one * hidden_one, axis=-1, keepdims=True) + EPSILON)
    normed_two = hidden_one * inverse_two
    normed_two_low = (normed_two * gain_two).astype(low)

    x_own = after(normed_two_low, og)
    xs = [x_own] + [swap(x_own, "ctx", m) for m in range(1, n_ctx)]
    weights = [own, *along_tp, along_x, *uppers, *lowers, *soon]
    backs = back_rows(og, weights, width)
    grads_x, acts, ggs, gus = [], [], [], []
    for at in range(0, n_ctx, 2):
        here = after(place, *acts[-1:])
        some_x, (act, gg, gu) = expert_rows(
            here, tuple(range(at, at + 2)), xs[at : at + 2], og, backs, weights, experts
        )
        grads_x += some_x
        acts.append(act)
        ggs.append(gg)
        gus.append(gu)
    come_x = [swap(grads_x[m], "ctx", m) for m in range(1, n_ctx)]
    core_leave, core_stay = weight_grads(place, xs, og, acts, ggs, gus, n_tp, 2)
    leave, stay = weight_grads(after(place, core_leave), xs, og, acts, ggs, gus, n_tp, 0)
    mixes = mix_rows(after(place, leave), acts, weights, n_ctx, width)

    grad_normed_two = after(grads_x[0], mixes).astype(f32)
    for come in come_x:
        grad_normed_two += come.astype(f32)
    gain_grad_two = jnp.sum(grad_normed_two * normed_two, axis=0)
    grad_hidden = own_half(out_grad).astype(f32) + norm_back(grad_normed_two, normed_two, inverse_two, gain_two)
    grad_attn = to_others(grad_hidden.astype(low))
    core_leave = swap(after(core_leave, mixes, *come_x), "fsdp", 1)
    come_mix = spread(after(mixes, grad_hidden))

    uppers_out = [
        total_of(leave[2 * m : 2 * m + 2], core_leave[2 * m : 2 * m + 2]) for m in range(n_tp - 1)
    ]
    lower_out = total_of(leave[2 * (n_tp - 1) :], core_leave[2 * (n_tp - 1) :])
    uppers_in = [swap(uppers_out[m - 1], "tp", m) for m in over_tp[1:]]
    lower_in = swap(lower_out, "fsdp", 2)

    dq_t, kv_grads = attend_back(
        after(place, lower_out, *uppers_out), probs, q_t, kv_all, grad_attn, out_t, cosine, sine
    )
    mixture = jnp.sum(after(come_mix, dq_t).astype(f32), axis=0)
    come = spread(kv_grads)
    core_stay = swap(after(core_stay, lower_out), "fsdp", 1)
    query_parts, query_part = query_grads(
        after(place, mixture), dq_t, norm_t, query_whole, grad_attn, head_t
    )

    lower_next = [
        total_of(stay[2 + m], core_stay[2 + m], after(lower_in, query_part)[m]) for m in over_tp[1:]
    ]
    upper_next = total_of(stay[1], core_stay[1], *(after(part, query_part)[1] for part in uppers_in))
    lowers_last = [swap(lower_next[m - 1], "tp", m) for m in over_tp[1:]]
    query_near, query_far = sum_cores(query_parts, upper_next, *lower_next)
    query_near = added(query_near, swap(query_far, "fsdp", 2))
    upper_last = swap(after(upper_next, query_near), "fsdp", 2)
    key_parts, (normed_own, *normed_others) = key_grads(
        after(place, query_near, *lowers_last), come, cosine, sine, norm_t, key_whole,
        tokens, query_part, gain_grad_two[None]
    )
    grad_normed_one = sum_own(normed_own, normed_others)
    block_parts = to_others((hidden_one + mixture).astype(low))
    inputs = own_half(tokens).astype(f32)
    inverse_one = lax.rsqrt(jnp.mean(inputs * inputs, axis=-1, keepdims=True) + EPSILON)
    in_parts = to_others(
        (grad_hidden + norm_back(grad_normed_one, inputs * inverse_one, inverse_one, gain_one)).astype(low)
    )
    key_near, key_far = sum_cores(key_parts, upper_last)
    query_grad = scatter_rows(query_near)
    upper_parts = [(stay, 0), (core_stay, 0)] + [(part, 0) for part in uppers_in] + [(upper_last[None], 0)]
    lower_parts = [(stay, 2), (core_stay, 2), (lower_in, 0)] + [(part[None], 0) for part in lowers_last]
    in_new = step_in(upper_parts, lower_parts, after(expert_in, key_far), in_moment, in_average)
    key_near = added(key_near, after(swap(key_far, "fsdp", 2), query_grad, in_new[0]))
    key_grad = scatter_rows(key_near)
    block_out = join(place, [after(part, key_near) for part in block_parts])
    out_new = step_out(query_grad, after(out_weight, block_out), out_moment, out_average)
    down_new = step_down(upper_parts, lower_parts, after(expert_down, out_new[0]), down_moment, down_average)
    in_grad = join(place, [after(part, down_new[0]) for part in in_parts])
    gains_grad = jnp.sum(key_grad[:, :, 2 * k_rows : 2 * k_rows + 2].astype(f32), axis=0).T
    gains_others = [swap(gains_grad, "tp", m) for m in over_tp[1:]]
    qkv_new = step_qkv(query_grad, after(key_grad, in_grad), qkv_weight, qkv_moment, qkv_average)
    gains_grad = gains_grad + sum(after(other, qkv_new[0]) for other in gains_others)
    gain_new = advance(norm_gains, gains_grad, gain_moment, gain_average, RATE_GAIN)
    return (block_out, in_grad, *qkv_new, *out_new, *gain_new, *in_new, *down_new)


def solution(mesh):
    return jax.shard_map(
        per_device,
        mesh=mesh,
        in_specs=(
            P(("fsdp", "ctx"), None),
            P(("fsdp", "ctx"), None),
            P("fsdp", None),
            P(("fsdp", "ctx"), None),
            P(("fsdp", "ctx"), None),
            P(("fsdp", "ctx"), "tp"),
            P("tp", ("fsdp", "ctx")),
            P(None, ("fsdp", "ctx")),
            P(("fsdp", "ctx"), None, None, "tp"),
            P(("fsdp", "ctx"), "tp", None),
            P(("fsdp", "ctx"), "tp"),
            P(("fsdp", "ctx"), "tp"),
            P("tp", ("fsdp", "ctx")),
            P("tp", ("fsdp", "ctx")),
            P(None, ("fsdp", "ctx")),
            P(None, ("fsdp", "ctx")),
            P(("fsdp", "ctx"), None, None, "tp"),
            P(("fsdp", "ctx"), None, None, "tp"),
            P(("fsdp", "ctx"), "tp", None),
            P(("fsdp", "ctx"), "tp", None),
        ),
        out_specs=(
            P(("fsdp", "ctx"), None),
            P(("fsdp", "ctx"), None),
            P(("fsdp", "ctx"), "tp"),
            P(("fsdp", "ctx"), "tp"),
            P(("fsdp", "ctx"), "tp"),
            P("tp", ("fsdp", "ctx")),
            P("tp", ("fsdp", "ctx")),
            P("tp", ("fsdp", "ctx")),
            P(None, ("fsdp", "ctx")),
            P(None, ("fsdp", "ctx")),
            P(None, ("fsdp", "ctx")),
            P(("fsdp", "ctx"), None, None, "tp"),
            P(("fsdp", "ctx"), None, None, "tp"),
            P(("fsdp", "ctx"), None, None, "tp"),
            P(("fsdp", "ctx"), "tp", None),
            P(("fsdp", "ctx"), "tp", None),
            P(("fsdp", "ctx"), "tp", None),
        ),
        check_vma=False,
    )
```

```python
import functools
import math

import jax
import jax.numpy as jnp
from jax import lax
from jax.experimental import pallas as pl
from jax.experimental.pallas import tpu as pltpu
from jax.sharding import PartitionSpec as P

HD = 64
GROUP = 3


EPSILON = 1e-05
ROPE_BASE = 10000.0
MOMENTUM = 0.9
AVERAGE = 0.7
RATE_QKV = 7e-05
RATE_OUT = 0.15
RATE_GAIN = 0.0005
RATE_IN = 0.0004
RATE_DOWN = 0.001


def doc_positions(lengths_row, places):
    doc_ends = jnp.cumsum(lengths_row)
    passed = places[:, None] >= doc_ends[None, :]
    segment = jnp.sum(passed.astype(jnp.int32), axis=1)
    doc_start = jnp.sum(jnp.where(passed, lengths_row[None, :], 0), axis=1)
    return (segment, places - doc_start)


def norm_back(grad_out, normed, inverse, gain_row):
    scaled = grad_out * gain_row
    return inverse * (scaled - normed * jnp.mean(scaled * normed, axis=-1, keepdims=True))


F_MASKS = (0, 2, 1, 3)
VMEM_LIMIT = 60 * 1024 * 1024


def advance(weight, gradient, moment, average, step_rate):
    moment_new = MOMENTUM * moment + gradient
    weight_new = weight - step_rate * (gradient + MOMENTUM * moment_new)
    average_new = AVERAGE * average + (1.0 - AVERAGE) * weight_new
    return (moment_new, average_new, weight_new)


def swap(value, axis, mask):
    size = lax.axis_size(axis)
    return lax.ppermute(value, axis, [(i, i ^ mask) for i in range(size)])


def after(value, *others):
    return lax.optimization_barrier((value, *others))[0]


def nt_dot(left_mat, right_mat):
    return lax.dot_general(
        left_mat, right_mat, (((1,), (1,)), ((), ())), preferred_element_type=jnp.float32
    )


def vmem_spec():
    return pl.BlockSpec(memory_space=pltpu.VMEM)


def any_spec():
    return pl.BlockSpec(memory_space=pl.ANY)


def smem_spec():
    return pl.BlockSpec(memory_space=pltpu.SMEM)


def added(left_mat, right_mat):
    return (left_mat.astype(jnp.float32) + right_mat.astype(jnp.float32)).astype(jnp.bfloat16)


def params():
    return pltpu.CompilerParams(vmem_limit_bytes=VMEM_LIMIT)


def cost(flops, mib):
    return pl.CostEstimate(flops=1, bytes_accessed=1, transcendentals=0)


def spread(blocks):
    return lax.all_to_all(blocks, "ctx", split_axis=0, concat_axis=0, tiled=True)


def gather_along_ctx(own):
    return spread(jnp.broadcast_to(own[None], (lax.axis_size("ctx"), *own.shape)))


def load_shards(place_ref, shard_refs, whole, sems, first=0):
    cols = slice(first, first + whole.shape[1])
    rows = shard_refs[0].shape[0]
    copies = []
    for i, shard in enumerate(shard_refs):
        at = pl.multiple_of((place_ref[0] ^ F_MASKS[i]) * rows, rows)
        copies.append(pltpu.make_async_copy(shard.at[:, cols], whole.at[pl.ds(at, rows)], sems.at[i]))
    return copies


def turn(first, second, cosine, sine):
    return first * cosine - second * sine, second * cosine + first * sine


def key_shard_kernel(qkv, gains, out, wide, square):
    rows, columns = qkv.shape
    kv = columns // ((GROUP + 2) * HD)
    for h in range(kv):
        at = h * (GROUP + 2) * HD + GROUP * HD
        wide[:, h * HD : (h + 1) * HD] = qkv[:, at : at + HD]
        wide[:, (kv + h) * HD : (kv + h + 1) * HD] = qkv[:, at + HD : at + 2 * HD]
    square[...] = jnp.zeros_like(square)
    square[: gains.shape[0], :rows] = gains[...]
    wide[:, 2 * kv * HD :] = square[...].T[:rows]
    low = wide[...].astype(jnp.bfloat16)
    for i in range(out.shape[0]):
        out[i] = low


def both_shard_kernel(qkv, weight, out, wide, tall):
    rows, columns = qkv.shape
    kv = columns // ((GROUP + 2) * HD)
    group = GROUP * HD
    for h in range(kv):
        at = h * (GROUP + 2) * HD
        wide[:, h * group : (h + 1) * group] = qkv[:, at : at + group]
    tall[...] = jnp.zeros_like(tall)
    tall[:, :rows] = weight[...]
    wide[:, kv * group :] = tall[...].T[:rows]
    low = wide[...].astype(jnp.bfloat16)
    for i in range(out.shape[0]):
        out[i] = low


def shard_copies(qkv, other, keys):
    rows, columns = qkv.shape
    kv = columns // ((GROUP + 2) * HD)
    wide = 2 * kv * HD + 128 if keys else 2 * GROUP * kv * HD
    padded = pltpu.VMEM((128, 128) if keys else (other.shape[0], 128), jnp.float32)
    return pl.pallas_call(
        key_shard_kernel if keys else both_shard_kernel,
        out_shape=jax.ShapeDtypeStruct((lax.axis_size("ctx"), rows, wide), jnp.bfloat16),
        in_specs=[vmem_spec()] * 2,
        out_specs=vmem_spec(),
        scratch_shapes=[pltpu.VMEM((rows, wide), jnp.float32), padded],
        compiler_params=params(),
        cost_estimate=cost(1, 1),
        name="key_shard" if keys else "both_shard",
    )(qkv, other)


def row_copies_kernel(experts, place, og, routes, gates, out):
    copies, rows, columns = out.shape
    width = columns - 128
    at = pl.ds(pl.multiple_of(place[2] * rows, rows), rows)
    lane = lax.broadcasted_iota(jnp.int32, (rows, 128), 1)
    high = jnp.zeros((rows, 128), jnp.float32)
    rest = jnp.zeros((rows, 128), jnp.float32)
    chosen, weights = routes[at], gates[at]
    for k in range(routes.shape[1]):
        weight = weights[:, k : k + 1]
        top = weight.astype(jnp.bfloat16).astype(jnp.float32)
        high += jnp.where(lane == chosen[:, k : k + 1], top, 0.0)
        rest += jnp.where(lane == chosen[:, k : k + 1] + experts, weight - top, 0.0)
    beside = (high + rest).astype(jnp.bfloat16)
    own = og[at]
    for i in range(copies):
        out[i, :, :width] = own
        out[i, :, width:] = beside


def row_copies(place, out_grad, routes, gate_weights, rows, experts):
    width = out_grad.shape[1]
    return pl.pallas_call(
        functools.partial(row_copies_kernel, experts),
        out_shape=jax.ShapeDtypeStruct((lax.axis_size("ctx"), rows, width + 128), jnp.bfloat16),
        in_specs=[smem_spec()] + [vmem_spec()] * 3,
        out_specs=vmem_spec(),
        compiler_params=params(),
        cost_estimate=cost(1, 1),
        name="row_copies",
    )(place, out_grad, routes, gate_weights)


def join_kernel(place, *refs):
    parts, out = refs[:-1], refs[-1]
    rows = parts[0].shape[0]
    for m, part in enumerate(parts):
        out[pl.ds(pl.multiple_of((place[2] ^ m) * rows, rows), rows)] = part[...]


def join(place, parts):
    rows, width = parts[0].shape
    return pl.pallas_call(
        join_kernel,
        out_shape=jax.ShapeDtypeStruct((len(parts) * rows, width), parts[0].dtype),
        in_specs=[smem_spec()] + [vmem_spec()] * len(parts),
        out_specs=vmem_spec(),
        compiler_params=params(),
        cost_estimate=cost(1, 1),
        name="join",
    )(place, *parts)


def project_keys_kernel(k_rows, *refs):
    place, tok, cos_ref, sin_ref = refs[:4]
    shard_refs, refs = refs[4 : 4 + len(F_MASKS)], refs[4 + len(F_MASKS) :]
    copies_ref, norm_ref, norm_t, whole, gain_ref, kv_ref, sems = refs
    copies = load_shards(place, shard_refs, whole, sems)
    for copy in copies:
        copy.start()
    x = tok[...].astype(jnp.float32)
    hat = x * lax.rsqrt(jnp.mean(x * x, axis=-1, keepdims=True) + EPSILON)
    for copy in copies:
        copy.wait()
    gains = whole[:, 2 * k_rows :].astype(jnp.float32).T
    gain_ref[...] = gains[:8]
    normed = (hat * gains[:1]).astype(jnp.bfloat16)
    norm_ref[...] = normed
    norm_t[...] = normed.T
    cosine, sine = cos_ref[...], sin_ref[...]
    half = HD // 2
    heads = jnp.dot(normed, whole[:, : 2 * k_rows], preferred_element_type=jnp.float32).T
    for at in range(0, k_rows, HD):
        a, b = turn(heads[at : at + half], heads[at + half : at + HD], cosine, sine)
        kv_ref[at : at + half] = a.astype(jnp.bfloat16)
        kv_ref[at + half : at + HD] = b.astype(jnp.bfloat16)
    kv_ref[k_rows:] = heads[k_rows:].astype(jnp.bfloat16)
    for i in range(copies_ref.shape[0]):
        copies_ref[i] = kv_ref[...]


def project_keys(place, tokens, cosine, sine, shards, k_rows):
    rows, width = tokens.shape
    low = jnp.bfloat16
    columns = shards[0].shape[1]
    return pl.pallas_call(
        functools.partial(project_keys_kernel, k_rows),
        out_shape=[
            jax.ShapeDtypeStruct((lax.axis_size("ctx"), 2 * k_rows, rows), low),
            jax.ShapeDtypeStruct((rows, width), low),
            jax.ShapeDtypeStruct((width, rows), low),
            jax.ShapeDtypeStruct((width, columns), low),
            jax.ShapeDtypeStruct((8, width), jnp.float32),
        ],
        in_specs=[smem_spec()] + [vmem_spec()] * 3 + [any_spec()] * len(shards),
        out_specs=[vmem_spec()] * 5,
        scratch_shapes=[
            pltpu.VMEM((2 * k_rows, rows), low),
            pltpu.SemaphoreType.DMA((len(shards),)),
        ],
        compiler_params=params(),
        cost_estimate=cost(2 * rows * width * columns, 8),
        name="project_keys",
    )(place, tokens, cosine, sine, *shards)


def project_queries_kernel(*refs):
    place, norm_ref, cos_ref, sin_ref = refs[:4]
    shard_refs, refs = refs[4 : 4 + len(F_MASKS)], refs[4 + len(F_MASKS) :]
    q_ref, whole, sems = refs
    copies = load_shards(place, shard_refs, whole, sems)
    for copy in copies:
        copy.start()
    for copy in copies:
        copy.wait()
    cosine, sine = cos_ref[...], sin_ref[...]
    half = HD // 2
    heads = jnp.dot(norm_ref[...], whole[...], preferred_element_type=jnp.float32).T
    scale = jnp.bfloat16(HD**-0.5)
    for at in range(0, q_ref.shape[0], HD):
        a, b = turn(heads[at : at + half], heads[at + half : at + HD], cosine, sine)
        q_ref[at : at + half] = a.astype(jnp.bfloat16) * scale
        q_ref[at + half : at + HD] = b.astype(jnp.bfloat16) * scale


def project_queries(place, normed, cosine, sine, shards):
    rows, width = normed.shape
    low = jnp.bfloat16
    columns = shards[0].shape[1] // 2
    return pl.pallas_call(
        project_queries_kernel,
        out_shape=[
            jax.ShapeDtypeStruct((columns, rows), low),
            jax.ShapeDtypeStruct((width, columns), low),
        ],
        in_specs=[smem_spec()] + [vmem_spec()] * 3 + [any_spec()] * len(shards),
        out_specs=[vmem_spec()] * 2,
        scratch_shapes=[pltpu.SemaphoreType.DMA((len(shards),))],
        compiler_params=params(),
        cost_estimate=cost(1, 1),
        name="project_queries",
    )(place, normed, cosine, sine, *shards)


def share_out(place, part, own_ref, other_refs):
    rows = own_ref.shape[0]
    for m, out in enumerate((own_ref, *other_refs)):
        at = pl.multiple_of((place[2] ^ m) * rows, rows)
        out[...] = part[pl.ds(at, rows)].astype(out.dtype)


def attend_kernel(n_ctx, *refs):
    place, start_ref, q_ref, piece_ref = refs[:4]
    refs = refs[4:]
    shard_refs, refs = refs[: len(F_MASKS)], refs[len(F_MASKS) :]
    p_ref, head_ref, kv_all, out_t, own_ref = refs[:5]
    other_refs, (bias, scores, q3, part, sems) = refs[5:-5], refs[-5:]
    rows = q_ref.shape[1]
    half_kv = kv_all.shape[0] // 2
    step = pl.program_id(0)
    copies = load_shards(place, shard_refs, out_t, sems, out_t.shape[1])

    @pl.when(step == 0)
    def _():
        for copy in copies:
            copy.start()
        key_at = lax.broadcasted_iota(jnp.int32, (rows, rows), 0)
        query_at = lax.broadcasted_iota(jnp.int32, (rows, rows), 1)
        for j in range(n_ctx):
            kv_all[:, j * rows : (j + 1) * rows] = piece_ref[j]
            allowed = key_at + j * rows >= start_ref[...]
            allowed = allowed & (key_at + j * rows <= query_at + place[1] * rows)
            bias[j * rows : (j + 1) * rows] = jnp.where(allowed, 0.0, -1e30)

    for h in range(GROUP):
        q3[:, h * rows : (h + 1) * rows] = q_ref[h * HD : (h + 1) * HD]
    keys = kv_all[pl.ds(pl.multiple_of(step * HD, HD), HD)]
    values = kv_all[pl.ds(pl.multiple_of(half_kv + step * HD, HD), HD)]
    scores[...] = jnp.dot(keys.T, q3[...], preferred_element_type=jnp.float32)
    for h in range(GROUP):
        cols = slice(h * rows, (h + 1) * rows)
        masked = scores[:, cols] + bias[...]
        exponent = jnp.exp(masked - jnp.max(masked, axis=0, keepdims=True))
        inverse = 1.0 / jnp.sum(exponent, axis=0, keepdims=True)
        p_ref[0, :, cols] = (exponent * inverse).astype(jnp.bfloat16)
    attended = jnp.dot(values, p_ref[0], preferred_element_type=jnp.float32).astype(jnp.bfloat16)
    for h in range(GROUP):
        at = pl.multiple_of((step * GROUP + h) * HD, HD)
        head_ref[pl.ds(at, HD)] = attended[:, h * rows : (h + 1) * rows]

    @pl.when(step == pl.num_programs(0) - 1)
    def _():
        for copy in copies:
            copy.wait()
        part[...] = nt_dot(head_ref[...].T, out_t[...])
        share_out(place, part, own_ref, other_refs)


def attend(place, starts, q_t, pieces, shards):
    n_ctx, n_tp = lax.axis_size("ctx"), lax.axis_size("tp")
    q_rows, rows = q_t.shape
    kv = q_rows // (GROUP * HD)
    width = shards[0].shape[0] * len(shards)
    seq = rows * n_ctx
    low = jnp.bfloat16
    return pl.pallas_call(
        functools.partial(attend_kernel, n_ctx),
        grid=(kv,),
        out_shape=[
            jax.ShapeDtypeStruct((kv, seq, GROUP * rows), low),
            jax.ShapeDtypeStruct((q_rows, rows), low),
            jax.ShapeDtypeStruct((2 * kv * HD, seq), low),
            jax.ShapeDtypeStruct((width, q_rows), low),
            jax.ShapeDtypeStruct((rows // n_tp, width), jnp.float32),
        ]
        + [jax.ShapeDtypeStruct((rows // n_tp, width), low)] * (n_tp - 1),
        in_specs=[smem_spec(), vmem_spec(), pl.BlockSpec((GROUP * HD, rows), lambda i: (i, 0))]
        + [vmem_spec()]
        + [any_spec()] * len(shards),
        out_specs=[pl.BlockSpec((1, seq, GROUP * rows), lambda i: (i, 0, 0))] + [vmem_spec()] * (3 + n_tp),
        scratch_shapes=[
            pltpu.VMEM((seq, rows), jnp.float32),
            pltpu.VMEM((seq, GROUP * rows), jnp.float32),
            pltpu.VMEM((HD, GROUP * rows), low),
            pltpu.VMEM((rows, width), jnp.float32),
            pltpu.SemaphoreType.DMA((len(shards),)),
        ],
        compiler_params=pltpu.CompilerParams(vmem_limit_bytes=VMEM_LIMIT),
        cost_estimate=pl.CostEstimate(
            flops=2 * q_rows * rows * (2 * seq + width), bytes_accessed=20 << 20, transcendentals=0
        ),
        name="attend",
    )(place, starts, q_t, pieces, *shards)


def attend_back_kernel(n_ctx, *refs):
    place, p_ref, q_ref, kv_all, out_t, cos_ref, sin_ref = refs[:7]
    grad_refs, (dq_ref, piece_ref, grad_all, grads, q3, g3) = refs[7:-6], refs[-6:]
    rows = q_ref.shape[1]
    half_kv = kv_all.shape[0] // 2
    step = pl.program_id(0)

    @pl.when(step == 0)
    def _():
        join_kernel(place, *grad_refs, grad_all)
        back = jnp.dot(grad_all[...], out_t[...], preferred_element_type=jnp.float32)
        grads[...] = back.astype(jnp.bfloat16).T

    for h in range(GROUP):
        cols = slice(h * rows, (h + 1) * rows)
        q3[:, cols] = q_ref[h * HD : (h + 1) * HD]
        g3[:, cols] = grads[pl.ds(pl.multiple_of((step * GROUP + h) * HD, HD), HD)]
    keys = kv_all[pl.ds(pl.multiple_of(step * HD, HD), HD)]
    values = kv_all[pl.ds(pl.multiple_of(half_kv + step * HD, HD), HD)]
    probs = p_ref[0].astype(jnp.float32)
    grad_probs = jnp.dot(values.T, g3[...], preferred_element_type=jnp.float32)
    inner = jnp.sum(probs * grad_probs, axis=0, keepdims=True)
    grad_scores = (probs * (grad_probs - inner)).astype(jnp.bfloat16)
    grad_query = jnp.dot(keys, grad_scores, preferred_element_type=jnp.float32) * HD**-0.5
    grad_key = nt_dot(grad_scores, q3[...]).T
    grad_value = nt_dot(p_ref[0], g3[...]).T
    half = HD // 2
    cosine, sine = cos_ref[...], -sin_ref[...]
    for h in range(GROUP):
        cols = slice(h * rows, (h + 1) * rows)
        a, b = turn(grad_query[:half, cols], grad_query[half:, cols], cosine, sine)
        dq_ref[h * HD : h * HD + half] = a.astype(jnp.bfloat16)
        dq_ref[h * HD + half : (h + 1) * HD] = b.astype(jnp.bfloat16)
    key_at = pl.ds(pl.multiple_of(step * HD, HD), HD)
    value_at = pl.ds(pl.multiple_of(half_kv + step * HD, HD), HD)
    for j in range(n_ctx):
        cols = slice(j * rows, (j + 1) * rows)
        piece_ref[j, key_at] = grad_key[:, cols].astype(jnp.bfloat16)
        piece_ref[j, value_at] = grad_value[:, cols].astype(jnp.bfloat16)


def attend_back(place, probs, q_t, kv_all, grads, out_t, cosine, sine):
    n_ctx = lax.axis_size("ctx")
    q_rows, rows = q_t.shape
    kv, seq = probs.shape[:2]
    low = jnp.bfloat16
    block = pl.BlockSpec((GROUP * HD, rows), lambda i: (i, 0))
    return pl.pallas_call(
        functools.partial(attend_back_kernel, n_ctx),
        grid=(kv,),
        out_shape=[
            jax.ShapeDtypeStruct((q_rows, rows), low),
            jax.ShapeDtypeStruct((n_ctx, 2 * kv * HD, rows), low),
        ],
        in_specs=[smem_spec(), pl.BlockSpec((1, seq, GROUP * rows), lambda i: (i, 0, 0)), block]
        + [vmem_spec()] * (4 + len(grads)),
        out_specs=[block, vmem_spec()],
        scratch_shapes=[
            pltpu.VMEM((rows, out_t.shape[0]), low),
            pltpu.VMEM((q_rows, rows), low),
            pltpu.VMEM((HD, GROUP * rows), low),
            pltpu.VMEM((HD, GROUP * rows), low),
        ],
        compiler_params=pltpu.CompilerParams(vmem_limit_bytes=VMEM_LIMIT),
        cost_estimate=pl.CostEstimate(flops=1, bytes_accessed=90 << 20, transcendentals=0),
        name="attend_back",
    )(place, probs, q_t, kv_all, out_t, cosine, sine, *grads)


def store_products(place, left_t, right, out_refs):
    rows = out_refs[0].shape[0]
    for mask, out in zip(F_MASKS, out_refs):
        at = pl.multiple_of((place[0] ^ mask) * rows, rows)
        out[...] = jnp.dot(
            left_t[pl.ds(at, rows)], right, preferred_element_type=jnp.float32
        ).astype(jnp.bfloat16)


def query_grad_kernel(place, dq_ref, norm_t, whole, head_ref, *refs):
    grad_refs, (near, far, core, part_ref, grad_all, grad_t) = refs[:-6], refs[-6:]
    columns = whole.shape[1]
    back = dq_ref[...].T
    outs = [near, far, core.at[0], core.at[1]]
    store_products(place, norm_t, back, [out.at[:, :columns] for out in outs])
    join_kernel(place, *grad_refs, grad_all)
    grad_t[...] = grad_all[...].T
    store_products(place, grad_t, head_ref[...].T, [out.at[:, columns:] for out in outs])
    part_ref[...] = nt_dot(back, whole[...])


def row_parts(rows, columns):
    low = jnp.bfloat16
    return [
        jax.ShapeDtypeStruct((rows, columns), low),
        jax.ShapeDtypeStruct((rows, columns), low),
        jax.ShapeDtypeStruct((2, rows, columns), low),
    ]


def query_grads(place, dq_t, norm_t, whole, grads, head_t):
    q_rows, rows = dq_t.shape
    width = norm_t.shape[0]
    outs = pl.pallas_call(
        query_grad_kernel,
        out_shape=row_parts(width // len(F_MASKS), 2 * q_rows)
        + [jax.ShapeDtypeStruct((rows, width), jnp.float32)],
        in_specs=[smem_spec()] + [vmem_spec()] * (4 + len(grads)),
        out_specs=[vmem_spec()] * 4,
        scratch_shapes=[pltpu.VMEM((rows, width), jnp.bfloat16), pltpu.VMEM((width, rows), jnp.bfloat16)],
        compiler_params=params(),
        cost_estimate=cost(6 * rows * width * q_rows, 15),
        name="query_grads",
    )(place, dq_t, norm_t, whole, head_t, *grads)
    return outs[:3], outs[3]


def key_grad_kernel(n_ctx, *refs):
    place, piece_ref = refs[:2]
    refs = refs[2:]
    cos_ref, sin_ref, norm_t, whole, tok, query_part, gain_two_ref = refs[:7]
    near, far, core, own_ref = refs[7:11]
    other_refs, (part_ref, back_t, right) = refs[11:-3], refs[-3:]
    kv_rows, rows = piece_ref.shape[1:]
    total = piece_ref[0].astype(jnp.float32)
    for j in range(1, n_ctx):
        total += piece_ref[j].astype(jnp.float32)
    cosine, sine = cos_ref[...], -sin_ref[...]
    half = HD // 2
    for at in range(0, kv_rows // 2, HD):
        a, b = turn(total[at : at + half], total[at + half : at + HD], cosine, sine)
        back_t[at : at + half] = a.astype(jnp.bfloat16)
        back_t[at + half : at + HD] = b.astype(jnp.bfloat16)
    back_t[kv_rows // 2 :] = total[kv_rows // 2 :].astype(jnp.bfloat16)
    back = back_t[...].T
    part = query_part[...] + nt_dot(back, whole[:, :kv_rows])
    part_ref[...] = part
    share_out(place, part_ref, own_ref, other_refs)
    outs = [near, far, core.at[0], core.at[1]]
    store_products(place, norm_t, back, [out.at[:, :kv_rows] for out in outs])
    x = tok[...].astype(jnp.float32)
    hat = x * lax.rsqrt(jnp.mean(x * x, axis=-1, keepdims=True) + EPSILON)
    gain_one = jnp.sum(part * hat, axis=0, keepdims=True)
    row = lax.broadcasted_iota(jnp.int32, (128, x.shape[1]), 0)
    columns = jnp.where(row == 0, gain_one, jnp.where(row == 1, gain_two_ref[...], 0.0))
    right[...] = columns.T
    count = near.shape[0]
    for mask, out in zip(F_MASKS, outs):
        at = pl.multiple_of((place[0] ^ mask) * count, count)
        out[:, kv_rows:] = right[pl.ds(at, count)].astype(jnp.bfloat16)


def key_grads(place, pieces, cosine, sine, norm_t, whole, tokens, query_part, gain_two):
    n_ctx, n_tp = lax.axis_size("ctx"), lax.axis_size("tp")
    kv_rows, rows = pieces.shape[1:]
    width = norm_t.shape[0]
    outs = pl.pallas_call(
        functools.partial(key_grad_kernel, n_ctx),
        out_shape=row_parts(width // len(F_MASKS), kv_rows + 128)
        + [jax.ShapeDtypeStruct((rows // n_tp, width), jnp.float32)]
        + [jax.ShapeDtypeStruct((rows // n_tp, width), jnp.bfloat16)] * (n_tp - 1),
        in_specs=[smem_spec()] + [vmem_spec()] * 8,
        out_specs=[vmem_spec()] * (3 + n_tp),
        scratch_shapes=[
            pltpu.VMEM((rows, width), jnp.float32),
            pltpu.VMEM((kv_rows, rows), jnp.bfloat16),
            pltpu.VMEM((width, 128), jnp.float32),
        ],
        compiler_params=params(),
        cost_estimate=cost(4 * rows * width * kv_rows, 12),
        name="key_grads",
    )(place, pieces, cosine, sine, norm_t, whole, tokens, query_part, gain_two)
    return outs[:3], outs[3:]


def sum_cores(parts, *before):
    near, far, core = parts
    core = after(swap(core, "fsdp", 1), *before)
    return added(near, core[0]), added(far, core[1])


def scatter_rows(near):
    n_ctx = lax.axis_size("ctx")
    return spread(near.reshape(n_ctx, near.shape[0] // n_ctx, near.shape[1]))


def table(count):
    near = [((m, 0), (m, 1)) for m in range(count)]
    far = [((count, 0), (count, 1))]
    far += [((count + m, 0), (2 * count - 1 + m, 0)) for m in range(1, count)]
    return [near, far] + [
        [tuple((array + 3 * count - 1, at) for array, at in piece) for piece in pieces] for pieces in (near, far)
    ]


def load_experts(refs, target, sems, kinds):
    half, hidden = refs[0].shape[2:]
    copies = []
    for expert, pieces in enumerate(table((len(refs) + 2) // 6)):
        for m, piece in enumerate(pieces):
            for at, kind in enumerate(kinds):
                for j, (array, index) in enumerate(piece):
                    copies.append(
                        pltpu.make_async_copy(
                            refs[array].at[index, kind],
                            target.at[at, expert, j * half : (j + 1) * half, m * hidden : (m + 1) * hidden],
                            sems.at[expert, (m * len(kinds) + at) * 2 + j],
                        )
                    )
    return copies


def weight_scratch(weights, kinds):
    count = (len(weights) + 2) // 6
    half, hidden = weights[0].shape[2:]
    return [
        pltpu.VMEM((kinds, len(F_MASKS), 2 * half, count * hidden), jnp.bfloat16),
        pltpu.SemaphoreType.DMA((len(F_MASKS), 2 * kinds * count)),
    ]


def back_kernel(og_ref, *refs):
    weight_refs, (back_ref, og_all, weights, sems) = refs[:-4], refs[-4:]
    copies = load_experts(weight_refs, weights, sems, (2,))
    for copy in copies:
        copy.start()
    blocks, rows, _ = og_ref.shape
    width = og_all.shape[1]
    for b in range(blocks):
        og_all[b * rows : (b + 1) * rows] = og_ref[b, :, :width]
    hidden = weights.shape[3]
    each = len(copies) // len(F_MASKS)
    for expert in range(len(F_MASKS)):
        for copy in copies[expert * each : (expert + 1) * each]:
            copy.wait()
        back = jnp.dot(og_all[...], weights[0, expert], preferred_element_type=jnp.float32)
        for b in range(blocks):
            back_ref[b, :, expert * hidden : (expert + 1) * hidden] = back[b * rows : (b + 1) * rows].astype(
                jnp.bfloat16
            )


def back_rows(og, weights, width):
    blocks, rows, _ = og.shape
    scratch = weight_scratch(weights, 1)
    hidden = scratch[0].shape[3] * len(F_MASKS)
    return pl.pallas_call(
        back_kernel,
        out_shape=jax.ShapeDtypeStruct((blocks, rows, hidden), jnp.bfloat16),
        in_specs=[vmem_spec()] + [any_spec()] * len(weights),
        out_specs=vmem_spec(),
        scratch_shapes=[pltpu.VMEM((blocks * rows, width), jnp.bfloat16)] + scratch,
        compiler_params=params(),
        cost_estimate=cost(2 * blocks * rows * width * hidden, 12),
        name="back_rows",
    )(og, *weights)


def expert_kernel(masks, experts, *refs):
    blocks = len(masks)
    place, refs = refs[0], refs[1:]
    x_refs, refs = refs[:blocks], refs[blocks:]
    gate_ref, back_ref, refs = refs[0], refs[1], refs[2:]
    weight_refs, refs = refs[: -8 - blocks], refs[-8 - blocks :]
    gx_refs, refs = refs[:blocks], refs[blocks:]
    act_ref, gg_ref, gu_ref, x_all, gates, total, weights, sems = refs
    copies = load_experts(weight_refs, weights, sems, (0, 1))
    for copy in copies:
        copy.start()
    rows = x_refs[0].shape[0]
    for b, mask in enumerate(masks):
        x_all[b * rows : (b + 1) * rows] = x_refs[b][...]
        gates[b * rows : (b + 1) * rows] = gate_ref[place[1] ^ mask].astype(jnp.float32)
    hidden = weights.shape[3]
    each = len(copies) // len(F_MASKS)
    lane = lax.broadcasted_iota(jnp.int32, gates.shape, 1)
    x = x_all[...]
    for i, mask in enumerate(F_MASKS):
        for copy in copies[i * each : (i + 1) * each]:
            copy.wait()
        expert = (place[0] ^ mask) * (experts // len(F_MASKS)) + place[1]
        chosen = (lane == expert) | (lane == expert + experts)
        weight = jnp.sum(jnp.where(chosen, gates[...], 0.0), axis=1, keepdims=True)
        gate = jnp.dot(x, weights[0, i], preferred_element_type=jnp.float32)
        up = jnp.dot(x, weights[1, i], preferred_element_type=jnp.float32)
        cols = slice(i * hidden, (i + 1) * hidden)
        back = jnp.concatenate([back_ref[place[1] ^ m, :, cols] for m in masks]).astype(jnp.float32) * weight
        sig = jax.nn.sigmoid(gate)
        silu = gate * sig
        act_ref[:, cols] = (silu * up * weight).astype(jnp.bfloat16)
        grad_gate = (back * up * (sig * (1.0 + gate * (1.0 - sig)))).astype(jnp.bfloat16)
        grad_up = (back * silu).astype(jnp.bfloat16)
        gg_ref[:, cols] = grad_gate
        gu_ref[:, cols] = grad_up
        more = nt_dot(grad_gate, weights[0, i]) + nt_dot(grad_up, weights[1, i])
        if i == 0:
            total[...] = more
        else:
            total[...] += more
    for b in range(blocks):
        gx_refs[b][...] = total[b * rows : (b + 1) * rows].astype(jnp.bfloat16)


def expert_rows(place, masks, xs, og, backs, weights, experts):
    blocks, (rows, width) = len(xs), xs[0].shape
    n_ctx = og.shape[0]
    low = jnp.bfloat16
    scratch = weight_scratch(weights, 2)
    hidden = scratch[0].shape[3] * len(F_MASKS)
    wide = jax.ShapeDtypeStruct((blocks * rows, hidden), low)
    outs = pl.pallas_call(
        functools.partial(expert_kernel, masks, experts),
        grid=(1,),
        out_shape=[jax.ShapeDtypeStruct((rows, width), low)] * blocks + [wide] * 3,
        in_specs=[smem_spec()]
        + [vmem_spec()] * blocks
        + [pl.BlockSpec((n_ctx, rows, 128), lambda i: (0, 0, width // 128)), vmem_spec()]
        + [any_spec()] * len(weights),
        out_specs=[vmem_spec()] * (blocks + 3),
        scratch_shapes=[
            pltpu.VMEM((blocks * rows, width), low),
            pltpu.VMEM((blocks * rows, 128), jnp.float32),
            pltpu.VMEM((blocks * rows, width), jnp.float32),
        ]
        + scratch,
        compiler_params=params(),
        cost_estimate=cost(8 * blocks * rows * width * hidden, 20),
        name="expert_rows",
    )(place, *xs, og, backs, *weights)
    return outs[:blocks], outs[blocks:]


def mix_kernel(calls, place, *refs):
    act_refs, refs = refs[:calls], refs[calls:]
    weight_refs, (mix_ref, total, weights, sems) = refs[:-4], refs[-4:]
    copies = load_experts(weight_refs, weights, sems, (2,))
    for copy in copies:
        copy.start()
    hidden = weights.shape[3]
    some = act_refs[0].shape[0]
    each = len(copies) // len(F_MASKS)
    for i in range(len(F_MASKS)):
        for copy in copies[i * each : (i + 1) * each]:
            copy.wait()
        for j in range(calls):
            more = nt_dot(act_refs[j][:, i * hidden : (i + 1) * hidden], weights[0, i])
            if i == 0:
                total[j * some : (j + 1) * some] = more
            else:
                total[j * some : (j + 1) * some] += more
    blocks, rows, _ = mix_ref.shape
    for b in range(blocks):
        mix_ref[place[1] ^ b] = total[b * rows : (b + 1) * rows].astype(jnp.bfloat16)


def mix_rows(place, acts, weights, blocks, width):
    calls, (some, hidden) = len(acts), acts[0].shape
    rows = some * calls // blocks
    return pl.pallas_call(
        functools.partial(mix_kernel, calls),
        out_shape=jax.ShapeDtypeStruct((blocks, rows, width), jnp.bfloat16),
        in_specs=[smem_spec()] + [vmem_spec()] * calls + [any_spec()] * len(weights),
        out_specs=vmem_spec(),
        scratch_shapes=[pltpu.VMEM((some * calls, width), jnp.float32)] + weight_scratch(weights, 1),
        compiler_params=params(),
        cost_estimate=cost(2 * blocks * rows * width * hidden, 12),
        name="mix_rows",
    )(place, *acts, *weights)


def weight_kernel(blocks, calls, count, *refs):
    place, og_ref, refs = refs[0], refs[1], refs[2:]
    x_refs, refs = refs[:blocks], refs[blocks:]
    act_refs, refs = refs[:calls], refs[calls:]
    gg_refs, refs = refs[:calls], refs[calls:]
    gu_refs, refs = refs[:calls], refs[calls:]
    leave, stay, x_t, og_t, right = refs
    rows, width = x_refs[0].shape
    step = pl.program_id(0)

    @pl.when(step == 0)
    def _():
        for b in range(blocks):
            x_t[:, b * rows : (b + 1) * rows] = x_refs[b][...].T
            og_t[:, b * rows : (b + 1) * rows] = og_ref[place[1] ^ b, :, :width].T

    some = act_refs[0].shape[0]
    half = width // 2
    hidden = right.shape[1] // count
    for kind, (left, parts) in enumerate(((x_t, gg_refs), (x_t, gu_refs), (og_t, act_refs))):
        for i in range(calls):
            right[i * some : (i + 1) * some] = parts[i][...]
        for j in range(2):
            product = jnp.dot(
                left[j * half : (j + 1) * half], right[...], preferred_element_type=jnp.float32
            ).astype(jnp.bfloat16)
            for m in range(count):
                piece = product[:, m * hidden : (m + 1) * hidden]
                if j == 0 and m == 0:
                    stay[step, kind] = piece
                elif j == 0:
                    leave[2 * (m - 1) + step, kind] = piece
                else:

                    @pl.when(step == 0)
                    def _(m=m, kind=kind, piece=piece):
                        stay[2 + m, kind] = piece

                    @pl.when(step == 1)
                    def _(m=m, kind=kind, piece=piece):
                        leave[2 * (count - 1) + m, kind] = piece


def weight_grads(place, xs, og, acts, ggs, gus, count, first):
    blocks, calls, (rows, width) = len(xs), len(acts), xs[0].shape
    some, wide = acts[0].shape
    whole = wide // len(F_MASKS)
    hidden, half = whole // count, width // 2
    column = pl.BlockSpec((some, whole), lambda i: (0, first + i))
    low = jnp.bfloat16
    total = blocks * rows
    outs = [(3 * count - 2, 3, half, hidden), (count + 2, 3, half, hidden)]
    return pl.pallas_call(
        functools.partial(weight_kernel, blocks, calls, count),
        grid=(2,),
        out_shape=[jax.ShapeDtypeStruct(shape, low) for shape in outs],
        in_specs=[smem_spec()] + [vmem_spec()] * (blocks + 1) + [column] * (3 * calls),
        out_specs=[pl.BlockSpec(shape, lambda i: (0, 0, 0, 0)) for shape in outs],
        scratch_shapes=[
            pltpu.VMEM((width, total), low),
            pltpu.VMEM((width, total), low),
            pltpu.VMEM((total, whole), low),
        ],
        compiler_params=params(),
        cost_estimate=cost(2 * 3 * total * width * 2 * whole, 20),
        name="weight_grads",
    )(place, og, *xs, *acts, *ggs, *gus)


def total_of(*parts):
    return sum(part.astype(jnp.float32) for part in parts).astype(jnp.bfloat16)


def pair_kernel(own, core, out):
    out[...] = (own[...].astype(jnp.float32) + core[...].astype(jnp.float32)).astype(jnp.bfloat16)


def pair_sum(own, core, first, count):
    block = (1, *own.shape[1:])
    part = pl.BlockSpec(block, lambda i: (first + i, 0, 0, 0))
    return pl.pallas_call(
        pair_kernel,
        grid=(count,),
        out_shape=jax.ShapeDtypeStruct((count, *own.shape[1:]), own.dtype),
        in_specs=[part] * 2,
        out_specs=pl.BlockSpec(block, lambda i: (i, 0, 0, 0)),
        compiler_params=params(),
        cost_estimate=cost(1, 1),
        name="pair_sum",
    )(own, core)


def step_in_kernel(uppers, lowers, *refs):
    up_refs, refs = refs[:uppers], refs[uppers:]
    low_refs, refs = refs[:lowers], refs[lowers:]
    weight, moment, average, moment_new, average_new, weight_new, grad = refs

    def gather(parts):
        total = parts[0][0, 0].astype(jnp.float32)
        for part in parts[1:]:
            total += part[0, 0].astype(jnp.float32)
        grad[...] = total

    @pl.when(pl.program_id(1) == 0)
    def _():
        gather(up_refs)

    @pl.when(pl.program_id(1) == 1)
    def _():
        gather(low_refs)

    new = advance(weight[0, 0], grad[...], moment[0, 0], average[0, 0], RATE_IN)
    moment_new[0, 0], average_new[0, 0], weight_new[0, 0] = new


def step_in(uppers, lowers, weight, moment, average):
    half, hidden = uppers[0][0].shape[2:]
    parts = uppers + lowers
    specs = [pl.BlockSpec((1, 1, half, hidden), lambda k, j, at=at: (at, k, 0, 0)) for _, at in parts]
    block = pl.BlockSpec((1, 1, half, hidden), lambda k, j: (0, k, j, 0))
    return pl.pallas_call(
        functools.partial(step_in_kernel, len(uppers), len(lowers)),
        grid=(2, 2),
        out_shape=[jax.ShapeDtypeStruct(weight.shape, jnp.float32)] * 3,
        in_specs=specs + [block] * 3,
        out_specs=[block] * 3,
        scratch_shapes=[pltpu.VMEM((half, hidden), jnp.float32)],
        compiler_params=params(),
        cost_estimate=cost(10 * weight.size, 22),
        name="step_in",
    )(*(part for part, _ in parts), weight, moment, average)


def step_down_kernel(uppers, lowers, *refs):
    up_refs, refs = refs[:uppers], refs[uppers:]
    low_refs, refs = refs[:lowers], refs[lowers:]
    weight, moment, average, moment_new, average_new, weight_new, grad = refs

    def gather(parts):
        total = parts[0][0, 0].astype(jnp.float32)
        for part in parts[1:]:
            total += part[0, 0].astype(jnp.float32)
        grad[...] = total.T

    @pl.when(pl.program_id(0) == 0)
    def _():
        gather(up_refs)

    @pl.when(pl.program_id(0) == 1)
    def _():
        gather(low_refs)

    new = advance(weight[0], grad[...], moment[0], average[0], RATE_DOWN)
    moment_new[0], average_new[0], weight_new[0] = new


def step_down(uppers, lowers, weight, moment, average):
    half, hidden = uppers[0][0].shape[2:]
    parts = uppers + lowers
    specs = [pl.BlockSpec((1, 1, half, hidden), lambda j, at=at: (at, 2, 0, 0)) for _, at in parts]
    block = pl.BlockSpec((1, hidden, half), lambda j: (0, 0, j))
    return pl.pallas_call(
        functools.partial(step_down_kernel, len(uppers), len(lowers)),
        grid=(2,),
        out_shape=[jax.ShapeDtypeStruct(weight.shape, jnp.float32)] * 3,
        in_specs=specs + [block] * 3,
        out_specs=[block] * 3,
        scratch_shapes=[pltpu.VMEM((hidden, half), jnp.float32)],
        compiler_params=params(),
        cost_estimate=cost(10 * weight.size, 12),
        name="step_down",
    )(*(part for part, _ in parts), weight, moment, average)


def sum_first(ref, cols):
    total = ref[0, :, cols].astype(jnp.float32)
    for i in range(1, ref.shape[0]):
        total += ref[i, :, cols].astype(jnp.float32)
    return total


def step_out_kernel(come, weight, moment, average, moment_new, average_new, weight_new, wide):
    rows = come.shape[1]
    wide[...] = jnp.zeros_like(wide)
    wide[:rows] = sum_first(come, slice(come.shape[2] // 2, come.shape[2]))
    new = advance(weight[...], wide[...].T[:, :rows], moment[...], average[...], RATE_OUT)
    moment_new[...], average_new[...], weight_new[...] = new


def step_out(come, weight, moment, average):
    return pl.pallas_call(
        step_out_kernel,
        out_shape=[jax.ShapeDtypeStruct(weight.shape, jnp.float32)] * 3,
        in_specs=[vmem_spec()] * 4,
        out_specs=[vmem_spec()] * 3,
        scratch_shapes=[pltpu.VMEM((128, weight.shape[0]), jnp.float32)],
        compiler_params=params(),
        cost_estimate=cost(1, 1),
        name="step_out",
    )(come, weight, moment, average)


def step_qkv_kernel(
    query_come, key_come, weight, moment, average, moment_new, average_new, weight_new, grad, wide
):
    kv = weight.shape[1] // ((GROUP + 2) * HD)
    group = GROUP * HD
    queries = sum_first(query_come, slice(0, kv * group))
    wide[...] = sum_first(key_come, slice(None))
    for h in range(kv):
        at = h * (GROUP + 2) * HD
        grad[:, at : at + group] = queries[:, h * group : (h + 1) * group]
        grad[:, at + group : at + group + HD] = wide[:, h * HD : (h + 1) * HD]
        grad[:, at + group + HD : at + group + 2 * HD] = wide[:, (kv + h) * HD : (kv + h + 1) * HD]
    new = advance(weight[...], grad[...], moment[...], average[...], RATE_QKV)
    moment_new[...], average_new[...], weight_new[...] = new


def step_qkv(query_come, key_come, weight, moment, average):
    return pl.pallas_call(
        step_qkv_kernel,
        out_shape=[jax.ShapeDtypeStruct(weight.shape, jnp.float32)] * 3,
        in_specs=[vmem_spec()] * 5,
        out_specs=[vmem_spec()] * 3,
        scratch_shapes=[
            pltpu.VMEM(weight.shape, jnp.float32),
            pltpu.VMEM(key_come.shape[1:], jnp.float32),
        ],
        compiler_params=params(),
        cost_estimate=cost(1, 1),
        name="step_qkv",
    )(query_come, key_come, weight, moment, average)


def per_device(
    tokens,
    out_grad,
    lengths,
    routes,
    gate_weights,
    qkv_weight,
    out_weight,
    norm_gains,
    expert_in,
    expert_down,
    qkv_moment,
    qkv_average,
    out_moment,
    out_average,
    gain_moment,
    gain_average,
    in_moment,
    in_average,
    down_moment,
    down_average,
):
    tok_rows, width = tokens.shape
    n_ctx, n_tp = lax.axis_size("ctx"), lax.axis_size("tp")
    experts = lax.axis_size(("fsdp", "ctx"))
    fsdp_index, ctx_index = lax.axis_index("fsdp"), lax.axis_index("ctx")
    tp_index = lax.axis_index("tp")
    place = jnp.stack([fsdp_index, ctx_index, tp_index]).astype(jnp.int32)
    low, f32 = jnp.bfloat16, jnp.float32
    half_rows = tok_rows // n_tp
    over_tp = range(n_tp)

    def part_of(value, mask):
        return lax.dynamic_slice_in_dim(value, (tp_index ^ mask) * half_rows, half_rows)

    def own_half(value):
        return part_of(value, 0)

    def sum_own(own, others):
        for m, other in enumerate(others, 1):
            own = own + swap(other, "tp", m).astype(f32)
        return own

    def to_others(own):
        return [own] + [swap(own, "tp", m) for m in over_tp[1:]]

    shard_rows, qkv_columns = qkv_weight.shape
    kv_local = qkv_columns // ((GROUP + 2) * HD)
    q_rows, k_rows = kv_local * GROUP * HD, kv_local * HD
    key_near = spread(shard_copies(qkv_weight, norm_gains, True)).reshape(-1, 2 * k_rows + 128)
    key_across = swap(key_near, "fsdp", 2)
    key_shards = [key_near, key_across, swap(key_near, "fsdp", 1), swap(key_across, "fsdp", 1)]
    both_copies = shard_copies(qkv_weight, out_weight, False)
    both_near = spread(after(both_copies, key_near)).reshape(-1, 2 * q_rows)

    down_t = expert_down[0].T[None]
    half = width // 2
    own = jnp.stack(
        [jnp.concatenate([expert_in[0, :, rows], down_t[:, rows]]) for rows in (slice(0, half), slice(half, width))]
    ).astype(low)
    along_tp = [swap(after(own, key_near), "tp", m) for m in over_tp[1:]]
    along_x = swap(after(own, *key_shards[2:]), "fsdp", 2)

    places = ctx_index * tok_rows + jnp.arange(tok_rows, dtype=jnp.int32)
    _, position = doc_positions(lengths[0], places)
    starts = (places - position)[None, :]
    frequency = jnp.exp(jnp.arange(HD // 2, dtype=f32) * (-2.0 * math.log(ROPE_BASE) / HD))
    angles = frequency[:, None] * position.astype(f32)[None, :]
    cosine, sine = jnp.cos(angles), jnp.sin(angles)
    kv_t, normed_low, norm_t, key_whole, gains = project_keys(
        place, tokens, cosine, sine, key_shards, k_rows
    )
    gain_one, gain_two = gains[0], gains[1]
    both_across = swap(after(both_near, kv_t, along_x), "fsdp", 2)
    both_shards = [
        both_near,
        both_across,
        swap(after(both_near, kv_t), "fsdp", 1),
        swap(after(both_across, kv_t), "fsdp", 1),
    ]
    kv_pieces = spread(kv_t)
    q_t, query_whole = project_queries(place, normed_low, cosine, sine, both_shards)

    uppers = [swap(along_x[:1], "tp", m) for m in over_tp[1:]]
    lowers = [swap(after(piece[1:], both_across), "fsdp", 2) for piece in along_tp]
    soon = [swap(after(own, both_near), "fsdp", 1)]

    grad_rows = row_copies(after(place, kv_t), out_grad, routes, gate_weights, half_rows, experts)
    og = spread(after(grad_rows, kv_pieces))

    probs, head_t, kv_all, out_t, attn_own, *attn_others = attend(
        after(place, *soon, *along_tp), starts, q_t, kv_pieces, both_shards
    )
    soon += [swap(after(piece, attn_own), "fsdp", 1) for piece in [*along_tp, along_x, *uppers, *lowers]]
    hidden_one = own_half(after(tokens, og, *soon)).astype(f32) + sum_own(attn_own, attn_others)
    inverse_two = lax.rsqrt(jnp.mean(hidden_one * hidden_one, axis=-1, keepdims=True) + EPSILON)
    normed_two = hidden_one * inverse_two
    normed_two_low = (normed_two * gain_two).astype(low)

    x_own = after(normed_two_low, og)
    xs = [x_own] + [swap(x_own, "ctx", m) for m in range(1, n_ctx)]
    weights = [own, *along_tp, along_x, *uppers, *lowers, *soon]
    backs = back_rows(og, weights, width)
    grads_x, acts, ggs, gus = [], [], [], []
    for at in range(0, n_ctx, 2):
        here = after(place, *acts[-1:])
        some_x, (act, gg, gu) = expert_rows(
            here, tuple(range(at, at + 2)), xs[at : at + 2], og, backs, weights, experts
        )
        grads_x += some_x
        acts.append(act)
        ggs.append(gg)
        gus.append(gu)
    come_x = [swap(grads_x[m], "ctx", m) for m in range(1, n_ctx)]
    core_leave, core_stay = weight_grads(place, xs, og, acts, ggs, gus, n_tp, 2)
    leave, stay = weight_grads(after(place, core_leave), xs, og, acts, ggs, gus, n_tp, 0)
    mixes = mix_rows(after(place, leave), acts, weights, n_ctx, width)

    grad_normed_two = after(grads_x[0], mixes).astype(f32)
    for come in come_x:
        grad_normed_two += come.astype(f32)
    gain_grad_two = jnp.sum(grad_normed_two * normed_two, axis=0)
    grad_hidden = own_half(out_grad).astype(f32) + norm_back(grad_normed_two, normed_two, inverse_two, gain_two)
    grad_attn = to_others(grad_hidden.astype(low))
    core_leave = swap(after(core_leave, mixes, *come_x), "fsdp", 1)
    come_mix = spread(after(mixes, grad_hidden))

    core_leave = after(core_leave, grad_hidden)
    uppers_out = [pair_sum(leave, core_leave, 2 * m, 2) for m in range(n_tp - 1)]
    lower_out = pair_sum(leave, core_leave, 2 * (n_tp - 1), n_tp)
    uppers_in = [swap(uppers_out[m - 1], "tp", m) for m in over_tp[1:]]
    lower_in = swap(lower_out, "fsdp", 2)

    dq_t, kv_grads = attend_back(
        after(place, lower_out, *uppers_out), probs, q_t, kv_all, grad_attn, out_t, cosine, sine
    )
    come_mix = after(come_mix, dq_t)
    come = spread(kv_grads)
    core_stay = swap(after(core_stay, lower_out), "fsdp", 1)
    query_parts, query_part = query_grads(
        after(place, come_mix), dq_t, norm_t, query_whole, grad_attn, head_t
    )

    lower_next = [
        total_of(stay[2 + m], core_stay[2 + m], after(lower_in, query_part)[m]) for m in over_tp[1:]
    ]
    upper_next = total_of(stay[1], core_stay[1], *(after(part, query_part)[1] for part in uppers_in))
    lowers_last = [swap(lower_next[m - 1], "tp", m) for m in over_tp[1:]]
    query_near, query_far = sum_cores(query_parts, upper_next, *lower_next)
    mixture = jnp.sum(after(come_mix, query_far).astype(f32), axis=0)
    query_near = added(query_near, swap(query_far, "fsdp", 2))
    upper_last = swap(after(upper_next, query_near), "fsdp", 2)
    key_parts, (normed_own, *normed_others) = key_grads(
        after(place, query_near, *lowers_last), come, cosine, sine, norm_t, key_whole,
        tokens, query_part, gain_grad_two[None]
    )
    grad_normed_one = sum_own(normed_own, normed_others)
    block_parts = to_others((hidden_one + mixture).astype(low))
    inputs = own_half(tokens).astype(f32)
    inverse_one = lax.rsqrt(jnp.mean(inputs * inputs, axis=-1, keepdims=True) + EPSILON)
    in_parts = to_others(
        (grad_hidden + norm_back(grad_normed_one, inputs * inverse_one, inverse_one, gain_one)).astype(low)
    )
    key_near, key_far = sum_cores(key_parts, upper_last)
    query_grad = scatter_rows(query_near)
    upper_parts = [(stay, 0), (core_stay, 0)] + [(part, 0) for part in uppers_in] + [(upper_last[None], 0)]
    lower_parts = [(stay, 2), (core_stay, 2), (lower_in, 0)] + [(part[None], 0) for part in lowers_last]
    in_new = step_in(upper_parts, lower_parts, after(expert_in, key_far), in_moment, in_average)
    key_near = added(key_near, after(swap(key_far, "fsdp", 2), query_grad, in_new[0]))
    key_grad = scatter_rows(key_near)
    block_out = join(place, [after(part, key_near) for part in block_parts])
    out_new = step_out(query_grad, after(out_weight, block_out), out_moment, out_average)
    down_new = step_down(upper_parts, lower_parts, after(expert_down, out_new[0]), down_moment, down_average)
    in_grad = join(place, [after(part, down_new[0]) for part in in_parts])
    key_grad = after(key_grad, in_grad)
    gains_grad = jnp.sum(key_grad[:, :, 2 * k_rows : 2 * k_rows + 2].astype(f32), axis=0).T
    gains_others = [swap(gains_grad, "tp", m) for m in over_tp[1:]]
    qkv_new = step_qkv(query_grad, key_grad, qkv_weight, qkv_moment, qkv_average)
    gains_grad = gains_grad + sum(after(other, qkv_new[0]) for other in gains_others)
    gain_new = advance(norm_gains, gains_grad, gain_moment, gain_average, RATE_GAIN)
    return (block_out, in_grad, *qkv_new, *out_new, *gain_new, *in_new, *down_new)


def solution(mesh):
    return jax.shard_map(
        per_device,
        mesh=mesh,
        in_specs=(
            P(("fsdp", "ctx"), None),
            P(("fsdp", "ctx"), None),
            P("fsdp", None),
            P(("fsdp", "ctx"), None),
            P(("fsdp", "ctx"), None),
            P(("fsdp", "ctx"), "tp"),
            P("tp", ("fsdp", "ctx")),
            P(None, ("fsdp", "ctx")),
            P(("fsdp", "ctx"), None, None, "tp"),
            P(("fsdp", "ctx"), "tp", None),
            P(("fsdp", "ctx"), "tp"),
            P(("fsdp", "ctx"), "tp"),
            P("tp", ("fsdp", "ctx")),
            P("tp", ("fsdp", "ctx")),
            P(None, ("fsdp", "ctx")),
            P(None, ("fsdp", "ctx")),
            P(("fsdp", "ctx"), None, None, "tp"),
            P(("fsdp", "ctx"), None, None, "tp"),
            P(("fsdp", "ctx"), "tp", None),
            P(("fsdp", "ctx"), "tp", None),
        ),
        out_specs=(
            P(("fsdp", "ctx"), None),
            P(("fsdp", "ctx"), None),
            P(("fsdp", "ctx"), "tp"),
            P(("fsdp", "ctx"), "tp"),
            P(("fsdp", "ctx"), "tp"),
            P("tp", ("fsdp", "ctx")),
            P("tp", ("fsdp", "ctx")),
            P("tp", ("fsdp", "ctx")),
            P(None, ("fsdp", "ctx")),
            P(None, ("fsdp", "ctx")),
            P(None, ("fsdp", "ctx")),
            P(("fsdp", "ctx"), None, None, "tp"),
            P(("fsdp", "ctx"), None, None, "tp"),
            P(("fsdp", "ctx"), None, None, "tp"),
            P(("fsdp", "ctx"), "tp", None),
            P(("fsdp", "ctx"), "tp", None),
            P(("fsdp", "ctx"), "tp", None),
        ),
        check_vma=False,
    )
```

```python
import functools
import math

import jax
import jax.numpy as jnp
from jax import lax
from jax.experimental import pallas as pl
from jax.experimental.pallas import tpu as pltpu
from jax.sharding import PartitionSpec as P

HD = 64
GROUP = 3


EPSILON = 1e-05
ROPE_BASE = 10000.0
MOMENTUM = 0.9
AVERAGE = 0.7
RATE_QKV = 7e-05
RATE_OUT = 0.15
RATE_GAIN = 0.0005
RATE_IN = 0.0004
RATE_DOWN = 0.001


def doc_positions(lengths_row, places):
    doc_ends = jnp.cumsum(lengths_row)
    passed = places[:, None] >= doc_ends[None, :]
    segment = jnp.sum(passed.astype(jnp.int32), axis=1)
    doc_start = jnp.sum(jnp.where(passed, lengths_row[None, :], 0), axis=1)
    return (segment, places - doc_start)


def norm_back(grad_out, normed, inverse, gain_row):
    scaled = grad_out * gain_row
    return inverse * (scaled - normed * jnp.mean(scaled * normed, axis=-1, keepdims=True))


F_MASKS = (0, 2, 1, 3)
VMEM_LIMIT = 60 * 1024 * 1024


def advance(weight, gradient, moment, average, step_rate):
    moment_new = MOMENTUM * moment + gradient
    weight_new = weight - step_rate * (gradient + MOMENTUM * moment_new)
    average_new = AVERAGE * average + (1.0 - AVERAGE) * weight_new
    return (moment_new, average_new, weight_new)


def swap(value, axis, mask):
    size = lax.axis_size(axis)
    return lax.ppermute(value, axis, [(i, i ^ mask) for i in range(size)])


def after(value, *others):
    return lax.optimization_barrier((value, *others))[0]


def nt_dot(left_mat, right_mat):
    return lax.dot_general(
        left_mat, right_mat, (((1,), (1,)), ((), ())), preferred_element_type=jnp.float32
    )


def vmem_spec():
    return pl.BlockSpec(memory_space=pltpu.VMEM)


def any_spec():
    return pl.BlockSpec(memory_space=pl.ANY)


def smem_spec():
    return pl.BlockSpec(memory_space=pltpu.SMEM)


def added(left_mat, right_mat):
    return (left_mat.astype(jnp.float32) + right_mat.astype(jnp.float32)).astype(jnp.bfloat16)


def params():
    return pltpu.CompilerParams(vmem_limit_bytes=VMEM_LIMIT)


def cost(flops, mib):
    return pl.CostEstimate(flops=1, bytes_accessed=1, transcendentals=0)


def spread(blocks):
    return lax.all_to_all(blocks, "ctx", split_axis=0, concat_axis=0, tiled=True)


def gather_along_ctx(own):
    return spread(jnp.broadcast_to(own[None], (lax.axis_size("ctx"), *own.shape)))


def load_shards(place_ref, shard_refs, whole, sems, first=0):
    cols = slice(first, first + whole.shape[1])
    rows = shard_refs[0].shape[0]
    copies = []
    for i, shard in enumerate(shard_refs):
        at = pl.multiple_of((place_ref[0] ^ F_MASKS[i]) * rows, rows)
        copies.append(pltpu.make_async_copy(shard.at[:, cols], whole.at[pl.ds(at, rows)], sems.at[i]))
    return copies


def turn(first, second, cosine, sine):
    return first * cosine - second * sine, second * cosine + first * sine


def key_shard_kernel(qkv, gains, out, wide, square):
    rows, columns = qkv.shape
    kv = columns // ((GROUP + 2) * HD)
    for h in range(kv):
        at = h * (GROUP + 2) * HD + GROUP * HD
        wide[:, h * HD : (h + 1) * HD] = qkv[:, at : at + HD]
        wide[:, (kv + h) * HD : (kv + h + 1) * HD] = qkv[:, at + HD : at + 2 * HD]
    square[...] = jnp.zeros_like(square)
    square[: gains.shape[0], :rows] = gains[...]
    wide[:, 2 * kv * HD :] = square[...].T[:rows]
    low = wide[...].astype(jnp.bfloat16)
    for i in range(out.shape[0]):
        out[i] = low


def both_shard_kernel(qkv, weight, out, wide, tall):
    rows, columns = qkv.shape
    kv = columns // ((GROUP + 2) * HD)
    group = GROUP * HD
    for h in range(kv):
        at = h * (GROUP + 2) * HD
        wide[:, h * group : (h + 1) * group] = qkv[:, at : at + group]
    tall[...] = jnp.zeros_like(tall)
    tall[:, :rows] = weight[...]
    wide[:, kv * group :] = tall[...].T[:rows]
    low = wide[...].astype(jnp.bfloat16)
    for i in range(out.shape[0]):
        out[i] = low


def shard_copies(qkv, other, keys):
    rows, columns = qkv.shape
    kv = columns // ((GROUP + 2) * HD)
    wide = 2 * kv * HD + 128 if keys else 2 * GROUP * kv * HD
    padded = pltpu.VMEM((128, 128) if keys else (other.shape[0], 128), jnp.float32)
    return pl.pallas_call(
        key_shard_kernel if keys else both_shard_kernel,
        out_shape=jax.ShapeDtypeStruct((lax.axis_size("ctx"), rows, wide), jnp.bfloat16),
        in_specs=[vmem_spec()] * 2,
        out_specs=vmem_spec(),
        scratch_shapes=[pltpu.VMEM((rows, wide), jnp.float32), padded],
        compiler_params=params(),
        cost_estimate=cost(1, 1),
        name="key_shard" if keys else "both_shard",
    )(qkv, other)


def row_copies_kernel(experts, place, og, routes, gates, out):
    copies, rows, columns = out.shape
    width = columns - 128
    at = pl.ds(pl.multiple_of(place[2] * rows, rows), rows)
    lane = lax.broadcasted_iota(jnp.int32, (rows, 128), 1)
    high = jnp.zeros((rows, 128), jnp.float32)
    rest = jnp.zeros((rows, 128), jnp.float32)
    chosen, weights = routes[at], gates[at]
    for k in range(routes.shape[1]):
        weight = weights[:, k : k + 1]
        top = weight.astype(jnp.bfloat16).astype(jnp.float32)
        high += jnp.where(lane == chosen[:, k : k + 1], top, 0.0)
        rest += jnp.where(lane == chosen[:, k : k + 1] + experts, weight - top, 0.0)
    beside = (high + rest).astype(jnp.bfloat16)
    own = og[at]
    for i in range(copies):
        out[i, :, :width] = own
        out[i, :, width:] = beside


def row_copies(place, out_grad, routes, gate_weights, rows, experts):
    width = out_grad.shape[1]
    return pl.pallas_call(
        functools.partial(row_copies_kernel, experts),
        out_shape=jax.ShapeDtypeStruct((lax.axis_size("ctx"), rows, width + 128), jnp.bfloat16),
        in_specs=[smem_spec()] + [vmem_spec()] * 3,
        out_specs=vmem_spec(),
        compiler_params=params(),
        cost_estimate=cost(1, 1),
        name="row_copies",
    )(place, out_grad, routes, gate_weights)


def join_kernel(place, *refs):
    parts, out = refs[:-1], refs[-1]
    rows = parts[0].shape[0]
    for m, part in enumerate(parts):
        out[pl.ds(pl.multiple_of((place[2] ^ m) * rows, rows), rows)] = part[...]


def join(place, parts):
    rows, width = parts[0].shape
    return pl.pallas_call(
        join_kernel,
        out_shape=jax.ShapeDtypeStruct((len(parts) * rows, width), parts[0].dtype),
        in_specs=[smem_spec()] + [vmem_spec()] * len(parts),
        out_specs=vmem_spec(),
        compiler_params=params(),
        cost_estimate=cost(1, 1),
        name="join",
    )(place, *parts)


def project_keys_kernel(k_rows, *refs):
    place, tok, cos_ref, sin_ref = refs[:4]
    shard_refs, refs = refs[4 : 4 + len(F_MASKS)], refs[4 + len(F_MASKS) :]
    copies_ref, norm_ref, norm_t, whole, gain_ref, kv_ref, sems = refs
    copies = load_shards(place, shard_refs, whole, sems)
    for copy in copies:
        copy.start()
    x = tok[...].astype(jnp.float32)
    hat = x * lax.rsqrt(jnp.mean(x * x, axis=-1, keepdims=True) + EPSILON)
    for copy in copies:
        copy.wait()
    gains = whole[:, 2 * k_rows :].astype(jnp.float32).T
    gain_ref[...] = gains[:8]
    normed = (hat * gains[:1]).astype(jnp.bfloat16)
    norm_ref[...] = normed
    norm_t[...] = normed.T
    cosine, sine = cos_ref[...], sin_ref[...]
    half = HD // 2
    heads = jnp.dot(normed, whole[:, : 2 * k_rows], preferred_element_type=jnp.float32).T
    for at in range(0, k_rows, HD):
        a, b = turn(heads[at : at + half], heads[at + half : at + HD], cosine, sine)
        kv_ref[at : at + half] = a.astype(jnp.bfloat16)
        kv_ref[at + half : at + HD] = b.astype(jnp.bfloat16)
    kv_ref[k_rows:] = heads[k_rows:].astype(jnp.bfloat16)
    for i in range(copies_ref.shape[0]):
        copies_ref[i] = kv_ref[...]


def project_keys(place, tokens, cosine, sine, shards, k_rows):
    rows, width = tokens.shape
    low = jnp.bfloat16
    columns = shards[0].shape[1]
    return pl.pallas_call(
        functools.partial(project_keys_kernel, k_rows),
        out_shape=[
            jax.ShapeDtypeStruct((lax.axis_size("ctx"), 2 * k_rows, rows), low),
            jax.ShapeDtypeStruct((rows, width), low),
            jax.ShapeDtypeStruct((width, rows), low),
            jax.ShapeDtypeStruct((width, columns), low),
            jax.ShapeDtypeStruct((8, width), jnp.float32),
        ],
        in_specs=[smem_spec()] + [vmem_spec()] * 3 + [any_spec()] * len(shards),
        out_specs=[vmem_spec()] * 5,
        scratch_shapes=[
            pltpu.VMEM((2 * k_rows, rows), low),
            pltpu.SemaphoreType.DMA((len(shards),)),
        ],
        compiler_params=params(),
        cost_estimate=cost(2 * rows * width * columns, 8),
        name="project_keys",
    )(place, tokens, cosine, sine, *shards)


def project_queries_kernel(*refs):
    place, norm_ref, cos_ref, sin_ref = refs[:4]
    shard_refs, refs = refs[4 : 4 + len(F_MASKS)], refs[4 + len(F_MASKS) :]
    q_ref, whole, sems = refs
    copies = load_shards(place, shard_refs, whole, sems)
    for copy in copies:
        copy.start()
    for copy in copies:
        copy.wait()
    cosine, sine = cos_ref[...], sin_ref[...]
    half = HD // 2
    heads = jnp.dot(norm_ref[...], whole[...], preferred_element_type=jnp.float32).T
    scale = jnp.bfloat16(HD**-0.5)
    for at in range(0, q_ref.shape[0], HD):
        a, b = turn(heads[at : at + half], heads[at + half : at + HD], cosine, sine)
        q_ref[at : at + half] = a.astype(jnp.bfloat16) * scale
        q_ref[at + half : at + HD] = b.astype(jnp.bfloat16) * scale


def project_queries(place, normed, cosine, sine, shards):
    rows, width = normed.shape
    low = jnp.bfloat16
    columns = shards[0].shape[1] // 2
    return pl.pallas_call(
        project_queries_kernel,
        out_shape=[
            jax.ShapeDtypeStruct((columns, rows), low),
            jax.ShapeDtypeStruct((width, columns), low),
        ],
        in_specs=[smem_spec()] + [vmem_spec()] * 3 + [any_spec()] * len(shards),
        out_specs=[vmem_spec()] * 2,
        scratch_shapes=[pltpu.SemaphoreType.DMA((len(shards),))],
        compiler_params=params(),
        cost_estimate=cost(1, 1),
        name="project_queries",
    )(place, normed, cosine, sine, *shards)


def share_out(place, part, own_ref, other_refs):
    rows = own_ref.shape[0]
    for m, out in enumerate((own_ref, *other_refs)):
        at = pl.multiple_of((place[2] ^ m) * rows, rows)
        out[...] = part[pl.ds(at, rows)].astype(out.dtype)


def attend_kernel(n_ctx, *refs):
    place, start_ref, q_ref, piece_ref = refs[:4]
    refs = refs[4:]
    shard_refs, refs = refs[: len(F_MASKS)], refs[len(F_MASKS) :]
    p_ref, head_ref, kv_all, out_t, own_ref = refs[:5]
    other_refs, (bias, scores, q3, part, sems) = refs[5:-5], refs[-5:]
    rows = q_ref.shape[1]
    half_kv = kv_all.shape[0] // 2
    step = pl.program_id(0)
    copies = load_shards(place, shard_refs, out_t, sems, out_t.shape[1])

    @pl.when(step == 0)
    def _():
        for copy in copies:
            copy.start()
        key_at = lax.broadcasted_iota(jnp.int32, (rows, rows), 0)
        query_at = lax.broadcasted_iota(jnp.int32, (rows, rows), 1)
        for j in range(n_ctx):
            kv_all[:, j * rows : (j + 1) * rows] = piece_ref[j]
            allowed = key_at + j * rows >= start_ref[...]
            allowed = allowed & (key_at + j * rows <= query_at + place[1] * rows)
            bias[j * rows : (j + 1) * rows] = jnp.where(allowed, 0.0, -1e30)

    for h in range(GROUP):
        q3[:, h * rows : (h + 1) * rows] = q_ref[h * HD : (h + 1) * HD]
    keys = kv_all[pl.ds(pl.multiple_of(step * HD, HD), HD)]
    values = kv_all[pl.ds(pl.multiple_of(half_kv + step * HD, HD), HD)]
    scores[...] = jnp.dot(keys.T, q3[...], preferred_element_type=jnp.float32)
    for h in range(GROUP):
        cols = slice(h * rows, (h + 1) * rows)
        masked = scores[:, cols] + bias[...]
        exponent = jnp.exp(masked - jnp.max(masked, axis=0, keepdims=True))
        inverse = 1.0 / jnp.sum(exponent, axis=0, keepdims=True)
        p_ref[0, :, cols] = (exponent * inverse).astype(jnp.bfloat16)
    attended = jnp.dot(values, p_ref[0], preferred_element_type=jnp.float32).astype(jnp.bfloat16)
    for h in range(GROUP):
        at = pl.multiple_of((step * GROUP + h) * HD, HD)
        head_ref[pl.ds(at, HD)] = attended[:, h * rows : (h + 1) * rows]

    @pl.when(step == pl.num_programs(0) - 1)
    def _():
        for copy in copies:
            copy.wait()
        part[...] = nt_dot(head_ref[...].T, out_t[...])
        share_out(place, part, own_ref, other_refs)


def attend(place, starts, q_t, pieces, shards):
    n_ctx, n_tp = lax.axis_size("ctx"), lax.axis_size("tp")
    q_rows, rows = q_t.shape
    kv = q_rows // (GROUP * HD)
    width = shards[0].shape[0] * len(shards)
    seq = rows * n_ctx
    low = jnp.bfloat16
    return pl.pallas_call(
        functools.partial(attend_kernel, n_ctx),
        grid=(kv,),
        out_shape=[
            jax.ShapeDtypeStruct((kv, seq, GROUP * rows), low),
            jax.ShapeDtypeStruct((q_rows, rows), low),
            jax.ShapeDtypeStruct((2 * kv * HD, seq), low),
            jax.ShapeDtypeStruct((width, q_rows), low),
            jax.ShapeDtypeStruct((rows // n_tp, width), jnp.float32),
        ]
        + [jax.ShapeDtypeStruct((rows // n_tp, width), low)] * (n_tp - 1),
        in_specs=[smem_spec(), vmem_spec(), pl.BlockSpec((GROUP * HD, rows), lambda i: (i, 0))]
        + [vmem_spec()]
        + [any_spec()] * len(shards),
        out_specs=[pl.BlockSpec((1, seq, GROUP * rows), lambda i: (i, 0, 0))] + [vmem_spec()] * (3 + n_tp),
        scratch_shapes=[
            pltpu.VMEM((seq, rows), jnp.float32),
            pltpu.VMEM((seq, GROUP * rows), jnp.float32),
            pltpu.VMEM((HD, GROUP * rows), low),
            pltpu.VMEM((rows, width), jnp.float32),
            pltpu.SemaphoreType.DMA((len(shards),)),
        ],
        compiler_params=pltpu.CompilerParams(vmem_limit_bytes=VMEM_LIMIT),
        cost_estimate=pl.CostEstimate(
            flops=2 * q_rows * rows * (2 * seq + width), bytes_accessed=20 << 20, transcendentals=0
        ),
        name="attend",
    )(place, starts, q_t, pieces, *shards)


def attend_back_kernel(n_ctx, *refs):
    place, p_ref, q_ref, kv_all, out_t, cos_ref, sin_ref = refs[:7]
    grad_refs, (dq_ref, piece_ref, grad_all, grads, q3, g3) = refs[7:-6], refs[-6:]
    rows = q_ref.shape[1]
    half_kv = kv_all.shape[0] // 2
    step = pl.program_id(0)

    @pl.when(step == 0)
    def _():
        join_kernel(place, *grad_refs, grad_all)
        back = jnp.dot(grad_all[...], out_t[...], preferred_element_type=jnp.float32)
        grads[...] = back.astype(jnp.bfloat16).T

    for h in range(GROUP):
        cols = slice(h * rows, (h + 1) * rows)
        q3[:, cols] = q_ref[h * HD : (h + 1) * HD]
        g3[:, cols] = grads[pl.ds(pl.multiple_of((step * GROUP + h) * HD, HD), HD)]
    keys = kv_all[pl.ds(pl.multiple_of(step * HD, HD), HD)]
    values = kv_all[pl.ds(pl.multiple_of(half_kv + step * HD, HD), HD)]
    probs = p_ref[0].astype(jnp.float32)
    grad_probs = jnp.dot(values.T, g3[...], preferred_element_type=jnp.float32)
    inner = jnp.sum(probs * grad_probs, axis=0, keepdims=True)
    grad_scores = (probs * (grad_probs - inner)).astype(jnp.bfloat16)
    grad_query = jnp.dot(keys, grad_scores, preferred_element_type=jnp.float32) * HD**-0.5
    grad_key = nt_dot(grad_scores, q3[...]).T
    grad_value = nt_dot(p_ref[0], g3[...]).T
    half = HD // 2
    cosine, sine = cos_ref[...], -sin_ref[...]
    for h in range(GROUP):
        cols = slice(h * rows, (h + 1) * rows)
        a, b = turn(grad_query[:half, cols], grad_query[half:, cols], cosine, sine)
        dq_ref[h * HD : h * HD + half] = a.astype(jnp.bfloat16)
        dq_ref[h * HD + half : (h + 1) * HD] = b.astype(jnp.bfloat16)
    key_at = pl.ds(pl.multiple_of(step * HD, HD), HD)
    value_at = pl.ds(pl.multiple_of(half_kv + step * HD, HD), HD)
    for j in range(n_ctx):
        cols = slice(j * rows, (j + 1) * rows)
        piece_ref[j, key_at] = grad_key[:, cols].astype(jnp.bfloat16)
        piece_ref[j, value_at] = grad_value[:, cols].astype(jnp.bfloat16)


def attend_back(place, probs, q_t, kv_all, grads, out_t, cosine, sine):
    n_ctx = lax.axis_size("ctx")
    q_rows, rows = q_t.shape
    kv, seq = probs.shape[:2]
    low = jnp.bfloat16
    block = pl.BlockSpec((GROUP * HD, rows), lambda i: (i, 0))
    return pl.pallas_call(
        functools.partial(attend_back_kernel, n_ctx),
        grid=(kv,),
        out_shape=[
            jax.ShapeDtypeStruct((q_rows, rows), low),
            jax.ShapeDtypeStruct((n_ctx, 2 * kv * HD, rows), low),
        ],
        in_specs=[smem_spec(), pl.BlockSpec((1, seq, GROUP * rows), lambda i: (i, 0, 0)), block]
        + [vmem_spec()] * (4 + len(grads)),
        out_specs=[block, vmem_spec()],
        scratch_shapes=[
            pltpu.VMEM((rows, out_t.shape[0]), low),
            pltpu.VMEM((q_rows, rows), low),
            pltpu.VMEM((HD, GROUP * rows), low),
            pltpu.VMEM((HD, GROUP * rows), low),
        ],
        compiler_params=pltpu.CompilerParams(vmem_limit_bytes=VMEM_LIMIT),
        cost_estimate=pl.CostEstimate(flops=1, bytes_accessed=90 << 20, transcendentals=0),
        name="attend_back",
    )(place, probs, q_t, kv_all, out_t, cosine, sine, *grads)


def store_products(place, left_t, right, out_refs):
    rows = out_refs[0].shape[0]
    for mask, out in zip(F_MASKS, out_refs):
        at = pl.multiple_of((place[0] ^ mask) * rows, rows)
        out[...] = jnp.dot(
            left_t[pl.ds(at, rows)], right, preferred_element_type=jnp.float32
        ).astype(jnp.bfloat16)


def query_grad_kernel(place, dq_ref, norm_t, whole, head_ref, *refs):
    grad_refs, (near, far, core, part_ref, grad_all, grad_t) = refs[:-6], refs[-6:]
    columns = whole.shape[1]
    back = dq_ref[...].T
    outs = [near, far, core.at[0], core.at[1]]
    store_products(place, norm_t, back, [out.at[:, :columns] for out in outs])
    join_kernel(place, *grad_refs, grad_all)
    grad_t[...] = grad_all[...].T
    store_products(place, grad_t, head_ref[...].T, [out.at[:, columns:] for out in outs])
    part_ref[...] = nt_dot(back, whole[...])


def row_parts(rows, columns):
    low = jnp.bfloat16
    return [
        jax.ShapeDtypeStruct((rows, columns), low),
        jax.ShapeDtypeStruct((rows, columns), low),
        jax.ShapeDtypeStruct((2, rows, columns), low),
    ]


def query_grads(place, dq_t, norm_t, whole, grads, head_t):
    q_rows, rows = dq_t.shape
    width = norm_t.shape[0]
    outs = pl.pallas_call(
        query_grad_kernel,
        out_shape=row_parts(width // len(F_MASKS), 2 * q_rows)
        + [jax.ShapeDtypeStruct((rows, width), jnp.float32)],
        in_specs=[smem_spec()] + [vmem_spec()] * (4 + len(grads)),
        out_specs=[vmem_spec()] * 4,
        scratch_shapes=[pltpu.VMEM((rows, width), jnp.bfloat16), pltpu.VMEM((width, rows), jnp.bfloat16)],
        compiler_params=params(),
        cost_estimate=cost(6 * rows * width * q_rows, 15),
        name="query_grads",
    )(place, dq_t, norm_t, whole, head_t, *grads)
    return outs[:3], outs[3]


def key_grad_kernel(n_ctx, *refs):
    place, piece_ref = refs[:2]
    refs = refs[2:]
    cos_ref, sin_ref, norm_t, whole, tok, query_part, gain_two_ref = refs[:7]
    near, far, core, own_ref = refs[7:11]
    other_refs, (part_ref, back_t, right) = refs[11:-3], refs[-3:]
    kv_rows, rows = piece_ref.shape[1:]
    total = piece_ref[0].astype(jnp.float32)
    for j in range(1, n_ctx):
        total += piece_ref[j].astype(jnp.float32)
    cosine, sine = cos_ref[...], -sin_ref[...]
    half = HD // 2
    for at in range(0, kv_rows // 2, HD):
        a, b = turn(total[at : at + half], total[at + half : at + HD], cosine, sine)
        back_t[at : at + half] = a.astype(jnp.bfloat16)
        back_t[at + half : at + HD] = b.astype(jnp.bfloat16)
    back_t[kv_rows // 2 :] = total[kv_rows // 2 :].astype(jnp.bfloat16)
    back = back_t[...].T
    part = query_part[...] + nt_dot(back, whole[:, :kv_rows])
    part_ref[...] = part
    share_out(place, part_ref, own_ref, other_refs)
    outs = [near, far, core.at[0], core.at[1]]
    store_products(place, norm_t, back, [out.at[:, :kv_rows] for out in outs])
    x = tok[...].astype(jnp.float32)
    hat = x * lax.rsqrt(jnp.mean(x * x, axis=-1, keepdims=True) + EPSILON)
    gain_one = jnp.sum(part * hat, axis=0, keepdims=True)
    row = lax.broadcasted_iota(jnp.int32, (128, x.shape[1]), 0)
    columns = jnp.where(row == 0, gain_one, jnp.where(row == 1, gain_two_ref[...], 0.0))
    right[...] = columns.T
    count = near.shape[0]
    for mask, out in zip(F_MASKS, outs):
        at = pl.multiple_of((place[0] ^ mask) * count, count)
        out[:, kv_rows:] = right[pl.ds(at, count)].astype(jnp.bfloat16)


def key_grads(place, pieces, cosine, sine, norm_t, whole, tokens, query_part, gain_two):
    n_ctx, n_tp = lax.axis_size("ctx"), lax.axis_size("tp")
    kv_rows, rows = pieces.shape[1:]
    width = norm_t.shape[0]
    outs = pl.pallas_call(
        functools.partial(key_grad_kernel, n_ctx),
        out_shape=row_parts(width // len(F_MASKS), kv_rows + 128)
        + [jax.ShapeDtypeStruct((rows // n_tp, width), jnp.float32)]
        + [jax.ShapeDtypeStruct((rows // n_tp, width), jnp.bfloat16)] * (n_tp - 1),
        in_specs=[smem_spec()] + [vmem_spec()] * 8,
        out_specs=[vmem_spec()] * (3 + n_tp),
        scratch_shapes=[
            pltpu.VMEM((rows, width), jnp.float32),
            pltpu.VMEM((kv_rows, rows), jnp.bfloat16),
            pltpu.VMEM((width, 128), jnp.float32),
        ],
        compiler_params=params(),
        cost_estimate=cost(4 * rows * width * kv_rows, 12),
        name="key_grads",
    )(place, pieces, cosine, sine, norm_t, whole, tokens, query_part, gain_two)
    return outs[:3], outs[3:]


def sum_cores(parts, *before):
    near, far, core = parts
    core = after(swap(core, "fsdp", 1), *before)
    return added(near, core[0]), added(far, core[1])


def scatter_rows(near):
    n_ctx = lax.axis_size("ctx")
    return spread(near.reshape(n_ctx, near.shape[0] // n_ctx, near.shape[1]))


def table(count):
    near = [((m, 0), (m, 1)) for m in range(count)]
    far = [((count, 0), (count, 1))]
    far += [((count + m, 0), (2 * count - 1 + m, 0)) for m in range(1, count)]
    return [near, far] + [
        [tuple((array + 3 * count - 1, at) for array, at in piece) for piece in pieces] for pieces in (near, far)
    ]


def load_experts(refs, target, sems, kinds):
    half, hidden = refs[0].shape[2:]
    copies = []
    for expert, pieces in enumerate(table((len(refs) + 2) // 6)):
        for m, piece in enumerate(pieces):
            for at, kind in enumerate(kinds):
                for j, (array, index) in enumerate(piece):
                    copies.append(
                        pltpu.make_async_copy(
                            refs[array].at[index, kind],
                            target.at[at, expert, j * half : (j + 1) * half, m * hidden : (m + 1) * hidden],
                            sems.at[expert, (m * len(kinds) + at) * 2 + j],
                        )
                    )
    return copies


def weight_scratch(weights, kinds):
    count = (len(weights) + 2) // 6
    half, hidden = weights[0].shape[2:]
    return [
        pltpu.VMEM((kinds, len(F_MASKS), 2 * half, count * hidden), jnp.bfloat16),
        pltpu.SemaphoreType.DMA((len(F_MASKS), 2 * kinds * count)),
    ]


def back_kernel(og_ref, *refs):
    weight_refs, (back_ref, og_all, weights, sems) = refs[:-4], refs[-4:]
    copies = load_experts(weight_refs, weights, sems, (2,))
    for copy in copies:
        copy.start()
    blocks, rows, _ = og_ref.shape
    width = og_all.shape[1]
    for b in range(blocks):
        og_all[b * rows : (b + 1) * rows] = og_ref[b, :, :width]
    hidden = weights.shape[3]
    each = len(copies) // len(F_MASKS)
    for expert in range(len(F_MASKS)):
        for copy in copies[expert * each : (expert + 1) * each]:
            copy.wait()
        back = jnp.dot(og_all[...], weights[0, expert], preferred_element_type=jnp.float32)
        for b in range(blocks):
            back_ref[b, :, expert * hidden : (expert + 1) * hidden] = back[b * rows : (b + 1) * rows].astype(
                jnp.bfloat16
            )


def back_rows(og, weights, width):
    blocks, rows, _ = og.shape
    scratch = weight_scratch(weights, 1)
    hidden = scratch[0].shape[3] * len(F_MASKS)
    return pl.pallas_call(
        back_kernel,
        out_shape=jax.ShapeDtypeStruct((blocks, rows, hidden), jnp.bfloat16),
        in_specs=[vmem_spec()] + [any_spec()] * len(weights),
        out_specs=vmem_spec(),
        scratch_shapes=[pltpu.VMEM((blocks * rows, width), jnp.bfloat16)] + scratch,
        compiler_params=params(),
        cost_estimate=cost(2 * blocks * rows * width * hidden, 12),
        name="back_rows",
    )(og, *weights)


def expert_kernel(masks, experts, *refs):
    blocks = len(masks)
    place, refs = refs[0], refs[1:]
    x_refs, refs = refs[:blocks], refs[blocks:]
    gate_ref, back_ref, refs = refs[0], refs[1], refs[2:]
    weight_refs, refs = refs[: -8 - blocks], refs[-8 - blocks :]
    gx_refs, refs = refs[:blocks], refs[blocks:]
    act_ref, gg_ref, gu_ref, x_all, gates, total, weights, sems = refs
    copies = load_experts(weight_refs, weights, sems, (0, 1))
    for copy in copies:
        copy.start()
    rows = x_refs[0].shape[0]
    for b, mask in enumerate(masks):
        x_all[b * rows : (b + 1) * rows] = x_refs[b][...]
        gates[b * rows : (b + 1) * rows] = gate_ref[place[1] ^ mask].astype(jnp.float32)
    hidden = weights.shape[3]
    each = len(copies) // len(F_MASKS)
    lane = lax.broadcasted_iota(jnp.int32, gates.shape, 1)
    x = x_all[...]
    for i, mask in enumerate(F_MASKS):
        for copy in copies[i * each : (i + 1) * each]:
            copy.wait()
        expert = (place[0] ^ mask) * (experts // len(F_MASKS)) + place[1]
        chosen = (lane == expert) | (lane == expert + experts)
        weight = jnp.sum(jnp.where(chosen, gates[...], 0.0), axis=1, keepdims=True)
        gate = jnp.dot(x, weights[0, i], preferred_element_type=jnp.float32)
        up = jnp.dot(x, weights[1, i], preferred_element_type=jnp.float32)
        cols = slice(i * hidden, (i + 1) * hidden)
        back = jnp.concatenate([back_ref[place[1] ^ m, :, cols] for m in masks]).astype(jnp.float32) * weight
        sig = jax.nn.sigmoid(gate)
        silu = gate * sig
        act_ref[:, cols] = (silu * up * weight).astype(jnp.bfloat16)
        grad_gate = (back * up * (sig * (1.0 + gate * (1.0 - sig)))).astype(jnp.bfloat16)
        grad_up = (back * silu).astype(jnp.bfloat16)
        gg_ref[:, cols] = grad_gate
        gu_ref[:, cols] = grad_up
        more = nt_dot(grad_gate, weights[0, i]) + nt_dot(grad_up, weights[1, i])
        if i == 0:
            total[...] = more
        else:
            total[...] += more
    for b in range(blocks):
        gx_refs[b][...] = total[b * rows : (b + 1) * rows].astype(jnp.bfloat16)


def expert_rows(place, masks, xs, og, backs, weights, experts):
    blocks, (rows, width) = len(xs), xs[0].shape
    n_ctx = og.shape[0]
    low = jnp.bfloat16
    scratch = weight_scratch(weights, 2)
    hidden = scratch[0].shape[3] * len(F_MASKS)
    wide = jax.ShapeDtypeStruct((blocks * rows, hidden), low)
    outs = pl.pallas_call(
        functools.partial(expert_kernel, masks, experts),
        grid=(1,),
        out_shape=[jax.ShapeDtypeStruct((rows, width), low)] * blocks + [wide] * 3,
        in_specs=[smem_spec()]
        + [vmem_spec()] * blocks
        + [pl.BlockSpec((n_ctx, rows, 128), lambda i: (0, 0, width // 128)), vmem_spec()]
        + [any_spec()] * len(weights),
        out_specs=[vmem_spec()] * (blocks + 3),
        scratch_shapes=[
            pltpu.VMEM((blocks * rows, width), low),
            pltpu.VMEM((blocks * rows, 128), jnp.float32),
            pltpu.VMEM((blocks * rows, width), jnp.float32),
        ]
        + scratch,
        compiler_params=params(),
        cost_estimate=cost(8 * blocks * rows * width * hidden, 20),
        name="expert_rows",
    )(place, *xs, og, backs, *weights)
    return outs[:blocks], outs[blocks:]


def mix_kernel(calls, place, *refs):
    act_refs, refs = refs[:calls], refs[calls:]
    weight_refs, (mix_ref, total, weights, sems) = refs[:-4], refs[-4:]
    copies = load_experts(weight_refs, weights, sems, (2,))
    for copy in copies:
        copy.start()
    hidden = weights.shape[3]
    some = act_refs[0].shape[0]
    each = len(copies) // len(F_MASKS)
    for i in range(len(F_MASKS)):
        for copy in copies[i * each : (i + 1) * each]:
            copy.wait()
        for j in range(calls):
            more = nt_dot(act_refs[j][:, i * hidden : (i + 1) * hidden], weights[0, i])
            if i == 0:
                total[j * some : (j + 1) * some] = more
            else:
                total[j * some : (j + 1) * some] += more
    blocks, rows, _ = mix_ref.shape
    for b in range(blocks):
        mix_ref[place[1] ^ b] = total[b * rows : (b + 1) * rows].astype(jnp.bfloat16)


def mix_rows(place, acts, weights, blocks, width):
    calls, (some, hidden) = len(acts), acts[0].shape
    rows = some * calls // blocks
    return pl.pallas_call(
        functools.partial(mix_kernel, calls),
        out_shape=jax.ShapeDtypeStruct((blocks, rows, width), jnp.bfloat16),
        in_specs=[smem_spec()] + [vmem_spec()] * calls + [any_spec()] * len(weights),
        out_specs=vmem_spec(),
        scratch_shapes=[pltpu.VMEM((some * calls, width), jnp.float32)] + weight_scratch(weights, 1),
        compiler_params=params(),
        cost_estimate=cost(2 * blocks * rows * width * hidden, 12),
        name="mix_rows",
    )(place, *acts, *weights)


def weight_kernel(blocks, calls, count, *refs):
    place, og_ref, refs = refs[0], refs[1], refs[2:]
    x_refs, refs = refs[:blocks], refs[blocks:]
    act_refs, refs = refs[:calls], refs[calls:]
    gg_refs, refs = refs[:calls], refs[calls:]
    gu_refs, refs = refs[:calls], refs[calls:]
    leave, stay, x_t, og_t, right = refs
    rows, width = x_refs[0].shape
    step = pl.program_id(0)

    @pl.when(step == 0)
    def _():
        for b in range(blocks):
            x_t[:, b * rows : (b + 1) * rows] = x_refs[b][...].T
            og_t[:, b * rows : (b + 1) * rows] = og_ref[place[1] ^ b, :, :width].T

    some = act_refs[0].shape[0]
    half = width // 2
    hidden = right.shape[1] // count
    for kind, (left, parts) in enumerate(((x_t, gg_refs), (x_t, gu_refs), (og_t, act_refs))):
        for i in range(calls):
            right[i * some : (i + 1) * some] = parts[i][...]
        for j in range(2):
            product = jnp.dot(
                left[j * half : (j + 1) * half], right[...], preferred_element_type=jnp.float32
            ).astype(jnp.bfloat16)
            for m in range(count):
                piece = product[:, m * hidden : (m + 1) * hidden]
                if j == 0 and m == 0:
                    stay[step, kind] = piece
                elif j == 0:
                    leave[2 * (m - 1) + step, kind] = piece
                else:

                    @pl.when(step == 0)
                    def _(m=m, kind=kind, piece=piece):
                        stay[2 + m, kind] = piece

                    @pl.when(step == 1)
                    def _(m=m, kind=kind, piece=piece):
                        leave[2 * (count - 1) + m, kind] = piece


def weight_grads(place, xs, og, acts, ggs, gus, count, first):
    blocks, calls, (rows, width) = len(xs), len(acts), xs[0].shape
    some, wide = acts[0].shape
    whole = wide // len(F_MASKS)
    hidden, half = whole // count, width // 2
    column = pl.BlockSpec((some, whole), lambda i: (0, first + i))
    low = jnp.bfloat16
    total = blocks * rows
    outs = [(3 * count - 2, 3, half, hidden), (count + 2, 3, half, hidden)]
    return pl.pallas_call(
        functools.partial(weight_kernel, blocks, calls, count),
        grid=(2,),
        out_shape=[jax.ShapeDtypeStruct(shape, low) for shape in outs],
        in_specs=[smem_spec()] + [vmem_spec()] * (blocks + 1) + [column] * (3 * calls),
        out_specs=[pl.BlockSpec(shape, lambda i: (0, 0, 0, 0)) for shape in outs],
        scratch_shapes=[
            pltpu.VMEM((width, total), low),
            pltpu.VMEM((width, total), low),
            pltpu.VMEM((total, whole), low),
        ],
        compiler_params=params(),
        cost_estimate=cost(2 * 3 * total * width * 2 * whole, 20),
        name="weight_grads",
    )(place, og, *xs, *acts, *ggs, *gus)


def total_of(*parts):
    return sum(part.astype(jnp.float32) for part in parts).astype(jnp.bfloat16)


def pair_kernel(own, core, out):
    out[...] = (own[...].astype(jnp.float32) + core[...].astype(jnp.float32)).astype(jnp.bfloat16)


def pair_sum(own, core, first, count):
    block = (1, *own.shape[1:])
    part = pl.BlockSpec(block, lambda i: (first + i, 0, 0, 0))
    return pl.pallas_call(
        pair_kernel,
        grid=(count,),
        out_shape=jax.ShapeDtypeStruct((count, *own.shape[1:]), own.dtype),
        in_specs=[part] * 2,
        out_specs=pl.BlockSpec(block, lambda i: (i, 0, 0, 0)),
        compiler_params=params(),
        cost_estimate=cost(1, 1),
        name="pair_sum",
    )(own, core)


def step_experts_kernel(parts, rate, down, *refs):
    part_refs, refs = refs[:parts], refs[parts:]
    weight, moment, average = refs[:3]
    moment_new, average_new, weight_new = refs[-3:]
    total = part_refs[0][0, 0].astype(jnp.float32)
    for part in part_refs[1:]:
        total += part[0, 0].astype(jnp.float32)
    at = (0,) if down else (0, 0)
    new = advance(weight[at], total.T if down else total, moment[at], average[at], rate)
    moment_new[at], average_new[at], weight_new[at] = new


def step_experts(parts, lower, weight, moment, average, before):
    down = weight.ndim == 3
    half, hidden = parts[0][0].shape[2:]
    if down:
        grid, block = (1,), pl.BlockSpec((1, hidden, half), lambda k: (0, 0, lower))
        specs = [pl.BlockSpec((1, 1, half, hidden), lambda k, at=at: (at, 2, 0, 0)) for _, at in parts]
    else:
        grid, block = (2,), pl.BlockSpec((1, 1, half, hidden), lambda k: (0, k, lower, 0))
        specs = [pl.BlockSpec((1, 1, half, hidden), lambda k, at=at: (at, k, 0, 0)) for _, at in parts]
    first = len(parts) + 3
    return pl.pallas_call(
        functools.partial(step_experts_kernel, len(parts), RATE_DOWN if down else RATE_IN, down),
        grid=grid,
        out_shape=[jax.ShapeDtypeStruct(weight.shape, jnp.float32)] * 3,
        in_specs=specs + [block] * 3 + [any_spec()] * len(before),
        out_specs=[block] * 3,
        input_output_aliases={first + i: i for i in range(len(before))},
        compiler_params=params(),
        cost_estimate=cost(1, 1),
        name="step_down" if down else "step_in",
    )(*(part for part, _ in parts), weight, moment, average, *before)


def sum_first(ref, cols):
    total = ref[0, :, cols].astype(jnp.float32)
    for i in range(1, ref.shape[0]):
        total += ref[i, :, cols].astype(jnp.float32)
    return total


def step_out_kernel(come, weight, moment, average, moment_new, average_new, weight_new, wide):
    rows = come.shape[1]
    wide[...] = jnp.zeros_like(wide)
    wide[:rows] = sum_first(come, slice(come.shape[2] // 2, come.shape[2]))
    new = advance(weight[...], wide[...].T[:, :rows], moment[...], average[...], RATE_OUT)
    moment_new[...], average_new[...], weight_new[...] = new


def step_out(come, weight, moment, average):
    return pl.pallas_call(
        step_out_kernel,
        out_shape=[jax.ShapeDtypeStruct(weight.shape, jnp.float32)] * 3,
        in_specs=[vmem_spec()] * 4,
        out_specs=[vmem_spec()] * 3,
        scratch_shapes=[pltpu.VMEM((128, weight.shape[0]), jnp.float32)],
        compiler_params=params(),
        cost_estimate=cost(1, 1),
        name="step_out",
    )(come, weight, moment, average)


def step_qkv_kernel(
    query_come, key_come, weight, moment, average, moment_new, average_new, weight_new, grad, wide
):
    kv = weight.shape[1] // ((GROUP + 2) * HD)
    group = GROUP * HD
    queries = sum_first(query_come, slice(0, kv * group))
    wide[...] = sum_first(key_come, slice(None))
    for h in range(kv):
        at = h * (GROUP + 2) * HD
        grad[:, at : at + group] = queries[:, h * group : (h + 1) * group]
        grad[:, at + group : at + group + HD] = wide[:, h * HD : (h + 1) * HD]
        grad[:, at + group + HD : at + group + 2 * HD] = wide[:, (kv + h) * HD : (kv + h + 1) * HD]
    new = advance(weight[...], grad[...], moment[...], average[...], RATE_QKV)
    moment_new[...], average_new[...], weight_new[...] = new


def step_qkv(query_come, key_come, weight, moment, average):
    return pl.pallas_call(
        step_qkv_kernel,
        out_shape=[jax.ShapeDtypeStruct(weight.shape, jnp.float32)] * 3,
        in_specs=[vmem_spec()] * 5,
        out_specs=[vmem_spec()] * 3,
        scratch_shapes=[
            pltpu.VMEM(weight.shape, jnp.float32),
            pltpu.VMEM(key_come.shape[1:], jnp.float32),
        ],
        compiler_params=params(),
        cost_estimate=cost(1, 1),
        name="step_qkv",
    )(query_come, key_come, weight, moment, average)


def per_device(
    tokens,
    out_grad,
    lengths,
    routes,
    gate_weights,
    qkv_weight,
    out_weight,
    norm_gains,
    expert_in,
    expert_down,
    qkv_moment,
    qkv_average,
    out_moment,
    out_average,
    gain_moment,
    gain_average,
    in_moment,
    in_average,
    down_moment,
    down_average,
):
    tok_rows, width = tokens.shape
    n_ctx, n_tp = lax.axis_size("ctx"), lax.axis_size("tp")
    experts = lax.axis_size(("fsdp", "ctx"))
    fsdp_index, ctx_index = lax.axis_index("fsdp"), lax.axis_index("ctx")
    tp_index = lax.axis_index("tp")
    place = jnp.stack([fsdp_index, ctx_index, tp_index]).astype(jnp.int32)
    low, f32 = jnp.bfloat16, jnp.float32
    half_rows = tok_rows // n_tp
    over_tp = range(n_tp)

    def part_of(value, mask):
        return lax.dynamic_slice_in_dim(value, (tp_index ^ mask) * half_rows, half_rows)

    def own_half(value):
        return part_of(value, 0)

    def sum_own(own, others):
        for m, other in enumerate(others, 1):
            own = own + swap(other, "tp", m).astype(f32)
        return own

    def to_others(own):
        return [own] + [swap(own, "tp", m) for m in over_tp[1:]]

    shard_rows, qkv_columns = qkv_weight.shape
    kv_local = qkv_columns // ((GROUP + 2) * HD)
    q_rows, k_rows = kv_local * GROUP * HD, kv_local * HD
    key_near = spread(shard_copies(qkv_weight, norm_gains, True)).reshape(-1, 2 * k_rows + 128)
    key_across = swap(key_near, "fsdp", 2)
    key_shards = [key_near, key_across, swap(key_near, "fsdp", 1), swap(key_across, "fsdp", 1)]
    both_copies = shard_copies(qkv_weight, out_weight, False)
    both_near = spread(after(both_copies, key_near)).reshape(-1, 2 * q_rows)

    down_t = expert_down[0].T[None]
    half = width // 2
    own = jnp.stack(
        [jnp.concatenate([expert_in[0, :, rows], down_t[:, rows]]) for rows in (slice(0, half), slice(half, width))]
    ).astype(low)
    along_tp = [swap(after(own, key_near), "tp", m) for m in over_tp[1:]]
    along_x = swap(after(own, *key_shards[2:]), "fsdp", 2)

    places = ctx_index * tok_rows + jnp.arange(tok_rows, dtype=jnp.int32)
    _, position = doc_positions(lengths[0], places)
    starts = (places - position)[None, :]
    frequency = jnp.exp(jnp.arange(HD // 2, dtype=f32) * (-2.0 * math.log(ROPE_BASE) / HD))
    angles = frequency[:, None] * position.astype(f32)[None, :]
    cosine, sine = jnp.cos(angles), jnp.sin(angles)
    kv_t, normed_low, norm_t, key_whole, gains = project_keys(
        place, tokens, cosine, sine, key_shards, k_rows
    )
    gain_one, gain_two = gains[0], gains[1]
    both_across = swap(after(both_near, kv_t, along_x), "fsdp", 2)
    both_shards = [
        both_near,
        both_across,
        swap(after(both_near, kv_t), "fsdp", 1),
        swap(after(both_across, kv_t), "fsdp", 1),
    ]
    kv_pieces = spread(kv_t)
    q_t, query_whole = project_queries(place, normed_low, cosine, sine, both_shards)

    uppers = [swap(along_x[:1], "tp", m) for m in over_tp[1:]]
    lowers = [swap(after(piece[1:], both_across), "fsdp", 2) for piece in along_tp]
    soon = [swap(after(own, both_near), "fsdp", 1)]

    grad_rows = row_copies(after(place, kv_t), out_grad, routes, gate_weights, half_rows, experts)
    og = spread(after(grad_rows, kv_pieces))

    probs, head_t, kv_all, out_t, attn_own, *attn_others = attend(
        after(place, *soon, *along_tp), starts, q_t, kv_pieces, both_shards
    )
    soon += [swap(after(piece, attn_own), "fsdp", 1) for piece in [*along_tp, along_x, *uppers, *lowers]]
    hidden_one = own_half(after(tokens, og, *soon)).astype(f32) + sum_own(attn_own, attn_others)
    inverse_two = lax.rsqrt(jnp.mean(hidden_one * hidden_one, axis=-1, keepdims=True) + EPSILON)
    normed_two = hidden_one * inverse_two
    normed_two_low = (normed_two * gain_two).astype(low)

    x_own = after(normed_two_low, og)
    xs = [x_own] + [swap(x_own, "ctx", m) for m in range(1, n_ctx)]
    weights = [own, *along_tp, along_x, *uppers, *lowers, *soon]
    backs = back_rows(og, weights, width)
    grads_x, acts, ggs, gus = [], [], [], []
    for at in range(0, n_ctx, 2):
        here = after(place, *acts[-1:])
        some_x, (act, gg, gu) = expert_rows(
            here, tuple(range(at, at + 2)), xs[at : at + 2], og, backs, weights, experts
        )
        grads_x += some_x
        acts.append(act)
        ggs.append(gg)
        gus.append(gu)
    come_x = [swap(grads_x[m], "ctx", m) for m in range(1, n_ctx)]
    core_leave, core_stay = weight_grads(place, xs, og, acts, ggs, gus, n_tp, 2)
    leave, stay = weight_grads(after(place, core_leave), xs, og, acts, ggs, gus, n_tp, 0)
    mixes = mix_rows(after(place, leave), acts, weights, n_ctx, width)

    grad_normed_two = after(grads_x[0], mixes).astype(f32)
    for come in come_x:
        grad_normed_two += come.astype(f32)
    gain_grad_two = jnp.sum(grad_normed_two * normed_two, axis=0)
    grad_hidden = own_half(out_grad).astype(f32) + norm_back(grad_normed_two, normed_two, inverse_two, gain_two)
    grad_attn = to_others(grad_hidden.astype(low))
    core_leave = swap(after(core_leave, mixes, *come_x), "fsdp", 1)
    come_mix = spread(after(mixes, grad_hidden))

    core_leave = after(core_leave, grad_hidden)
    uppers_out = [pair_sum(leave, core_leave, 2 * m, 2) for m in range(n_tp - 1)]
    lower_out = pair_sum(leave, core_leave, 2 * (n_tp - 1), n_tp)
    uppers_in = [swap(uppers_out[m - 1], "tp", m) for m in over_tp[1:]]
    lower_in = swap(lower_out, "fsdp", 2)

    dq_t, kv_grads = attend_back(
        after(place, lower_out, *uppers_out), probs, q_t, kv_all, grad_attn, out_t, cosine, sine
    )
    come_mix = after(come_mix, dq_t)
    come = spread(kv_grads)
    core_stay = swap(after(core_stay, lower_out), "fsdp", 1)
    query_parts, query_part = query_grads(
        after(place, come_mix), dq_t, norm_t, query_whole, grad_attn, head_t
    )

    lower_next = [
        total_of(stay[2 + m], core_stay[2 + m], after(lower_in, query_part)[m]) for m in over_tp[1:]
    ]
    upper_next = total_of(stay[1], core_stay[1], *(after(part, query_part)[1] for part in uppers_in))
    lowers_last = [swap(lower_next[m - 1], "tp", m) for m in over_tp[1:]]
    query_near, query_far = sum_cores(query_parts, upper_next, *lower_next)
    mixture = jnp.sum(after(come_mix, query_far).astype(f32), axis=0)
    query_near = added(query_near, swap(query_far, "fsdp", 2))
    key_parts, (normed_own, *normed_others) = key_grads(
        after(place, query_near, *lowers_last), come, cosine, sine, norm_t, key_whole,
        tokens, query_part, gain_grad_two[None]
    )
    grad_normed_one = sum_own(normed_own, normed_others)
    block_parts = to_others((hidden_one + mixture).astype(low))
    inputs = own_half(tokens).astype(f32)
    inverse_one = lax.rsqrt(jnp.mean(inputs * inputs, axis=-1, keepdims=True) + EPSILON)
    in_own = (
        (grad_hidden + norm_back(grad_normed_one, inputs * inverse_one, inverse_one, gain_one)).astype(low)
    )
    in_parts = to_others(in_own)
    key_near, key_far = sum_cores(key_parts)
    key_come = swap(key_far, "fsdp", 2)
    upper_last = swap(after(upper_next, key_come), "fsdp", 2)
    lower_parts = [(stay, 2), (core_stay, 2), (lower_in, 0)] + [(part[None], 0) for part in lowers_last]
    in_new = step_experts(lower_parts, 1, after(expert_in, key_far, in_own), in_moment, in_average, ())
    query_grad = scatter_rows(query_near)
    upper_parts = [(stay, 0), (core_stay, 0)] + [(part, 0) for part in uppers_in] + [(upper_last[None], 0)]
    key_near = added(key_near, after(key_come, query_grad, in_new[0]))
    key_grad = scatter_rows(key_near)
    block_out = join(place, [after(part, key_near) for part in block_parts])
    out_new = step_out(query_grad, after(out_weight, block_out), out_moment, out_average)
    down_new = step_experts(lower_parts, 1, after(expert_down, out_new[0]), down_moment, down_average, ())
    in_new = step_experts(upper_parts, 0, after(expert_in, down_new[0]), in_moment, in_average, in_new)
    down_new = step_experts(upper_parts, 0, after(expert_down, in_new[0]), down_moment, down_average, down_new)
    in_grad = join(place, [after(part, down_new[0]) for part in in_parts])
    key_grad = after(key_grad, in_grad)
    gains_grad = jnp.sum(key_grad[:, :, 2 * k_rows : 2 * k_rows + 2].astype(f32), axis=0).T
    gains_others = [swap(gains_grad, "tp", m) for m in over_tp[1:]]
    qkv_new = step_qkv(query_grad, key_grad, qkv_weight, qkv_moment, qkv_average)
    gains_grad = gains_grad + sum(after(other, qkv_new[0]) for other in gains_others)
    gain_new = advance(norm_gains, gains_grad, gain_moment, gain_average, RATE_GAIN)
    return (block_out, in_grad, *qkv_new, *out_new, *gain_new, *in_new, *down_new)


def solution(mesh):
    return jax.shard_map(
        per_device,
        mesh=mesh,
        in_specs=(
            P(("fsdp", "ctx"), None),
            P(("fsdp", "ctx"), None),
            P("fsdp", None),
            P(("fsdp", "ctx"), None),
            P(("fsdp", "ctx"), None),
            P(("fsdp", "ctx"), "tp"),
            P("tp", ("fsdp", "ctx")),
            P(None, ("fsdp", "ctx")),
            P(("fsdp", "ctx"), None, None, "tp"),
            P(("fsdp", "ctx"), "tp", None),
            P(("fsdp", "ctx"), "tp"),
            P(("fsdp", "ctx"), "tp"),
            P("tp", ("fsdp", "ctx")),
            P("tp", ("fsdp", "ctx")),
            P(None, ("fsdp", "ctx")),
            P(None, ("fsdp", "ctx")),
            P(("fsdp", "ctx"), None, None, "tp"),
            P(("fsdp", "ctx"), None, None, "tp"),
            P(("fsdp", "ctx"), "tp", None),
            P(("fsdp", "ctx"), "tp", None),
        ),
        out_specs=(
            P(("fsdp", "ctx"), None),
            P(("fsdp", "ctx"), None),
            P(("fsdp", "ctx"), "tp"),
            P(("fsdp", "ctx"), "tp"),
            P(("fsdp", "ctx"), "tp"),
            P("tp", ("fsdp", "ctx")),
            P("tp", ("fsdp", "ctx")),
            P("tp", ("fsdp", "ctx")),
            P(None, ("fsdp", "ctx")),
            P(None, ("fsdp", "ctx")),
            P(None, ("fsdp", "ctx")),
            P(("fsdp", "ctx"), None, None, "tp"),
            P(("fsdp", "ctx"), None, None, "tp"),
            P(("fsdp", "ctx"), None, None, "tp"),
            P(("fsdp", "ctx"), "tp", None),
            P(("fsdp", "ctx"), "tp", None),
            P(("fsdp", "ctx"), "tp", None),
        ),
        check_vma=False,
    )
```
